32 devices in a mesh: dp: 4 (over y, x), expert: 8 (over z, core).
Axes of the slice: x: 2, y: 2, z: 4, core: 2. Of those that a mesh axis runs over, the one named last changes fastest.
Arguments:
- tokens: bfloat16 [4, 4096, 512], P('dp', 'expert'), may hold values from -6 to 6
- segments: int32 [4, 4096], P('dp', 'expert'), may hold values from 0 to 2, as said below
- expert_ids: int32 [4, 4096, 2], P('dp', 'expert'), may hold values from 0 to 7, all different within a row; in each aligned block of 512 rows (0 to 511, 512 to 1023, ..., all dimensions but the last counted through in order) at most 192 rows name the same one
- keep: int32 [4, 4096, 2], P('dp', 'expert'), may hold values 0 or 1
- gain_one: float32 [512], replicated, may hold values from 0.1 to 1.9
- kv_weight: bfloat16 [512, 128], replicated, may hold values from -0.25 to 0.25
- router_weight: bfloat16 [512, 8], replicated, may hold values from -0.1875 to 0.1875
- query_weight: bfloat16 [8, 512, 64], replicated, may hold values from -0.5 to 0.5
- out_weight: bfloat16 [8, 512, 64], replicated, may hold values from -1.5 to 1.5
- gain_two: float32 [512], replicated, may hold values from 0.1 to 1.9
- up_weight: bfloat16 [512, 2048], replicated, may hold values from -0.25 to 0.25
- down_weight: bfloat16 [2048, 512], replicated, may hold values from -0.125 to 0.125
- cotangent: bfloat16 [4, 4096, 512], P('dp', 'expert'), may hold values from -6 to 6
Outputs:
- layer_out: bfloat16 [4, 4096, 512], P('dp', 'expert')
- grad_tokens: float32 [4, 4096, 512], P('dp', 'expert')
- grad_gain_one: float32 [512], replicated
- grad_kv_weight: float32 [512, 128], replicated
- grad_router_weight: float32 [512, 8], replicated
- grad_query_weight: float32 [8, 512, 64], P(None, 'expert', 'dp')
- grad_out_weight: float32 [8, 512, 64], P(None, 'expert', 'dp')
- grad_gain_two: float32 [512], replicated
- grad_up_weight: float32 [512, 2048], replicated
- grad_down_weight: float32 [2048, 512], replicated
The draws below stay inside these ranges and needn't reach their ends.
Inputs may be any that keep to these rules, and one draw needn't show every extreme that they name: `expert_ids`: each token names two different experts; among the 512 positions of one device (aligned blocks of a row) no expert is named more than 192 times, a bound that some block reaches. `segments`: ids never fall along a row; id 1 starts within the first 512 positions of the row and ends within the last 512, id 0 before it and id 2 after it.
All inputs are finite; a program needn't handle non-finite values. No bound on the sum of `keep` on one device may be relied on, other than what follows from the above.
Results may differ from the reference program's by a relative error of at most 0.017.
Values may be sent and summed in bfloat16 or wider, within the bound.
A program may use at most 128 MiB of HBM per device.

```python
import math
import jax
import jax.numpy as jnp
import numpy as np
from jax import lax

D = 512
HEAD = 64
EXPERTS = 8
FF = 2048
POS_DEV = 512
ROWS = 4
ROW_LEN = 4096
EXP_CAP = 192


def draw_segments(key, part):
    key = jax.random.fold_in(key, 11)
    first_key, last_key = jax.random.split(key)
    starts = jax.random.randint(first_key, (ROWS, 1), 1, POS_DEV)
    ends = jax.random.randint(last_key, (ROWS, 1), ROW_LEN - POS_DEV + 1, ROW_LEN)
    places = jnp.arange(ROW_LEN, dtype=jnp.int32)[None, :]
    return (places >= starts).astype(jnp.int32) + (places >= ends).astype(jnp.int32)


def touch_ends(values, own_key, least, largest):
    longest = values.shape.index(max(values.shape))
    spots = []
    for shift in (0, 1):
        where = [jax.random.randint(jax.random.fold_in(own_key, axis), (), 0, length) for axis, length in enumerate(values.shape)]
        where[longest] = (where[longest] + shift) % values.shape[longest]
        spots.append(tuple(where))
    return values.at[spots[0]].set(least).at[spots[1]].set(largest)


def shard_levels(stream_key, extent, cuts, smallest, high):
    def one(dim, blocks):
        heights = jax.random.uniform(jax.random.fold_in(jax.random.fold_in(stream_key, 6), dim), (blocks,), jnp.float32, smallest / len(cuts), high / len(cuts))
        return jnp.repeat(jnp.exp(heights), extent[dim] // blocks).reshape((-1,) + (1,) * (len(extent) - dim - 1))

    factor_of = one(*cuts[0])
    for cut in cuts[1:]:
        factor_of = factor_of * one(*cut)
    return factor_of


def assign_block(stream_key, own, number, rows, number_of, top, limit, slope):
    order = jax.random.permutation(stream_key, number_of)
    crowded, usual = load_shares(number_of, rows * top, limit, slope, True), load_shares(number_of, rows * top, limit, slope, False)
    places = jnp.arange(number_of)

    def named(lengths, turn):
        used = int((lengths > 0).sum())
        fixed = max(1, used // 4)
        passed = fixed + (places - fixed + turn * (used - fixed)) % max(1, number_of - fixed)
        return jnp.zeros((number_of,), jnp.int32).at[order[jnp.where(places < fixed, places, passed)]].set(jnp.asarray(lengths, jnp.int32))

    lengths = jnp.where(number % 4 == 0, named(crowded, number // 4), named(usual, number - number // 4 - 1))
    mixed = jax.random.permutation(jax.random.fold_in(own, 3), number_of)
    source_of, receiver = mixed[0:number_of // 2 * 2:2], mixed[1:number_of // 2 * 2:2]
    margin = jnp.minimum(lengths[source_of] - 1, limit - lengths[receiver]) // 2
    margin = jnp.where((source_of == order[0]) | (receiver == order[0]) | (lengths[receiver] == 0), 0, jnp.maximum(margin, 0))
    passed = jax.random.randint(jax.random.fold_in(own, 4), (number_of // 2,), 0, 1 << 20) % (margin + 1)
    lengths = lengths.at[source_of].add(-passed).at[receiver].add(passed)
    items = jnp.searchsorted(jnp.cumsum(lengths), jnp.arange(rows * top), side="right").astype(jnp.int32)
    grid = items.reshape(top, rows).T
    grid = grid[jax.random.permutation(jax.random.fold_in(own, 1), rows)]
    turn = jax.random.randint(jax.random.fold_in(own, 2), (rows, 1), 0, top)
    return jnp.take_along_axis(grid, (jnp.arange(top)[None, :] + turn) % top, axis=1)


def load_shares(count, total, limit, slope, full):
    portions = [(1 << 20) // math.isqrt(grade ** slope) + 1 for grade in range(1, count + 1)]
    largest = limit if full else min(limit, max(-(-total // count), total * portions[0] // sum(portions)))
    least = 1 if total - largest >= count - 1 else 0
    counts, surplus = [largest] + [least] * (count - 1), total - largest - least * (count - 1)
    while surplus > 0:
        free = [i for i in range(1, count) if counts[i] < largest] or [i for i in range(1, count) if counts[i] < limit]
        mass, remaining = sum([portions[i] for i in free]), surplus
        for i in free:
            extra = min(limit - counts[i], max(1, remaining * portions[i] // mass), surplus)
            counts[i] = counts[i] + extra
            surplus = surplus - extra
    return np.array(counts)


def gaussian(stream_key, extent, scale, limit, cuts=(), kind=jnp.bfloat16):
    factor_of = shard_levels(stream_key, extent, cuts, -0.22, 0.18) if cuts else 1.0
    values = jax.random.normal(stream_key, extent, jnp.float32) * scale * factor_of
    return jnp.minimum(jnp.maximum(values, -limit), limit).astype(kind)


def setup_inputs(seed: int = 0) -> dict:
    keys = jax.random.split(jax.random.key(seed), 14)
    tokens = gaussian(keys[0], (ROWS, ROW_LEN, D), 1.0, 6.0, ((0, 4), (1, 8)))
    segments = draw_segments(jax.random.fold_in(keys[13], 71), 0)
    expert_ids_keys = jax.random.split(jax.random.fold_in(keys[2], 1), ROWS * ROW_LEN // POS_DEV)
    expert_ids_turns = jax.random.permutation(jax.random.fold_in(keys[2], 3), ROWS * ROW_LEN // POS_DEV)
    expert_ids = jax.vmap(lambda own, number: assign_block(jax.random.fold_in(keys[2], 2), own, number, POS_DEV, EXPERTS, 2, EXP_CAP, 2))(expert_ids_keys, expert_ids_turns).reshape((ROWS, ROW_LEN, 2))
    keep = touch_ends((jax.random.randint(keys[3], (ROWS, ROW_LEN, 2), 0, 16) < 15).astype(jnp.int32), jax.random.fold_in(keys[3], 1), 0, 1)
    gain_one = jnp.clip(1.0 + 0.18 * jax.random.normal(keys[4], (D,), jnp.float32), 0.1, 1.9)
    kv_weight = gaussian(keys[5], (D, 2 * HEAD), D ** -0.5, 0.25)
    router_weight = gaussian(keys[6], (D, EXPERTS), (2 * D) ** -0.5, 0.1875)
    query_weight = gaussian(keys[7], (EXPERTS, D, HEAD), (D // 4) ** -0.5, 0.5)
    out_weight = gaussian(keys[8], (EXPERTS, D, HEAD), 16 ** -0.5, 1.5)
    gain_two = jnp.clip(1.0 + 0.18 * jax.random.normal(keys[9], (D,), jnp.float32), 0.1, 1.9)
    up_weight = gaussian(keys[10], (D, FF), D ** -0.5, 0.25)
    down_weight = gaussian(keys[11], (FF, D), FF ** -0.5, 0.125)
    cotangent = gaussian(keys[12], (ROWS, ROW_LEN, D), 1.0, 6.0, ((0, 4), (1, 8)))
    return {"tokens": tokens, "segments": segments, "expert_ids": expert_ids, "keep": keep, "gain_one": gain_one, "kv_weight": kv_weight, "router_weight": router_weight, "query_weight": query_weight, "out_weight": out_weight, "gain_two": gain_two, "up_weight": up_weight, "down_weight": down_weight, "cotangent": cotangent}


HIGH = lax.Precision.HIGHEST
SCALE = 0.125
NEGATIVE = -1e+30
EPS = 1e-05

@jax.custom_vjp
def low(v):
    return lax.optimization_barrier(v.astype(jnp.bfloat16)).astype(jnp.float32)

@jax.custom_vjp
def low_back(v):
    return v

def low_keep(v):
    return (low(v), None)

def low_pass(kept, grad):
    return (grad,)

def back_keep(v):
    return (v, None)

def back_low(kept, grad):
    return (low(grad),)
low.defvjp(low_keep, low_pass)
low_back.defvjp(back_keep, back_low)

def layer_norm(values, gain):
    row_mean = lax.optimization_barrier(jnp.mean(values, -1, keepdims=True))
    centred = values - row_mean
    row_var = lax.optimization_barrier(jnp.mean(centred * centred, -1, keepdims=True))
    return centred * lax.rsqrt(row_var + EPS) * gain

def attend_block(query_rows, query_segs, kv_row, seg_row):
    key_part = kv_row[:, :HEAD]
    value_part = kv_row[:, HEAD:]
    scores = low_back(jnp.dot(query_rows, key_part.T, precision=HIGH) * SCALE)
    scores = jnp.where(query_segs[:, None] == seg_row[None, :], scores, NEGATIVE)
    row_peak = lax.optimization_barrier(jnp.max(scores, 1, keepdims=True))
    expo = jnp.exp(scores - row_peak)
    probs_row = expo / lax.optimization_barrier(jnp.sum(expo, 1, keepdims=True))
    return jnp.dot(low(probs_row), value_part, precision=HIGH)

def attend_row(running, row_item):
    query_rows, query_segs, kv_row, seg_row = row_item
    span = min(2048, 2 * ROW_LEN)
    blocks = query_rows.reshape(-1, span, HEAD)
    seg_blocks = query_segs.reshape(-1, span)

    def one_block(block_item):
        return attend_block(block_item[0], block_item[1], kv_row, seg_row)
    outputs = lax.map(jax.checkpoint(one_block), (blocks, seg_blocks))
    return (running, outputs.reshape(-1, HEAD))

def forward(token_rows, gain_one, kv_weight, router_weight, query_weight, out_weight, gain_two, up_weight, down_weight, segments, expert_ids, keep):
    normed = low(layer_norm(token_rows, gain_one))
    kv_all = low_back(low(jnp.einsum('rld,dk->rlk', normed, kv_weight, precision=HIGH)))
    logits = jnp.einsum('rld,de->rle', normed, router_weight, precision=HIGH)
    onehots = jax.nn.one_hot(expert_ids, EXPERTS, dtype=jnp.float32)
    chosen = jnp.einsum('rlce,rle->rlc', onehots, logits, precision=HIGH)
    gates = jax.nn.softmax(chosen, axis=-1) * keep.astype(jnp.float32)
    query_list = []
    for which in range(2):
        copy_rows = low_back(normed)
        all_queries = jnp.einsum('rld,edh->rleh', copy_rows, query_weight, precision=HIGH)
        picked = jnp.einsum('rle,rleh->rlh', onehots[:, :, which], all_queries, precision=HIGH)
        query_list.append(low_back(low(picked)))
    queries = jnp.stack(query_list, 2).reshape(ROWS, 2 * ROW_LEN, HEAD)
    query_segs = jnp.repeat(segments, 2, axis=1)
    carry_none, attended = lax.scan(attend_row, jnp.float32(0.0), (queries, query_segs, kv_all, segments))
    attended = attended.reshape(ROWS, ROW_LEN, 2, HEAD)
    mixed = token_rows
    for which in range(2):
        out_rows = low_back(low(attended[:, :, which]))
        spread = onehots[:, :, which, :, None] * out_rows[:, :, None, :]
        branch = low_back(low(jnp.einsum('rleh,edh->rld', spread, out_weight, precision=HIGH)))
        mixed = mixed + gates[:, :, which:which + 1] * branch
    hidden_in = low(layer_norm(mixed, gain_two))
    pre_act = low_back(jnp.einsum('rld,df->rlf', hidden_in, up_weight, precision=HIGH))
    activated = low(jax.nn.gelu(pre_act, approximate=True))
    return mixed + jnp.einsum('rlf,fd->rld', activated, down_weight, precision=HIGH)

def reference(tokens, segments, expert_ids, keep, gain_one, kv_weight, router_weight, query_weight, out_weight, gain_two, up_weight, down_weight, cotangent):
    floats = (tokens.astype(jnp.float32), gain_one.astype(jnp.float32), kv_weight.astype(jnp.float32), router_weight.astype(jnp.float32), query_weight.astype(jnp.float32), out_weight.astype(jnp.float32), gain_two.astype(jnp.float32), up_weight.astype(jnp.float32), down_weight.astype(jnp.float32))

    def layer_fn(*weights):
        return forward(*weights, segments, expert_ids, keep)
    result, pull_back = jax.vjp(layer_fn, *floats)
    grads = pull_back(cotangent.astype(jnp.float32))
    return (result.astype(jnp.bfloat16), grads[0], grads[1], grads[2], grads[3], grads[4], grads[5], grads[6], grads[7], grads[8])
```

```python
import functools

import jax
import jax.numpy as jnp
from jax import lax
from jax.experimental import pallas as pl
from jax.experimental.pallas import tpu as pltpu
from jax.sharding import PartitionSpec as P

EPS = 1e-05
SCALE = 0.125
NEGATIVE = -1e30
LOW = jnp.bfloat16
F32 = jnp.float32
HIGH = lax.Precision.HIGHEST
MESH = pl.DeviceIdType.MESH
TILE = 128
SPAN = 256
SEG_ROWS = 16


def dot(left, right, left_dim, right_dim, precision=None):
    return lax.dot_general(
        left,
        right,
        (((left_dim,), (right_dim,)), ((), ())),
        preferred_element_type=F32,
        precision=precision,
    )


def loop(count, body):
    def step(i, carry):
        body(i)
        return carry

    lax.fori_loop(0, count, step, 0)


def moments(values):
    mean = jnp.mean(values, -1, keepdims=True)
    centred = values - mean
    scale = lax.rsqrt(jnp.mean(centred * centred, -1, keepdims=True) + EPS)
    return centred * scale, scale


def norm_back(hat, scale, gain, grad):
    scaled = grad * gain
    inner = jnp.mean(scaled, -1, keepdims=True) + hat * jnp.mean(scaled * hat, -1, keepdims=True)
    return scale * (scaled - inner), jnp.sum(grad * hat, 0, keepdims=True)


def spread(ids, rows, experts):
    pieces = []
    for e in range(experts):
        pieces.append(
            jnp.where(ids[0:1] == e, rows[0], 0.0) + jnp.where(ids[1:2] == e, rows[1], 0.0)
        )
    return jnp.concatenate(pieces, 0).astype(LOW)


def pick(ids, everything, experts, head):
    picked = []
    for c in range(2):
        total = jnp.zeros((head, everything.shape[1]), F32)
        for e in range(experts):
            part = everything[e * head : (e + 1) * head]
            total = total + jnp.where(ids[c : c + 1] == e, part, 0.0)
        picked.append(total)
    return picked


def thirds(values):
    first = values.astype(LOW)
    rest = values - first.astype(F32)
    second = rest.astype(LOW)
    third = (rest - second.astype(F32)).astype(LOW)
    return [first.astype(F32), second.astype(F32), third.astype(F32)]


def gelu_both(x):
    root, cubic = 0.7978845608028654, 0.044715
    square = x * x
    t = jnp.tanh(root * x * (1.0 + cubic * square))
    half = 0.5 * (1.0 + t)
    slope = half + 0.5 * x * (1.0 - t * t) * (root + 3.0 * root * cubic * square)
    return x * half, slope


def kernel(
    chips,
    tokens_hbm,
    segments_ref,
    ids_ref,
    keep_ref,
    gain_one_ref,
    kv_weight_ref,
    router_ref,
    query_hbm,
    out_hbm,
    gain_two_ref,
    up_hbm,
    down_hbm,
    cot_hbm,
    layer_out_ref,
    grad_tokens_ref,
    grad_gain_one_ref,
    grad_kv_weight_ref,
    grad_router_ref,
    grad_query_ref,
    grad_out_ref,
    grad_gain_two_ref,
    grad_up_ref,
    grad_down_ref,
    tokens,
    cot,
    query_all,
    out_all,
    up,
    down,
    normed,
    kv,
    q_aug,
    o_aug,
    q_rows,
    peak,
    total,
    gates_ref,
    soft_ref,
    gated,
    mixed,
    hidden,
    hidden_t,
    act,
    grad_pre,
    result,
    grad_hidden,
    grad_mixed,
    grad_mixed_low,
    grad_logits_ref,
    grad_q,
    part,
    kv_pair,
    kv_out,
    kv_in,
    kv_own,
    grad_spread,
    load_sem,
    kv_send,
    kv_recv,
    pair_send,
    pair_recv,
    back_send,
    back_recv,
):
    positions, width = tokens.shape
    experts, head = router_ref.shape[0], kv_weight_ref.shape[1] // 2
    dp = lax.axis_index("dp")
    device = lax.axis_index("expert")
    chip, core = device // 2, device % 2
    sibling = (dp, chip * 2 + 1 - core)

    def ahead(k):
        return (dp, lax.rem(chip + k, chips) * 2 + core)

    def behind(k):
        return (dp, lax.rem(chip + chips - k, chips) * 2 + core)

    loads = [
        pltpu.make_async_copy(a, b, load_sem.at[i])
        for i, (a, b) in enumerate(
            [
                (tokens_hbm, tokens),
                (query_hbm, query_all),
                (out_hbm, out_all),
                (up_hbm, up),
                (cot_hbm, cot),
                (down_hbm, down),
            ]
        )
    ]
    for load in loads:
        load.start()

    barrier = pltpu.get_barrier_semaphore()
    pl.semaphore_signal(barrier, inc=1, device_id=sibling, device_id_type=MESH)
    loop(
        chips - 1,
        lambda k: pl.semaphore_signal(
            barrier, inc=1, device_id=ahead(k + 1), device_id_type=MESH
        ),
    )

    loads[0].wait()

    def norm_rows(i):
        rows = pl.ds(pl.multiple_of(i * TILE, TILE), TILE)
        hat, _ = moments(tokens[rows].astype(F32))
        low = (hat * gain_one_ref[...]).astype(LOW)
        normed[rows] = low
        kv[0, rows] = dot(low, kv_weight_ref[...], 1, 0).astype(LOW)

    loop(positions // TILE, norm_rows)
    segs = segments_ref[...].astype(F32)
    lanes = kv.shape[2]
    seg_rows = [segs[:, i * lanes : (i + 1) * lanes] for i in range(positions // lanes)]
    seg_rows.append(jnp.full((SEG_ROWS - len(seg_rows), lanes), 3.0, F32))
    kv[0, positions:] = jnp.concatenate(seg_rows, 0).astype(LOW)

    pl.semaphore_wait(barrier, chips)

    def kv_copy(source, target, device_id):
        return pltpu.make_async_remote_copy(
            src_ref=kv.at[source],
            dst_ref=kv.at[target],
            send_sem=kv_send.at[target],
            recv_sem=kv_recv.at[target],
            device_id=device_id,
            device_id_type=MESH,
        )

    kv_copy(0, 1, sibling).start()
    loop(chips - 1, lambda k: kv_copy(0, 2 * (k + 1), ahead(k + 1)).start())

    ids = ids_ref[...]
    kept = keep_ref[...].astype(F32)
    loads[1].wait()
    queries = jnp.concatenate(
        pick(ids, dot(query_all[...], normed[...], 1, 1), experts, head), 1
    )
    queries = queries.astype(LOW).astype(F32) * SCALE
    seg_twice = jnp.concatenate([segs, segs], 1)
    count = 2 * positions
    others = [jnp.where(seg_twice == s, 0.0, NEGATIVE) for s in range(3)]
    blank = jnp.zeros((head, count), F32)
    q_aug[0 : 2 * head] = jnp.concatenate([queries, blank], 0).astype(LOW)
    q_aug[2 * head :] = jnp.concatenate(
        others + [jnp.zeros((2 * head - 3, count), F32)], 0
    ).astype(LOW)
    q_rows[0:count] = jnp.concatenate([queries, blank], 0).T.astype(LOW)
    logits = dot(router_ref[...], normed[...], 1, 1)
    places = lax.broadcasted_iota(jnp.int32, logits.shape, 0)
    onehots = [(places == ids[c : c + 1]).astype(F32) for c in range(2)]
    chosen = [jnp.sum(onehots[c] * logits, 0, keepdims=True) for c in range(2)]
    top = jnp.maximum(chosen[0], chosen[1])
    expo = [jnp.exp(chosen[c] - top) for c in range(2)]
    soft_ref[...] = jnp.concatenate([e / (expo[0] + expo[1]) for e in expo], 0)
    gates_ref[...] = soft_ref[...] * kept

    peak[...] = jnp.full(peak.shape, -3e38, F32)
    total[...] = jnp.zeros(total.shape, F32)

    def key_block(slot):
        block = kv[slot, :positions]
        seg = kv[slot, positions:].astype(F32)
        first = jnp.sum(jnp.where(seg < 0.5, 1.0, 0.0), keepdims=True)
        second = jnp.sum(jnp.where(seg < 1.5, 1.0, 0.0), keepdims=True)
        row = lax.broadcasted_iota(jnp.int32, (positions, lanes), 0).astype(F32)
        lane = lax.broadcasted_iota(jnp.int32, (positions, lanes), 1)
        segment = jnp.where(row < first, 0, jnp.where(row < second, 1, 2))
        extra = jnp.where((segment == lane) | ((lane >= 3) & (lane < 6)), 1.0, 0.0)
        return block, jnp.concatenate([block, extra.astype(LOW)], 1)

    def attend(slot):
        block, keys = key_block(slot)
        values_t = jnp.concatenate([jnp.ones((16, positions), LOW), block.T[head:]], 0)

        def one_span(i):
            at = pl.ds(pl.multiple_of(i * SPAN, SPAN), SPAN)
            scores = dot(keys, q_aug[:, at], 1, 0)
            old = peak[:, at]
            new = jnp.maximum(old, jnp.max(scores, 0, keepdims=True))
            probs = jnp.exp(scores - new).astype(LOW)
            total[:, at] = total[:, at] * jnp.exp(old - new) + dot(values_t, probs, 1, 0)
            peak[:, at] = new

        loop(count // SPAN, one_span)

    def attend_chip(k):
        @pl.when(k > 0)
        def _():
            kv_copy(0, 2 * k, ahead(k)).wait_recv()
            kv_copy(2 * k, 2 * k + 1, sibling).start()

        attend(2 * k)
        kv_copy(2 * k, 2 * k + 1, sibling).wait_recv()
        attend(2 * k + 1)

    loop(chips, attend_chip)

    weight = total[0:1]
    attended = total[16:] / weight
    log_total = peak[...] + jnp.log(weight)
    total[16:] = attended
    rows = [thirds(-log_total)[i] for i in range(3)]
    q_aug[2 * head :] = jnp.concatenate(
        others + rows + [jnp.zeros((2 * head - 6, count), F32)], 0
    ).astype(LOW)
    halves = [attended[:, :positions], attended[:, positions:]]
    gates = gates_ref[...]
    gated[...] = spread(ids, [halves[c] * gates[c : c + 1] for c in range(2)], experts)
    loads[2].wait()

    def mix_rows(i):
        rows = pl.ds(pl.multiple_of(i * TILE, TILE), TILE)
        new = tokens[rows].astype(F32) + dot(gated[:, rows], out_all[...], 0, 0)
        mixed[rows] = new
        hat, _ = moments(new)
        low = (hat * gain_two_ref[...]).astype(LOW)
        hidden[rows] = low
        result[rows] = new
        grad_hidden[rows] = jnp.zeros((TILE, width), F32)

    loop(positions // TILE, mix_rows)
    hidden_t[...] = hidden[...].T

    for i in (3, 4, 5):
        loads[i].wait()
    chunk = act.shape[1]

    def feed(c):
        units = pl.ds(pl.multiple_of(c * chunk, chunk), chunk)

        def feed_rows(i):
            rows = pl.ds(pl.multiple_of(i * TILE, TILE), TILE)
            value, slope = gelu_both(dot(hidden[rows], up[:, units], 1, 0))
            value = value.astype(LOW)
            grad = (dot(cot[rows], down[units], 1, 1) * slope).astype(LOW)
            act[rows] = value
            grad_pre[rows] = grad
            result[rows] = result[rows] + dot(value, down[units], 1, 0)
            grad_hidden[rows] = grad_hidden[rows] + dot(grad, up[:, units], 1, 1)

        loop(positions // TILE, feed_rows)
        grad_up_ref[:, units] = dot(hidden_t[...], grad_pre[...], 1, 0).astype(LOW)
        grad_down_ref[units] = dot(act[...], cot[...], 0, 0).astype(LOW)

    loop(up.shape[1] // chunk, feed)

    grad_gain_two_ref[...] = jnp.zeros(grad_gain_two_ref.shape, F32)

    def mix_back(i):
        rows = pl.ds(pl.multiple_of(i * TILE, TILE), TILE)
        layer_out_ref[rows] = result[rows].astype(LOW)
        hat, scale = moments(mixed[rows])
        grad, gain = norm_back(hat, scale, gain_two_ref[...], grad_hidden[rows])
        grad = grad + cot[rows].astype(F32)
        grad_mixed[rows] = grad
        grad_mixed_low[rows] = grad.astype(LOW)
        grad_gain_two_ref[...] = grad_gain_two_ref[...] + gain

    loop(positions // TILE, mix_back)

    shown = pick(ids, dot(out_all[...], grad_mixed_low[...], 1, 1), experts, head)
    grad_out_ref[...] = dot(gated[...], grad_mixed_low[...], 1, 0).astype(LOW)
    attended = total[16:]
    grad_gates = [
        jnp.sum(shown[c] * attended[:, c * positions : (c + 1) * positions], 0, keepdims=True)
        for c in range(2)
    ]
    gates = gates_ref[...]
    soft = [soft_ref[c : c + 1] for c in range(2)]
    kept_grad = [grad_gates[c] * kept[c : c + 1] for c in range(2)]
    inner = soft[0] * kept_grad[0] + soft[1] * kept_grad[1]
    grad_logits = onehots[0] * (soft[0] * (kept_grad[0] - inner)) + onehots[1] * (
        soft[1] * (kept_grad[1] - inner)
    )
    grad_logits_ref[...] = grad_logits
    grad_router_ref[...] = dot(grad_logits, normed[...].astype(F32), 1, 0, HIGH)
    delta = jnp.concatenate([gates[c : c + 1] * grad_gates[c] for c in range(2)], 1)
    grad_attended = jnp.concatenate([gates[c : c + 1] * shown[c] for c in range(2)], 1)
    stacked = jnp.concatenate([blank, grad_attended], 0)
    o_aug[0 : 2 * head] = stacked.astype(LOW)
    o_aug[2 * head :] = jnp.concatenate(
        [jnp.zeros((3, count), F32)] + thirds(-delta) + [jnp.zeros((2 * head - 6, count), F32)], 0
    ).astype(LOW)
    q_rows[count:] = stacked.T.astype(LOW)

    grad_q[...] = jnp.zeros(grad_q.shape, F32)

    def attend_back(slot):
        block, keys = key_block(slot)
        keys_t = block.T[:head]
        part[...] = jnp.zeros(part.shape, F32)

        def one_span(i):
            at = pl.ds(pl.multiple_of(i * SPAN, SPAN), SPAN)
            also = pl.ds(pl.multiple_of(count + i * SPAN, SPAN), SPAN)
            probs = jnp.exp(dot(keys, q_aug[:, at], 1, 0))
            grads = (probs * dot(keys, o_aug[:, at], 1, 0)).astype(LOW)
            grad_q[:, at] = grad_q[:, at] + dot(keys_t, grads, 1, 0)
            part[...] = (
                part[...] + dot(grads, q_rows[at], 1, 0) + dot(probs.astype(LOW), q_rows[also], 1, 0)
            )

        loop(count // SPAN, one_span)

    def pair_copy(k):
        return pltpu.make_async_remote_copy(
            src_ref=kv_out.at[chips + k],
            dst_ref=kv_pair.at[k],
            send_sem=pair_send.at[k],
            recv_sem=pair_recv.at[k],
            device_id=sibling,
            device_id_type=MESH,
        )

    def back_copy(k):
        return pltpu.make_async_remote_copy(
            src_ref=kv_out.at[k],
            dst_ref=kv_in.at[k],
            send_sem=back_send.at[k],
            recv_sem=back_recv.at[k],
            device_id=behind(k),
            device_id_type=MESH,
        )

    def back_chip(step):
        k = lax.rem(step + 1, chips)
        attend_back(2 * k + 1)
        kv_out[chips + k] = part[...].astype(LOW)
        pair_copy(k).start()
        attend_back(2 * k)
        pair_copy(k).wait_recv()
        both = part[...] + kv_pair[k].astype(F32)

        @pl.when(k > 0)
        def _():
            kv_out[k] = both.astype(LOW)
            back_copy(k).start()

        @pl.when(k == 0)
        def _():
            kv_own[...] = both

    loop(chips, back_chip)

    grad_queries = grad_q[...] * SCALE
    grad_spread[...] = spread(
        ids, [grad_queries[:, :positions], grad_queries[:, positions:]], experts
    )
    grad_query_ref[...] = dot(grad_spread[...], normed[...], 1, 0).astype(LOW)

    def add_in(k):
        back_copy(k + 1).wait_recv()
        kv_own[...] = kv_own[...] + kv_in[k + 1].astype(F32)

    loop(chips - 1, add_in)
    grad_kv = kv_own[...].astype(LOW)
    grad_kv_weight_ref[...] = dot(grad_kv, normed[...], 0, 0)
    kv_out[0] = grad_kv

    grad_gain_one_ref[...] = jnp.zeros(grad_gain_one_ref.shape, F32)

    def token_back(i):
        rows = pl.ds(pl.multiple_of(i * TILE, TILE), TILE)
        grad = (
            dot(grad_spread[:, rows], query_all[...], 0, 0)
            + dot(kv_out[0, rows], kv_weight_ref[...], 1, 1)
            + dot(grad_logits_ref[:, rows], router_ref[...].astype(F32), 0, 0, HIGH)
        )
        hat, scale = moments(tokens[rows].astype(F32))
        grad, gain = norm_back(hat, scale, gain_one_ref[...], grad)
        grad_tokens_ref[rows] = grad + grad_mixed[rows]
        grad_gain_one_ref[...] = grad_gain_one_ref[...] + gain

    loop(positions // TILE, token_back)

    kv_copy(0, 1, sibling).wait_send()

    def sent(k):
        kv_copy(0, 2 * (k + 1), ahead(k + 1)).wait_send()
        kv_copy(2 * (k + 1), 2 * (k + 1) + 1, sibling).wait_send()
        back_copy(k + 1).wait_send()

    loop(chips - 1, sent)
    loop(chips, lambda k: pair_copy(k).wait_send())


def shards(
    tokens,
    segments,
    expert_ids,
    keep,
    gain_one,
    kv_weight,
    router_weight,
    query_weight,
    out_weight,
    gain_two,
    up_weight,
    down_weight,
    cotangent,
):
    positions, width = tokens.shape[1:]
    experts, _, head = query_weight.shape
    hidden_units = up_weight.shape[1]
    chips = lax.axis_size("expert") // 2
    chunk = 512
    count = 2 * positions
    query_all = jnp.swapaxes(query_weight, 1, 2).reshape(experts * head, width)
    out_all = jnp.swapaxes(out_weight, 1, 2).reshape(experts * head, width)

    vmem = pl.BlockSpec(memory_space=pltpu.VMEM)
    hbm = pl.BlockSpec(memory_space=pl.ANY)
    dma = pltpu.SemaphoreType.DMA

    def struct(*shape_and_type):
        return jax.ShapeDtypeStruct(shape_and_type[:-1], shape_and_type[-1])

    outs = pl.pallas_call(
        functools.partial(kernel, chips),
        out_shape=(
            struct(positions, width, LOW),
            struct(positions, width, F32),
            struct(1, width, F32),
            struct(2 * head, width, F32),
            struct(experts, width, F32),
            struct(experts * head, width, LOW),
            struct(experts * head, width, LOW),
            struct(1, width, F32),
            struct(width, hidden_units, LOW),
            struct(hidden_units, width, LOW),
        ),
        in_specs=[hbm, vmem, vmem, vmem, vmem, vmem, vmem, hbm, hbm, vmem, hbm, hbm, hbm],
        out_specs=(vmem,) * 10,
        scratch_shapes=[
            pltpu.VMEM((positions, width), LOW),
            pltpu.VMEM((positions, width), LOW),
            pltpu.VMEM((experts * head, width), LOW),
            pltpu.VMEM((experts * head, width), LOW),
            pltpu.VMEM((width, hidden_units), LOW),
            pltpu.VMEM((hidden_units, width), LOW),
            pltpu.VMEM((positions, width), LOW),
            pltpu.VMEM((2 * chips, positions + SEG_ROWS, 2 * head), LOW),
            pltpu.VMEM((4 * head, count), LOW),
            pltpu.VMEM((4 * head, count), LOW),
            pltpu.VMEM((2 * count, 2 * head), LOW),
            pltpu.VMEM((1, count), F32),
            pltpu.VMEM((16 + head, count), F32),
            pltpu.VMEM((2, positions), F32),
            pltpu.VMEM((2, positions), F32),
            pltpu.VMEM((experts * head, positions), LOW),
            pltpu.VMEM((positions, width), F32),
            pltpu.VMEM((positions, width), LOW),
            pltpu.VMEM((width, positions), LOW),
            pltpu.VMEM((positions, chunk), LOW),
            pltpu.VMEM((positions, chunk), LOW),
            pltpu.VMEM((positions, width), F32),
            pltpu.VMEM((positions, width), F32),
            pltpu.VMEM((positions, width), F32),
            pltpu.VMEM((positions, width), LOW),
            pltpu.VMEM((experts, positions), F32),
            pltpu.VMEM((head, count), F32),
            pltpu.VMEM((positions, 2 * head), F32),
            pltpu.VMEM((chips, positions, 2 * head), LOW),
            pltpu.VMEM((2 * chips, positions, 2 * head), LOW),
            pltpu.VMEM((chips, positions, 2 * head), LOW),
            pltpu.VMEM((positions, 2 * head), F32),
            pltpu.VMEM((experts * head, positions), LOW),
            dma((6,)),
            dma((2 * chips,)),
            dma((2 * chips,)),
            dma((chips,)),
            dma((chips,)),
            dma((chips,)),
            dma((chips,)),
        ],
        compiler_params=pltpu.CompilerParams(
            collective_id=0, has_side_effects=True, vmem_limit_bytes=56 << 20
        ),
    )(
        tokens[0],
        segments,
        expert_ids[0].T,
        keep[0].T,
        gain_one[None],
        kv_weight,
        router_weight.T,
        query_all,
        out_all,
        gain_two[None],
        up_weight,
        down_weight,
        cotangent[0],
    )
    big = lax.psum((outs[8], outs[9]), ("dp", "expert"))
    small = lax.psum((outs[2], outs[3], outs[4], outs[7]), ("dp", "expert"))

    def own_part(whole):
        whole = whole.reshape(experts, head, width)
        whole = lax.psum_scatter(whole, "expert", scatter_dimension=2, tiled=True)
        whole = lax.psum_scatter(whole, "dp", scatter_dimension=1, tiled=True)
        return jnp.swapaxes(whole, 1, 2).astype(F32)

    return (
        outs[0][None],
        outs[1][None],
        small[0][0],
        small[1].T,
        small[2].T,
        own_part(outs[5]),
        own_part(outs[6]),
        small[3][0],
        big[0].astype(F32),
        big[1].astype(F32),
    )


def solution(mesh):
    row = P("dp", "expert", None)
    in_specs = (row, P("dp", "expert"), row, row) + (P(),) * 8 + (row,)
    expert = P(None, "expert", "dp")
    out_specs = (row, row, P(), P(), P(), expert, expert, P(), P(), P())
    return jax.shard_map(shards, mesh=mesh, in_specs=in_specs, out_specs=out_specs, check_vma=False)
```

```python
import functools

import jax
import jax.numpy as jnp
from jax import lax
from jax.experimental import pallas as pl
from jax.experimental.pallas import tpu as pltpu
from jax.sharding import PartitionSpec as P

EPS = 1e-05
SCALE = 0.125
NEGATIVE = -1e30
LOW = jnp.bfloat16
F32 = jnp.float32
HIGH = lax.Precision.HIGHEST
MESH = pl.DeviceIdType.MESH
TILE = 128
SPAN = 256
CHUNKS = 4
SEG_ROWS = 16


def dot(left, right, left_dim, right_dim, precision=None):
    return lax.dot_general(
        left,
        right,
        (((left_dim,), (right_dim,)), ((), ())),
        preferred_element_type=F32,
        precision=precision,
    )


def loop(count, body):
    def step(i, carry):
        body(i)
        return carry

    lax.fori_loop(0, count, step, 0)


def moments(values):
    mean = jnp.mean(values, -1, keepdims=True)
    centred = values - mean
    scale = lax.rsqrt(jnp.mean(centred * centred, -1, keepdims=True) + EPS)
    return centred * scale, scale


def norm_back(hat, scale, gain, grad):
    scaled = grad * gain
    inner = jnp.mean(scaled, -1, keepdims=True) + hat * jnp.mean(scaled * hat, -1, keepdims=True)
    return scale * (scaled - inner), jnp.sum(grad * hat, 0, keepdims=True)


def spread(ids, rows, experts):
    pieces = []
    for e in range(experts):
        pieces.append(
            jnp.where(ids[0:1] == e, rows[0], 0.0) + jnp.where(ids[1:2] == e, rows[1], 0.0)
        )
    return jnp.concatenate(pieces, 0).astype(LOW)


def pick(ids, everything, experts, head):
    picked = []
    for c in range(2):
        total = jnp.zeros((head, everything.shape[1]), F32)
        for e in range(experts):
            part = everything[e * head : (e + 1) * head]
            total = total + jnp.where(ids[c : c + 1] == e, part, 0.0)
        picked.append(total)
    return picked


def thirds(values):
    first = values.astype(LOW)
    rest = values - first.astype(F32)
    second = rest.astype(LOW)
    third = (rest - second.astype(F32)).astype(LOW)
    return [first.astype(F32), second.astype(F32), third.astype(F32)]


def gelu_both(x):
    root, cubic = 0.7978845608028654, 0.044715
    square = x * x
    t = jnp.tanh(root * x * (1.0 + cubic * square))
    half = 0.5 * (1.0 + t)
    slope = half + 0.5 * x * (1.0 - t * t) * (root + 3.0 * root * cubic * square)
    return x * half, slope


def kernel(
    chips,
    tokens_hbm,
    segments_ref,
    ids_ref,
    keep_ref,
    gain_one_ref,
    kv_weight_ref,
    router_ref,
    query_hbm,
    out_hbm,
    gain_two_ref,
    up_hbm,
    down_hbm,
    cot_hbm,
    layer_out_ref,
    grad_tokens_ref,
    grad_gain_one_ref,
    grad_kv_weight_ref,
    grad_router_ref,
    grad_query_ref,
    grad_out_ref,
    grad_gain_two_ref,
    grad_up_ref,
    grad_down_ref,
    tokens,
    cot,
    query_all,
    out_all,
    up,
    down,
    normed,
    kv,
    q_aug,
    o_aug,
    q_rows,
    peak,
    total,
    gates_ref,
    soft_ref,
    gated,
    mixed,
    hidden,
    hidden_t,
    act,
    grad_pre,
    result,
    grad_hidden,
    grad_mixed,
    grad_mixed_low,
    grad_logits_ref,
    grad_q,
    part,
    kv_pair,
    kv_out,
    kv_in,
    kv_own,
    grad_spread,
    own,
    whole,
    pair_in,
    near_in,
    far_in,
    line_sum,
    line_in,
    line_whole,
    load_sem,
    kv_send,
    kv_recv,
    pair_send,
    pair_recv,
    back_send,
    back_recv,
    reduce_send,
    reduce_recv,
    line_send,
    line_recv,
    store_sem,
):
    positions, width = tokens.shape
    experts, head = router_ref.shape[0], kv_weight_ref.shape[1] // 2
    dp = lax.axis_index("dp")
    device = lax.axis_index("expert")
    chip, core = device // 2, device % 2
    sibling = (dp, chip * 2 + 1 - core)
    y, x = dp // 2, dp % 2
    beside = [(2 * y + 1 - x, device), (2 * (1 - y) + x, device)]
    place = [x, y]

    def ahead(k):
        return (dp, lax.rem(chip + k, chips) * 2 + core)

    def behind(k):
        return (dp, lax.rem(chip + chips - k, chips) * 2 + core)

    loads = [
        pltpu.make_async_copy(a, b, load_sem.at[i])
        for i, (a, b) in enumerate(
            [
                (tokens_hbm, tokens),
                (query_hbm, query_all),
                (out_hbm, out_all),
                (up_hbm, up),
                (cot_hbm, cot),
                (down_hbm, down),
            ]
        )
    ]
    for load in loads:
        load.start()

    barrier = pltpu.get_barrier_semaphore()
    for peer in [sibling] + beside:
        pl.semaphore_signal(barrier, inc=1, device_id=peer, device_id_type=MESH)
    loop(
        chips - 1,
        lambda k: pl.semaphore_signal(
            barrier, inc=1, device_id=ahead(k + 1), device_id_type=MESH
        ),
    )

    loads[0].wait()

    def norm_rows(i):
        rows = pl.ds(pl.multiple_of(i * TILE, TILE), TILE)
        hat, _ = moments(tokens[rows].astype(F32))
        low = (hat * gain_one_ref[...]).astype(LOW)
        normed[rows] = low
        kv[0, rows] = dot(low, kv_weight_ref[...], 1, 0).astype(LOW)

    loop(positions // TILE, norm_rows)
    segs = segments_ref[...].astype(F32)
    lanes = kv.shape[2]
    seg_rows = [segs[:, i * lanes : (i + 1) * lanes] for i in range(positions // lanes)]
    seg_rows.append(jnp.full((SEG_ROWS - len(seg_rows), lanes), 3.0, F32))
    kv[0, positions:] = jnp.concatenate(seg_rows, 0).astype(LOW)

    pl.semaphore_wait(barrier, chips + 2)

    def kv_copy(source, target, device_id):
        return pltpu.make_async_remote_copy(
            src_ref=kv.at[source],
            dst_ref=kv.at[target],
            send_sem=kv_send.at[target],
            recv_sem=kv_recv.at[target],
            device_id=device_id,
            device_id_type=MESH,
        )

    kv_copy(0, 1, sibling).start()
    loop(chips - 1, lambda k: kv_copy(0, 2 * (k + 1), ahead(k + 1)).start())

    ids = ids_ref[...]
    kept = keep_ref[...].astype(F32)
    loads[1].wait()
    queries = jnp.concatenate(
        pick(ids, dot(query_all[...], normed[...], 1, 1), experts, head), 1
    )
    queries = queries.astype(LOW).astype(F32) * SCALE
    seg_twice = jnp.concatenate([segs, segs], 1)
    count = 2 * positions
    others = [jnp.where(seg_twice == s, 0.0, NEGATIVE) for s in range(3)]
    blank = jnp.zeros((head, count), F32)
    q_aug[0 : 2 * head] = jnp.concatenate([queries, blank], 0).astype(LOW)
    q_aug[2 * head :] = jnp.concatenate(
        others + [jnp.zeros((2 * head - 3, count), F32)], 0
    ).astype(LOW)
    q_rows[0:count] = jnp.concatenate([queries, blank], 0).T.astype(LOW)
    logits = dot(router_ref[...], normed[...], 1, 1)
    places = lax.broadcasted_iota(jnp.int32, logits.shape, 0)
    onehots = [(places == ids[c : c + 1]).astype(F32) for c in range(2)]
    chosen = [jnp.sum(onehots[c] * logits, 0, keepdims=True) for c in range(2)]
    top = jnp.maximum(chosen[0], chosen[1])
    expo = [jnp.exp(chosen[c] - top) for c in range(2)]
    soft_ref[...] = jnp.concatenate([e / (expo[0] + expo[1]) for e in expo], 0)
    gates_ref[...] = soft_ref[...] * kept

    peak[...] = jnp.full(peak.shape, -3e38, F32)
    total[...] = jnp.zeros(total.shape, F32)

    def key_block(slot):
        block = kv[slot, :positions]
        seg = kv[slot, positions:].astype(F32)
        first = jnp.sum(jnp.where(seg < 0.5, 1.0, 0.0), keepdims=True)
        second = jnp.sum(jnp.where(seg < 1.5, 1.0, 0.0), keepdims=True)
        row = lax.broadcasted_iota(jnp.int32, (positions, lanes), 0).astype(F32)
        lane = lax.broadcasted_iota(jnp.int32, (positions, lanes), 1)
        segment = jnp.where(row < first, 0, jnp.where(row < second, 1, 2))
        extra = jnp.where((segment == lane) | ((lane >= 3) & (lane < 6)), 1.0, 0.0)
        return block, jnp.concatenate([block, extra.astype(LOW)], 1)

    def attend(slot):
        block, keys = key_block(slot)
        values_t = jnp.concatenate([jnp.ones((16, positions), LOW), block.T[head:]], 0)

        def one_span(i):
            at = pl.ds(pl.multiple_of(i * SPAN, SPAN), SPAN)
            scores = dot(keys, q_aug[:, at], 1, 0)
            old = peak[:, at]
            new = jnp.maximum(old, jnp.max(scores, 0, keepdims=True))
            probs = jnp.exp(scores - new).astype(LOW)
            total[:, at] = total[:, at] * jnp.exp(old - new) + dot(values_t, probs, 1, 0)
            peak[:, at] = new

        loop(count // SPAN, one_span)

    def attend_chip(k):
        @pl.when(k > 0)
        def _():
            kv_copy(0, 2 * k, ahead(k)).wait_recv()
            kv_copy(2 * k, 2 * k + 1, sibling).start()

        attend(2 * k)
        kv_copy(2 * k, 2 * k + 1, sibling).wait_recv()
        attend(2 * k + 1)

    loop(chips, attend_chip)

    weight = total[0:1]
    attended = total[16:] / weight
    log_total = peak[...] + jnp.log(weight)
    total[16:] = attended
    rows = [thirds(-log_total)[i] for i in range(3)]
    q_aug[2 * head :] = jnp.concatenate(
        others + rows + [jnp.zeros((2 * head - 6, count), F32)], 0
    ).astype(LOW)
    halves = [attended[:, :positions], attended[:, positions:]]
    gates = gates_ref[...]
    gated[...] = spread(ids, [halves[c] * gates[c : c + 1] for c in range(2)], experts)
    loads[2].wait()

    def mix_rows(i):
        rows = pl.ds(pl.multiple_of(i * TILE, TILE), TILE)
        new = tokens[rows].astype(F32) + dot(gated[:, rows], out_all[...], 0, 0)
        mixed[rows] = new
        hat, _ = moments(new)
        low = (hat * gain_two_ref[...]).astype(LOW)
        hidden[rows] = low
        result[rows] = new
        grad_hidden[rows] = jnp.zeros((TILE, width), F32)

    loop(positions // TILE, mix_rows)
    hidden_t[...] = hidden[...].T

    groups, line_rows = line_sum.shape[:2]
    share = line_rows // chips
    each = CHUNKS // groups
    block_rows = own.shape[1]

    def remote(source, target, kind, block, device_id):
        return pltpu.make_async_remote_copy(
            src_ref=source,
            dst_ref=target,
            send_sem=reduce_send.at[kind, block],
            recv_sem=reduce_recv.at[kind, block],
            device_id=device_id,
            device_id_type=MESH,
        )

    def cut(start, size):
        return pl.ds(pl.multiple_of(start, 16), size)

    def low_sum(first, second):
        return (first.astype(F32) + second.astype(F32)).astype(LOW)

    half, quarter, eighth = block_rows // 2, block_rows // 4, block_rows // 8

    def send_pair(b):
        return remote(own.at[b, cut((1 - core) * half, half)], pair_in.at[b], 0, b, sibling)

    def send_near(b, w):
        at = cut(core * half + (1 - place[w]) * quarter, quarter)
        return remote(own.at[b, at], near_in.at[b], 1, b, beside[w])

    def send_far(b, w):
        at = cut(core * half + place[w] * quarter + (1 - place[1 - w]) * eighth, eighth)
        return remote(own.at[b, at], far_in.at[b], 2, b, beside[1 - w])

    def send_line(g, k):
        return pltpu.make_async_remote_copy(
            src_ref=line_sum.at[g, cut(lax.rem(chip + k, chips) * share, share)],
            dst_ref=line_in.at[g, k],
            send_sem=line_send.at[0, g, k],
            recv_sem=line_recv.at[0, g, k],
            device_id=ahead(k),
            device_id_type=MESH,
        )

    def give_line(g, k):
        at = cut(chip * share, share)
        return pltpu.make_async_remote_copy(
            src_ref=line_whole.at[g, at],
            dst_ref=line_whole.at[g, at],
            send_sem=line_send.at[1, g, k],
            recv_sem=line_recv.at[1, g, k],
            device_id=ahead(k),
            device_id_type=MESH,
        )

    def give_far(b, w, g, i):
        at = cut(core * half + place[w] * quarter + place[1 - w] * eighth, eighth)
        return remote(
            line_whole.at[g, cut(i * eighth, eighth)], whole.at[b, at], 3, b, beside[1 - w]
        )

    def give_near(b, w):
        at = cut(core * half + place[w] * quarter, quarter)
        return remote(whole.at[b, at], whole.at[b, at], 4, b, beside[w])

    def give_pair(b):
        at = cut(core * half, half)
        return remote(whole.at[b, at], whole.at[b, at], 5, b, sibling)

    def store(c, w):
        span = cut(c * block_rows, block_rows)
        target = grad_up_ref.at[:, pl.ds(pl.multiple_of(c * block_rows, 128), block_rows)]
        if w:
            target = grad_down_ref.at[span]
        return pltpu.make_async_copy(whole.at[2 * c + w], target, store_sem.at[2 * c + w])

    def stage_0(c):
        for w in range(2):
            send_pair(2 * c + w).start()

    def stage_1(c):
        for w in range(2):
            b = 2 * c + w
            send_pair(b).wait_recv()
            at = cut(core * half, half)
            own[b, at] = low_sum(own[b, at], pair_in[b])
            send_near(b, w).start()

    def stage_2(c):
        for w in range(2):
            b = 2 * c + w
            send_near(b, w).wait_recv()
            at = cut(core * half + place[w] * quarter, quarter)
            own[b, at] = low_sum(own[b, at], near_in[b])
            send_far(b, w).start()

    def stage_3(c):
        g = c // each
        for w in range(2):
            b = 2 * c + w
            send_far(b, w).wait_recv()
            at = cut(core * half + place[w] * quarter + place[1 - w] * eighth, eighth)
            to = cut((lax.rem(c, each) * 2 + w) * eighth, eighth)
            line_sum[g, to] = low_sum(own[b, at], far_in[b])

        @pl.when(lax.rem(c, each) == each - 1)
        def _():
            loop(chips - 1, lambda k: send_line(g, k + 1).start())

    def at_group_end(body):
        def stage(c):
            @pl.when(lax.rem(c, each) == each - 1)
            def _():
                body(c // each)

        return stage

    @at_group_end
    def stage_4(g):
        at = cut(chip * share, share)

        def add_line(k, sum_so_far):
            send_line(g, k).wait_recv()
            return sum_so_far + line_in[g, k].astype(F32)

        line_whole[g, at] = lax.fori_loop(
            1, chips, add_line, line_sum[g, at].astype(F32)
        ).astype(LOW)
        loop(chips - 1, lambda k: give_line(g, k + 1).start())

    @at_group_end
    def stage_5(g):
        loop(chips - 1, lambda k: give_line(g, k + 1).wait_recv())
        for i in range(2 * each):
            w = i % 2
            b = g * 2 * each + i
            at = cut(core * half + place[w] * quarter + place[1 - w] * eighth, eighth)
            whole[b, at] = line_whole[g, i * eighth : (i + 1) * eighth]
            give_far(b, w, g, i).start()

    @at_group_end
    def stage_6(g):
        for i in range(2 * each):
            b = g * 2 * each + i
            give_far(b, i % 2, g, i).wait_recv()
            give_near(b, i % 2).start()

    @at_group_end
    def stage_7(g):
        for i in range(2 * each):
            b = g * 2 * each + i
            give_near(b, i % 2).wait_recv()
            give_pair(b).start()

    @at_group_end
    def stage_8(g):
        for i in range(2 * each):
            b = g * 2 * each + i
            give_pair(b).wait_recv()
            store(g * each + i // 2, i % 2).start()

    stages = [stage_0, stage_1, stage_2, stage_3, stage_4, stage_5, stage_6, stage_7, stage_8]

    def service(turn, least=0, most=len(stages)):
        for i in reversed(range(least, most)):

            @pl.when((turn - i >= 0) & (turn - i < CHUNKS))
            def _():
                stages[i](turn - i)

    for i in (3, 4, 5):
        loads[i].wait()
    chunk = act.shape[1]

    def feed(c):
        units = pl.ds(pl.multiple_of(c * chunk, chunk), chunk)

        def feed_rows(i):
            rows = pl.ds(pl.multiple_of(i * TILE, TILE), TILE)
            value, slope = gelu_both(dot(hidden[rows], up[:, units], 1, 0))
            value = value.astype(LOW)
            grad = (dot(cot[rows], down[units], 1, 1) * slope).astype(LOW)
            act[rows] = value
            grad_pre[rows] = grad
            result[rows] = result[rows] + dot(value, down[units], 1, 0)
            grad_hidden[rows] = grad_hidden[rows] + dot(grad, up[:, units], 1, 1)

        loop(positions // TILE, feed_rows)
        own[2 * c] = dot(hidden_t[...], grad_pre[...], 1, 0).astype(LOW)
        own[2 * c + 1] = dot(act[...], cot[...], 0, 0).astype(LOW)
        service(c, 0, CHUNKS)

    loop(CHUNKS, feed)

    grad_gain_two_ref[...] = jnp.zeros(grad_gain_two_ref.shape, F32)

    def mix_back(i):
        rows = pl.ds(pl.multiple_of(i * TILE, TILE), TILE)
        layer_out_ref[rows] = result[rows].astype(LOW)
        hat, scale = moments(mixed[rows])
        grad, gain = norm_back(hat, scale, gain_two_ref[...], grad_hidden[rows])
        grad = grad + cot[rows].astype(F32)
        grad_mixed[rows] = grad
        grad_mixed_low[rows] = grad.astype(LOW)
        grad_gain_two_ref[...] = grad_gain_two_ref[...] + gain

    loop(positions // TILE, mix_back)

    shown = pick(ids, dot(out_all[...], grad_mixed_low[...], 1, 1), experts, head)
    grad_out_ref[...] = dot(gated[...], grad_mixed_low[...], 1, 0).astype(LOW)
    attended = total[16:]
    grad_gates = [
        jnp.sum(shown[c] * attended[:, c * positions : (c + 1) * positions], 0, keepdims=True)
        for c in range(2)
    ]
    gates = gates_ref[...]
    soft = [soft_ref[c : c + 1] for c in range(2)]
    kept_grad = [grad_gates[c] * kept[c : c + 1] for c in range(2)]
    inner = soft[0] * kept_grad[0] + soft[1] * kept_grad[1]
    grad_logits = onehots[0] * (soft[0] * (kept_grad[0] - inner)) + onehots[1] * (
        soft[1] * (kept_grad[1] - inner)
    )
    grad_logits_ref[...] = grad_logits
    grad_router_ref[...] = dot(grad_logits, normed[...].astype(F32), 1, 0, HIGH)
    delta = jnp.concatenate([gates[c : c + 1] * grad_gates[c] for c in range(2)], 1)
    grad_attended = jnp.concatenate([gates[c : c + 1] * shown[c] for c in range(2)], 1)
    stacked = jnp.concatenate([blank, grad_attended], 0)
    o_aug[0 : 2 * head] = stacked.astype(LOW)
    o_aug[2 * head :] = jnp.concatenate(
        [jnp.zeros((3, count), F32)] + thirds(-delta) + [jnp.zeros((2 * head - 6, count), F32)], 0
    ).astype(LOW)
    q_rows[count:] = stacked.T.astype(LOW)

    service(CHUNKS)

    grad_q[...] = jnp.zeros(grad_q.shape, F32)

    def attend_back(slot):
        block, keys = key_block(slot)
        keys_t = block.T[:head]
        part[...] = jnp.zeros(part.shape, F32)

        def one_span(i):
            at = pl.ds(pl.multiple_of(i * SPAN, SPAN), SPAN)
            also = pl.ds(pl.multiple_of(count + i * SPAN, SPAN), SPAN)
            probs = jnp.exp(dot(keys, q_aug[:, at], 1, 0))
            grads = (probs * dot(keys, o_aug[:, at], 1, 0)).astype(LOW)
            grad_q[:, at] = grad_q[:, at] + dot(keys_t, grads, 1, 0)
            part[...] = (
                part[...] + dot(grads, q_rows[at], 1, 0) + dot(probs.astype(LOW), q_rows[also], 1, 0)
            )

        loop(count // SPAN, one_span)

    def pair_copy(k):
        return pltpu.make_async_remote_copy(
            src_ref=kv_out.at[k],
            dst_ref=kv_pair.at[k],
            send_sem=pair_send.at[k],
            recv_sem=pair_recv.at[k],
            device_id=sibling,
            device_id_type=MESH,
        )

    def back_copy(k):
        return pltpu.make_async_remote_copy(
            src_ref=kv_pair.at[k],
            dst_ref=kv_in.at[k],
            send_sem=back_send.at[k],
            recv_sem=back_recv.at[k],
            device_id=behind(k),
            device_id_type=MESH,
        )

    def back_chip(step):
        k = lax.rem(step + 1, chips)
        attend_back(2 * k + 1)
        kv_out[k] = part[...].astype(LOW)
        pair_copy(k).start()
        attend_back(2 * k)
        pair_copy(k).wait_recv()
        both = part[...] + kv_pair[k].astype(F32)

        @pl.when(k > 0)
        def _():
            kv_pair[k] = both.astype(LOW)
            back_copy(k).start()

        @pl.when(k == 0)
        def _():
            kv_own[...] = both

        service(CHUNKS + 1 + step)

    loop(chips, back_chip)

    grad_queries = grad_q[...] * SCALE
    grad_spread[...] = spread(
        ids, [grad_queries[:, :positions], grad_queries[:, positions:]], experts
    )
    grad_query_ref[...] = dot(grad_spread[...], normed[...], 1, 0).astype(LOW)
    turn = CHUNKS + 1 + chips
    service(turn)

    def add_in(k):
        back_copy(k + 1).wait_recv()
        kv_own[...] = kv_own[...] + kv_in[k + 1].astype(F32)

    loop(chips - 1, add_in)
    grad_kv = kv_own[...].astype(LOW)
    grad_kv_weight_ref[...] = dot(grad_kv, normed[...], 0, 0)
    kv_in[0] = grad_kv

    grad_gain_one_ref[...] = jnp.zeros(grad_gain_one_ref.shape, F32)

    def token_back(i):
        rows = pl.ds(pl.multiple_of(i * TILE, TILE), TILE)
        grad = (
            dot(grad_spread[:, rows], query_all[...], 0, 0)
            + dot(kv_in[0, rows], kv_weight_ref[...], 1, 1)
            + dot(grad_logits_ref[:, rows], router_ref[...].astype(F32), 0, 0, HIGH)
        )
        hat, scale = moments(tokens[rows].astype(F32))
        grad, gain = norm_back(hat, scale, gain_one_ref[...], grad)
        grad_tokens_ref[rows] = grad + grad_mixed[rows]
        grad_gain_one_ref[...] = grad_gain_one_ref[...] + gain

    loop(positions // TILE, token_back)

    for later in range(turn + 1, CHUNKS + len(stages) - 1):
        service(later)

    for c in range(CHUNKS):
        for w in range(2):
            b = 2 * c + w
            g, i = c // each, (c % each) * 2 + w
            send_pair(b).wait_send()
            send_near(b, w).wait_send()
            send_far(b, w).wait_send()
            give_far(b, w, g, i).wait_send()
            give_near(b, w).wait_send()
            give_pair(b).wait_send()
            store(c, w).wait()

    def line_sent(k):
        for g in range(groups):
            send_line(g, k + 1).wait_send()
            give_line(g, k + 1).wait_send()

    loop(chips - 1, line_sent)
    kv_copy(0, 1, sibling).wait_send()

    def sent(k):
        kv_copy(0, 2 * (k + 1), ahead(k + 1)).wait_send()
        kv_copy(2 * (k + 1), 2 * (k + 1) + 1, sibling).wait_send()
        back_copy(k + 1).wait_send()

    loop(chips - 1, sent)
    loop(chips, lambda k: pair_copy(k).wait_send())


def shards(
    tokens,
    segments,
    expert_ids,
    keep,
    gain_one,
    kv_weight,
    router_weight,
    query_weight,
    out_weight,
    gain_two,
    up_weight,
    down_weight,
    cotangent,
):
    positions, width = tokens.shape[1:]
    experts, _, head = query_weight.shape
    hidden_units = up_weight.shape[1]
    chips = lax.axis_size("expert") // 2
    chunk = hidden_units // CHUNKS
    blocks = 2 * CHUNKS
    groups = max(1, min(CHUNKS, blocks * (width // 8) // (16 * chips)))
    line_rows = blocks * (width // 8) // groups
    count = 2 * positions
    query_all = jnp.swapaxes(query_weight, 1, 2).reshape(experts * head, width)
    out_all = jnp.swapaxes(out_weight, 1, 2).reshape(experts * head, width)

    vmem = pl.BlockSpec(memory_space=pltpu.VMEM)
    hbm = pl.BlockSpec(memory_space=pl.ANY)
    dma = pltpu.SemaphoreType.DMA

    def struct(*shape_and_type):
        return jax.ShapeDtypeStruct(shape_and_type[:-1], shape_and_type[-1])

    outs = pl.pallas_call(
        functools.partial(kernel, chips),
        out_shape=(
            struct(positions, width, LOW),
            struct(positions, width, F32),
            struct(1, width, F32),
            struct(2 * head, width, F32),
            struct(experts, width, F32),
            struct(experts * head, width, LOW),
            struct(experts * head, width, LOW),
            struct(1, width, F32),
            struct(width, hidden_units, LOW),
            struct(hidden_units, width, LOW),
        ),
        in_specs=[hbm, vmem, vmem, vmem, vmem, vmem, vmem, hbm, hbm, vmem, hbm, hbm, hbm],
        out_specs=(vmem,) * 8 + (hbm,) * 2,
        scratch_shapes=[
            pltpu.VMEM((positions, width), LOW),
            pltpu.VMEM((positions, width), LOW),
            pltpu.VMEM((experts * head, width), LOW),
            pltpu.VMEM((experts * head, width), LOW),
            pltpu.VMEM((width, hidden_units), LOW),
            pltpu.VMEM((hidden_units, width), LOW),
            pltpu.VMEM((positions, width), LOW),
            pltpu.VMEM((2 * chips, positions + SEG_ROWS, 2 * head), LOW),
            pltpu.VMEM((4 * head, count), LOW),
            pltpu.VMEM((4 * head, count), LOW),
            pltpu.VMEM((2 * count, 2 * head), LOW),
            pltpu.VMEM((1, count), F32),
            pltpu.VMEM((16 + head, count), F32),
            pltpu.VMEM((2, positions), F32),
            pltpu.VMEM((2, positions), F32),
            pltpu.VMEM((experts * head, positions), LOW),
            pltpu.VMEM((positions, width), F32),
            pltpu.VMEM((positions, width), LOW),
            pltpu.VMEM((width, positions), LOW),
            pltpu.VMEM((positions, chunk), LOW),
            pltpu.VMEM((positions, chunk), LOW),
            pltpu.VMEM((positions, width), F32),
            pltpu.VMEM((positions, width), F32),
            pltpu.VMEM((positions, width), F32),
            pltpu.VMEM((positions, width), LOW),
            pltpu.VMEM((experts, positions), F32),
            pltpu.VMEM((head, count), F32),
            pltpu.VMEM((positions, 2 * head), F32),
            pltpu.VMEM((chips, positions, 2 * head), LOW),
            pltpu.VMEM((chips, positions, 2 * head), LOW),
            pltpu.VMEM((chips, positions, 2 * head), LOW),
            pltpu.VMEM((positions, 2 * head), F32),
            pltpu.VMEM((experts * head, positions), LOW),
            pltpu.VMEM((blocks, width, chunk), LOW),
            pltpu.VMEM((blocks, width, chunk), LOW),
            pltpu.VMEM((blocks, width // 2, chunk), LOW),
            pltpu.VMEM((blocks, width // 4, chunk), LOW),
            pltpu.VMEM((blocks, width // 8, chunk), LOW),
            pltpu.VMEM((groups, line_rows, chunk), LOW),
            pltpu.VMEM((groups, chips, line_rows // chips, chunk), LOW),
            pltpu.VMEM((groups, line_rows, chunk), LOW),
            dma((6,)),
            dma((2 * chips,)),
            dma((2 * chips,)),
            dma((chips,)),
            dma((chips,)),
            dma((chips,)),
            dma((chips,)),
            dma((6, blocks)),
            dma((6, blocks)),
            dma((2, groups, chips)),
            dma((2, groups, chips)),
            dma((blocks,)),
        ],
        compiler_params=pltpu.CompilerParams(
            collective_id=0, has_side_effects=True, vmem_limit_bytes=60 << 20
        ),
    )(
        tokens[0],
        segments,
        expert_ids[0].T,
        keep[0].T,
        gain_one[None],
        kv_weight,
        router_weight.T,
        query_all,
        out_all,
        gain_two[None],
        up_weight,
        down_weight,
        cotangent[0],
    )
    small = lax.psum((outs[2], outs[3], outs[4], outs[7]), ("dp", "expert"))

    def own_part(whole):
        whole = whole.reshape(experts, head, width)
        whole = lax.psum_scatter(whole, "expert", scatter_dimension=2, tiled=True)
        whole = lax.psum_scatter(whole, "dp", scatter_dimension=1, tiled=True)
        return jnp.swapaxes(whole, 1, 2).astype(F32)

    return (
        outs[0][None],
        outs[1][None],
        small[0][0],
        small[1].T,
        small[2].T,
        own_part(outs[5]),
        own_part(outs[6]),
        small[3][0],
        outs[8].astype(F32),
        outs[9].astype(F32),
    )


def solution(mesh):
    row = P("dp", "expert", None)
    in_specs = (row, P("dp", "expert"), row, row) + (P(),) * 8 + (row,)
    expert = P(None, "expert", "dp")
    out_specs = (row, row, P(), P(), P(), expert, expert, P(), P(), P())
    return jax.shard_map(shards, mesh=mesh, in_specs=in_specs, out_specs=out_specs, check_vma=False)
```

```python
import functools

import jax
import jax.numpy as jnp
from jax import lax
from jax.experimental import pallas as pl
from jax.experimental.pallas import tpu as pltpu
from jax.sharding import PartitionSpec as P

EPS = 1e-05
SCALE = 0.125
NEGATIVE = -1e30
LOW = jnp.bfloat16
F32 = jnp.float32
HIGH = lax.Precision.HIGHEST
MESH = pl.DeviceIdType.MESH
TILE = 512
SPAN = 1024
STAGES = (0, 2, 6, 9, 14, 19, 22, 26, 28)
EXPERT_STAGES = (0, 2, 5, 8, 12, 14)
CHUNKS = 4
SEG_ROWS = 16


def dot(left, right, left_dim, right_dim, precision=None):
    return lax.dot_general(
        left,
        right,
        (((left_dim,), (right_dim,)), ((), ())),
        preferred_element_type=F32,
        precision=precision,
    )


def loop(count, body):
    def step(i, carry):
        body(i)
        return carry

    lax.fori_loop(0, count, step, 0)


def moments(values):
    mean = jnp.mean(values, -1, keepdims=True)
    centred = values - mean
    scale = lax.rsqrt(jnp.mean(centred * centred, -1, keepdims=True) + EPS)
    return centred * scale, scale


def norm_back(hat, scale, gain, grad):
    scaled = grad * gain
    inner = jnp.mean(scaled, -1, keepdims=True) + hat * jnp.mean(scaled * hat, -1, keepdims=True)
    return scale * (scaled - inner), jnp.sum(grad * hat, 0, keepdims=True)


def spread(ids, rows, experts):
    pieces = []
    for e in range(experts):
        pieces.append(
            jnp.where(ids[0:1] == e, rows[0], 0.0) + jnp.where(ids[1:2] == e, rows[1], 0.0)
        )
    return jnp.concatenate(pieces, 0).astype(LOW)


def pick(ids, everything, experts, head):
    picked = []
    for c in range(2):
        total = jnp.zeros((head, everything.shape[1]), F32)
        for e in range(experts):
            part = everything[e * head : (e + 1) * head]
            total = total + jnp.where(ids[c : c + 1] == e, part, 0.0)
        picked.append(total)
    return picked


def thirds(values):
    first = values.astype(LOW)
    rest = values - first.astype(F32)
    second = rest.astype(LOW)
    third = (rest - second.astype(F32)).astype(LOW)
    return [first.astype(F32), second.astype(F32), third.astype(F32)]


def gelu_both(x):
    root, cubic = 0.7978845608028654, 0.7978845608028654 * 0.044715
    square = x * x
    h = 0.5 + 0.5 * jnp.tanh(x * (root + cubic * square))
    slope = h * (1.0 + (1.0 - h) * (x * (2.0 * root + 6.0 * cubic * square)))
    return x * h, slope


def kernel(
    chips,
    tokens_hbm,
    segments_ref,
    ids_ref,
    keep_ref,
    gain_one_ref,
    kv_weight_ref,
    router_ref,
    query_hbm,
    out_hbm,
    gain_two_ref,
    up_hbm,
    down_hbm,
    cot_hbm,
    layer_out_ref,
    grad_tokens_ref,
    grad_gain_one_ref,
    grad_kv_weight_ref,
    grad_router_ref,
    grad_query_ref,
    grad_out_ref,
    grad_gain_two_ref,
    grad_up_ref,
    grad_down_ref,
    tokens,
    cot,
    query_all,
    out_all,
    up,
    down,
    normed,
    kv,
    q_aug,
    o_aug,
    q_rows,
    peak,
    total,
    gates_ref,
    soft_ref,
    gated,
    mixed,
    hidden,
    hidden_t,
    act,
    grad_pre,
    result,
    grad_hidden,
    grad_mixed,
    grad_mixed_low,
    grad_logits_ref,
    grad_q,
    part,
    kv_pair,
    kv_out,
    kv_in,
    kv_own,
    grad_spread,
    expert_own,
    expert_pair,
    expert_near,
    expert_far,
    expert_line,
    expert_last,
    kv_grad,
    kv_grad_pair,
    kv_grad_dp,
    kv_grad_line,
    kv_grad_whole,
    gain_two,
    vectors,
    vectors_pair,
    vectors_dp,
    vectors_line,
    own,
    whole,
    pair_in,
    near_in,
    far_in,
    line_sum,
    line_in,
    line_whole,
    load_sem,
    kv_send,
    kv_recv,
    pair_send,
    pair_recv,
    back_send,
    back_recv,
    reduce_send,
    reduce_recv,
    line_send,
    line_recv,
    store_sem,
    expert_send,
    expert_recv,
    expert_line_send,
    expert_line_recv,
    late_send,
    late_recv,
    dp_send,
    dp_recv,
    late_line_send,
    late_line_recv,
):
    positions, width = tokens.shape
    experts, head = router_ref.shape[0], kv_weight_ref.shape[1] // 2
    dp = lax.axis_index("dp")
    device = lax.axis_index("expert")
    chip, core = device // 2, device % 2
    sibling = (dp, chip * 2 + 1 - core)
    y, x = dp // 2, dp % 2
    beside = [(2 * y + 1 - x, device), (2 * (1 - y) + x, device)]
    place = [x, y]

    def ahead(k):
        return (dp, lax.rem(chip + k, chips) * 2 + core)

    def behind(k):
        return (dp, lax.rem(chip + chips - k, chips) * 2 + core)

    loads = [
        pltpu.make_async_copy(a, b, load_sem.at[i])
        for i, (a, b) in enumerate(
            [
                (tokens_hbm, tokens),
                (query_hbm, query_all),
                (out_hbm, out_all),
                (up_hbm, up),
                (cot_hbm, cot),
                (down_hbm, down),
            ]
        )
    ]
    for load in loads:
        load.start()

    barrier = pltpu.get_barrier_semaphore()
    dp_count = dp_send.shape[1]
    around = [(lax.rem(dp + k, dp_count), device) for k in range(1, dp_count)]
    for peer in [sibling] + around:
        pl.semaphore_signal(barrier, inc=1, device_id=peer, device_id_type=MESH)
    loop(
        chips - 1,
        lambda k: pl.semaphore_signal(
            barrier, inc=1, device_id=ahead(k + 1), device_id_type=MESH
        ),
    )

    loads[0].wait()

    def norm_rows(i):
        rows = pl.ds(pl.multiple_of(i * TILE, TILE), TILE)
        hat, _ = moments(tokens[rows].astype(F32))
        low = (hat * gain_one_ref[...]).astype(LOW)
        normed[rows] = low
        kv[0, rows] = dot(low, kv_weight_ref[...], 1, 0).astype(LOW)

    loop(positions // TILE, norm_rows)
    segs = segments_ref[...].astype(F32)
    lanes = kv.shape[2]
    seg_rows = [segs[:, i * lanes : (i + 1) * lanes] for i in range(positions // lanes)]
    seg_rows.append(jnp.full((SEG_ROWS - len(seg_rows), lanes), 3.0, F32))
    kv[0, positions:] = jnp.concatenate(seg_rows, 0).astype(LOW)

    pl.semaphore_wait(barrier, chips + dp_count - 1)

    def kv_copy(source, target, device_id):
        return pltpu.make_async_remote_copy(
            src_ref=kv.at[source],
            dst_ref=kv.at[target],
            send_sem=kv_send.at[target],
            recv_sem=kv_recv.at[target],
            device_id=device_id,
            device_id_type=MESH,
        )

    kv_copy(0, 1, sibling).start()
    loop(chips - 1, lambda k: kv_copy(0, 2 * (k + 1), ahead(k + 1)).start())

    ids = ids_ref[...]
    kept = keep_ref[...].astype(F32)
    loads[1].wait()
    queries = jnp.concatenate(
        pick(ids, dot(query_all[...], normed[...], 1, 1), experts, head), 1
    )
    queries = queries.astype(LOW).astype(F32) * SCALE
    seg_twice = jnp.concatenate([segs, segs], 1)
    count = 2 * positions
    others = [jnp.where(seg_twice == s, 0.0, NEGATIVE) for s in range(3)]
    blank = jnp.zeros((head, count), F32)
    q_aug[0 : 2 * head] = jnp.concatenate([queries, blank], 0).astype(LOW)
    q_aug[2 * head :] = jnp.concatenate(
        others + [jnp.zeros((2 * head - 3, count), F32)], 0
    ).astype(LOW)
    q_rows[0:count] = jnp.concatenate([queries, blank], 0).T.astype(LOW)
    logits = dot(router_ref[...], normed[...], 1, 1)
    places = lax.broadcasted_iota(jnp.int32, logits.shape, 0)
    onehots = [(places == ids[c : c + 1]).astype(F32) for c in range(2)]
    chosen = [jnp.sum(onehots[c] * logits, 0, keepdims=True) for c in range(2)]
    top = jnp.maximum(chosen[0], chosen[1])
    expo = [jnp.exp(chosen[c] - top) for c in range(2)]
    soft_ref[...] = jnp.concatenate([e / (expo[0] + expo[1]) for e in expo], 0)
    gates_ref[...] = soft_ref[...] * kept

    peak[...] = jnp.full(peak.shape, -3e38, F32)
    total[...] = jnp.zeros(total.shape, F32)

    def key_block(slot):
        block = kv[slot, :positions]
        seg = kv[slot, positions:].astype(F32)
        first = jnp.sum(jnp.where(seg < 0.5, 1.0, 0.0), keepdims=True)
        second = jnp.sum(jnp.where(seg < 1.5, 1.0, 0.0), keepdims=True)
        row = lax.broadcasted_iota(jnp.int32, (positions, lanes), 0).astype(F32)
        lane = lax.broadcasted_iota(jnp.int32, (positions, lanes), 1)
        segment = jnp.where(row < first, 0, jnp.where(row < second, 1, 2))
        extra = jnp.where((segment == lane) | ((lane >= 3) & (lane < 6)), 1.0, 0.0)
        return block, jnp.concatenate([block, extra.astype(LOW)], 1)

    def attend(slot):
        block, keys = key_block(slot)
        values_t = jnp.concatenate([jnp.ones((16, positions), LOW), block.T[head:]], 0)

        def one_span(i):
            at = pl.ds(pl.multiple_of(i * SPAN, SPAN), SPAN)
            scores = dot(keys, q_aug[:, at], 1, 0)
            old = peak[:, at]
            new = jnp.maximum(old, jnp.max(scores, 0, keepdims=True))
            probs = jnp.exp(scores - new).astype(LOW)
            total[:, at] = total[:, at] * jnp.exp(old - new) + dot(values_t, probs, 1, 0)
            peak[:, at] = new

        loop(count // SPAN, one_span)

    def attend_chip(k):
        @pl.when(k > 0)
        def _():
            kv_copy(0, 2 * k, ahead(k)).wait_recv()
            kv_copy(2 * k, 2 * k + 1, sibling).start()

        attend(2 * k)
        kv_copy(2 * k, 2 * k + 1, sibling).wait_recv()
        attend(2 * k + 1)

    loop(chips, attend_chip)

    weight = total[0:1]
    attended = total[16:] / weight
    log_total = peak[...] + jnp.log(weight)
    total[16:] = attended
    rows = [thirds(-log_total)[i] for i in range(3)]
    q_aug[2 * head :] = jnp.concatenate(
        others + rows + [jnp.zeros((2 * head - 6, count), F32)], 0
    ).astype(LOW)
    halves = [attended[:, :positions], attended[:, positions:]]
    gates = gates_ref[...]
    gated[...] = spread(ids, [halves[c] * gates[c : c + 1] for c in range(2)], experts)
    loads[2].wait()

    def mix_rows(i):
        rows = pl.ds(pl.multiple_of(i * TILE, TILE), TILE)
        new = tokens[rows].astype(F32) + dot(gated[:, rows], out_all[...], 0, 0)
        mixed[rows] = new
        hat, _ = moments(new)
        low = (hat * gain_two_ref[...]).astype(LOW)
        hidden[rows] = low
        result[rows] = new
        grad_hidden[rows] = jnp.zeros((TILE, width), F32)

    loop(positions // TILE, mix_rows)
    hidden_t[...] = hidden[...].T

    groups, line_rows = line_sum.shape[:2]
    share = line_rows // chips
    each = CHUNKS // groups
    block_rows = own.shape[1]

    def remote(source, target, kind, block, device_id):
        return pltpu.make_async_remote_copy(
            src_ref=source,
            dst_ref=target,
            send_sem=reduce_send.at[kind, block],
            recv_sem=reduce_recv.at[kind, block],
            device_id=device_id,
            device_id_type=MESH,
        )

    def cut(start, size):
        return pl.ds(pl.multiple_of(start, 16), size)

    def low_sum(first, second):
        return (first.astype(F32) + second.astype(F32)).astype(LOW)

    half, quarter, eighth = block_rows // 2, block_rows // 4, block_rows // 8

    def send_pair(b):
        return remote(own.at[b, cut((1 - core) * half, half)], pair_in.at[b], 0, b, sibling)

    def send_near(b, w):
        at = cut(core * half + (1 - place[w]) * quarter, quarter)
        return remote(own.at[b, at], near_in.at[b], 1, b, beside[w])

    def send_far(b, w):
        at = cut(core * half + place[w] * quarter + (1 - place[1 - w]) * eighth, eighth)
        return remote(own.at[b, at], far_in.at[b], 2, b, beside[1 - w])

    def send_line(g, k):
        return pltpu.make_async_remote_copy(
            src_ref=line_sum.at[g, cut(lax.rem(chip + k, chips) * share, share)],
            dst_ref=line_in.at[g, k],
            send_sem=line_send.at[0, g, k],
            recv_sem=line_recv.at[0, g, k],
            device_id=ahead(k),
            device_id_type=MESH,
        )

    def give_line(g, k):
        at = cut(chip * share, share)
        return pltpu.make_async_remote_copy(
            src_ref=line_whole.at[g, at],
            dst_ref=line_whole.at[g, at],
            send_sem=line_send.at[1, g, k],
            recv_sem=line_recv.at[1, g, k],
            device_id=ahead(k),
            device_id_type=MESH,
        )

    def give_far(b, w, g, i):
        at = cut(core * half + place[w] * quarter + place[1 - w] * eighth, eighth)
        return remote(
            line_whole.at[g, cut(i * eighth, eighth)], whole.at[b, at], 3, b, beside[1 - w]
        )

    def give_near(b, w):
        at = cut(core * half + place[w] * quarter, quarter)
        return remote(whole.at[b, at], whole.at[b, at], 4, b, beside[w])

    def give_pair(b):
        at = cut(core * half, half)
        return remote(whole.at[b, at], whole.at[b, at], 5, b, sibling)

    def store(c, w):
        span = cut(c * block_rows, block_rows)
        target = grad_up_ref.at[:, pl.ds(pl.multiple_of(c * block_rows, 128), block_rows)]
        if w:
            target = grad_down_ref.at[span]
        return pltpu.make_async_copy(whole.at[2 * c + w], target, store_sem.at[2 * c + w])

    def stage_0(c):
        for w in range(2):
            send_pair(2 * c + w).start()

    def stage_1(c):
        for w in range(2):
            b = 2 * c + w
            send_pair(b).wait_recv()
            at = cut(core * half, half)
            own[b, at] = low_sum(own[b, at], pair_in[b])
            send_near(b, w).start()

    def stage_2(c):
        for w in range(2):
            b = 2 * c + w
            send_near(b, w).wait_recv()
            at = cut(core * half + place[w] * quarter, quarter)
            own[b, at] = low_sum(own[b, at], near_in[b])
            send_far(b, w).start()

    def stage_3(c):
        g = c // each
        for w in range(2):
            b = 2 * c + w
            send_far(b, w).wait_recv()
            at = cut(core * half + place[w] * quarter + place[1 - w] * eighth, eighth)
            to = cut(((c % each) * 2 + w) * eighth, eighth)
            line_sum[g, to] = low_sum(own[b, at], far_in[b])

        if c % each == each - 1:
            loop(chips - 1, lambda k: send_line(g, k + 1).start())

    def at_group_end(body):
        def stage(c):
            if c % each == each - 1:
                body(c // each)

        return stage

    @at_group_end
    def stage_4(g):
        at = cut(chip * share, share)

        def add_line(k, sum_so_far):
            send_line(g, k).wait_recv()
            return sum_so_far + line_in[g, k].astype(F32)

        line_whole[g, at] = lax.fori_loop(
            1, chips, add_line, line_sum[g, at].astype(F32)
        ).astype(LOW)
        loop(chips - 1, lambda k: give_line(g, k + 1).start())

    @at_group_end
    def stage_5(g):
        loop(chips - 1, lambda k: give_line(g, k + 1).wait_recv())
        for i in range(2 * each):
            w = i % 2
            b = g * 2 * each + i
            at = cut(core * half + place[w] * quarter + place[1 - w] * eighth, eighth)
            whole[b, at] = line_whole[g, i * eighth : (i + 1) * eighth]
            give_far(b, w, g, i).start()

    @at_group_end
    def stage_6(g):
        for i in range(2 * each):
            b = g * 2 * each + i
            give_far(b, i % 2, g, i).wait_recv()
            give_near(b, i % 2).start()

    @at_group_end
    def stage_7(g):
        for i in range(2 * each):
            b = g * 2 * each + i
            give_near(b, i % 2).wait_recv()
            give_pair(b).start()

    @at_group_end
    def stage_8(g):
        for i in range(2 * each):
            b = g * 2 * each + i
            give_pair(b).wait_recv()
            store(g * each + i // 2, i % 2).start()

    stages = [stage_0, stage_1, stage_2, stage_3, stage_4, stage_5, stage_6, stage_7, stage_8]

    few = experts // 2

    def expert_cut(a, h, size):
        return expert_own.at[a, pl.ds(core * few, few), cut(h, size)]

    def expert_copy(a, kind, source, target, device_id):
        return pltpu.make_async_remote_copy(
            src_ref=source,
            dst_ref=target,
            send_sem=expert_send.at[a, kind],
            recv_sem=expert_recv.at[a, kind],
            device_id=device_id,
            device_id_type=MESH,
        )

    def expert_to_pair(a):
        source = expert_own.at[a, pl.ds((1 - core) * few, few)]
        return expert_copy(a, 0, source, expert_pair.at[a], sibling)

    def expert_to_near(a):
        source = expert_cut(a, (1 - y) * (head // 2), head // 2)
        return expert_copy(a, 1, source, expert_near.at[a], beside[1])

    def expert_to_far(a):
        source = expert_cut(a, y * (head // 2) + (1 - x) * (head // 4), head // 4)
        return expert_copy(a, 2, source, expert_far.at[a], beside[0])

    fine = width // chips % 128 == 0

    def expert_to_line(a, k):
        at = pl.ds(pl.multiple_of(lax.rem(chip + k, chips) * (width // chips), 128), width // chips)
        return pltpu.make_async_remote_copy(
            src_ref=expert_cut(a, dp * (head // 4), head // 4).at[:, :, at],
            dst_ref=expert_line.at[a, k],
            send_sem=expert_line_send.at[a, k],
            recv_sem=expert_line_recv.at[a, k],
            device_id=ahead(k),
            device_id_type=MESH,
        )

    def expert_to_last(a):
        return expert_copy(a, 3, expert_last.at[a, 0], expert_last.at[a, 1], sibling)

    def expert_0(a):
        expert_to_pair(a).start()

    def expert_add(a, h, size, arrived):
        at = pl.ds(core * few, few), cut(h, size)
        expert_own[(a, *at)] = low_sum(expert_own[(a, *at)], arrived[a])

    def expert_1(a):
        expert_to_pair(a).wait_recv()
        expert_add(a, 0, head, expert_pair)
        expert_to_near(a).start()

    def expert_2(a):
        expert_to_near(a).wait_recv()
        expert_add(a, y * (head // 2), head // 2, expert_near)
        expert_to_far(a).start()

    def expert_3(a):
        expert_to_far(a).wait_recv()
        expert_add(a, dp * (head // 4), head // 4, expert_far)
        if fine:
            loop(chips - 1, lambda k: expert_to_line(a, k + 1).start())

    def expert_4(a):
        if not fine:
            return
        at = pl.ds(pl.multiple_of(chip * (width // chips), 128), width // chips)
        own_part = expert_own[a, pl.ds(core * few, few), cut(dp * (head // 4), head // 4), at]

        def add_line(k, sum_so_far):
            expert_to_line(a, k).wait_recv()
            return sum_so_far + expert_line[a, k].astype(F32)

        expert_last[a, 0] = lax.fori_loop(1, chips, add_line, own_part.astype(F32)).astype(LOW)
        expert_to_last(a).start()

    def expert_5(a):
        target = (grad_out_ref, grad_query_ref)[a]
        if not fine:
            target[...] = expert_own[a, pl.ds(core * few, few), cut(dp * (head // 4), head // 4)]
            return
        expert_to_last(a).wait_recv()
        side = width // chips // 2
        for place_of in range(2):
            mine = expert_last[a, 0].astype(F32)
            other = expert_last[a, 1].astype(F32)
            rows = jnp.where(core == place_of, mine, other)
            target[place_of * few : (place_of + 1) * few] = jnp.where(
                core == 0, rows[:, :, :side], rows[:, :, side:]
            )

    expert_stages = [expert_0, expert_1, expert_2, expert_3, expert_4, expert_5]

    def expert_sent(a):
        expert_to_pair(a).wait_send()
        expert_to_near(a).wait_send()
        expert_to_far(a).wait_send()
        if fine:
            loop(chips - 1, lambda k: expert_to_line(a, k + 1).wait_send())
            expert_to_last(a).wait_send()

    def late_copy(kind, source, target):
        return pltpu.make_async_remote_copy(
            src_ref=source,
            dst_ref=target,
            send_sem=late_send.at[kind],
            recv_sem=late_recv.at[kind],
            device_id=sibling,
            device_id_type=MESH,
        )

    def dp_copy(kind, k, source, target):
        return pltpu.make_async_remote_copy(
            src_ref=source,
            dst_ref=target,
            send_sem=dp_send.at[kind, k],
            recv_sem=dp_recv.at[kind, k],
            device_id=around[k - 1],
            device_id_type=MESH,
        )

    def late_line(kind, k, buffer):
        return pltpu.make_async_remote_copy(
            src_ref=buffer.at[chip],
            dst_ref=buffer.at[chip],
            send_sem=late_line_send.at[kind, k],
            recv_sem=late_line_recv.at[kind, k],
            device_id=ahead(k),
            device_id_type=MESH,
        )

    kv_half = width // 2
    kv_part = kv_half // dp_count
    others_dp = range(1, dp_count)

    def kv_to_pair():
        return late_copy(0, kv_grad.at[cut((1 - core) * kv_half, kv_half)], kv_grad_pair)

    def kv_to_dp(k):
        at = cut(core * kv_half + lax.rem(dp + k, dp_count) * kv_part, kv_part)
        return dp_copy(0, k, kv_grad.at[at], kv_grad_dp.at[k])

    def kv_from_dp(k):
        at = cut(core * kv_half + dp * kv_part, kv_part)
        return dp_copy(1, k, kv_grad_whole.at[at], kv_grad_whole.at[at])

    def kv_from_pair():
        at = cut(core * kv_half, kv_half)
        return late_copy(1, kv_grad_whole.at[at], kv_grad_whole.at[at])

    def kv_0():
        kv_to_pair().start()

    def kv_1():
        kv_to_pair().wait_recv()
        at = cut(core * kv_half, kv_half)
        kv_grad[at] = low_sum(kv_grad[at], kv_grad_pair[...])
        for k in others_dp:
            kv_to_dp(k).start()

    def kv_2():
        summed = kv_grad[cut(core * kv_half + dp * kv_part, kv_part)].astype(F32)
        for k in others_dp:
            kv_to_dp(k).wait_recv()
            summed = summed + kv_grad_dp[k].astype(F32)
        kv_grad_line[chip] = summed.astype(LOW)
        loop(chips - 1, lambda k: late_line(0, k + 1, kv_grad_line).start())

    def kv_3():
        loop(chips - 1, lambda k: late_line(0, k + 1, kv_grad_line).wait_recv())
        summed = lax.fori_loop(
            1,
            chips,
            lambda k, sum_so_far: sum_so_far + kv_grad_line[k].astype(F32),
            kv_grad_line[0].astype(F32),
        )
        kv_grad_whole[cut(core * kv_half + dp * kv_part, kv_part)] = summed
        for k in others_dp:
            kv_from_dp(k).start()

    def kv_4():
        for k in others_dp:
            kv_from_dp(k).wait_recv()
        kv_from_pair().start()

    def kv_5():
        kv_from_pair().wait_recv()
        grad_kv_weight_ref[...] = kv_grad_whole[...]

    def vectors_to_pair():
        return late_copy(2, vectors, vectors_pair)

    def vectors_to_dp(k):
        return dp_copy(2, k, vectors_dp.at[dp], vectors_dp.at[dp])

    def vectors_0():
        vectors_to_pair().start()

    def vectors_1():
        vectors_to_pair().wait_recv()
        vectors_dp[dp] = vectors[...] + vectors_pair[...]
        for k in others_dp:
            vectors_to_dp(k).start()

    def vectors_2():
        for k in others_dp:
            vectors_to_dp(k).wait_recv()
        summed = vectors_dp[0]
        for k in others_dp:
            summed = summed + vectors_dp[k]
        vectors_line[chip] = summed
        loop(chips - 1, lambda k: late_line(1, k + 1, vectors_line).start())

    def vectors_3():
        loop(chips - 1, lambda k: late_line(1, k + 1, vectors_line).wait_recv())
        summed = lax.fori_loop(
            1, chips, lambda k, sum_so_far: sum_so_far + vectors_line[k], vectors_line[0]
        )
        grad_router_ref[...] = summed[0:experts]
        grad_gain_one_ref[...] = summed[experts : experts + 1]
        grad_gain_two_ref[...] = summed[experts + 1 : experts + 2]

    def late_sent():
        kv_to_pair().wait_send()
        kv_from_pair().wait_send()
        vectors_to_pair().wait_send()
        for k in others_dp:
            kv_to_dp(k).wait_send()
            kv_from_dp(k).wait_send()
            vectors_to_dp(k).wait_send()

        def line_sent(k):
            late_line(0, k + 1, kv_grad_line).wait_send()
            late_line(1, k + 1, vectors_line).wait_send()

        loop(chips - 1, line_sent)

    first_turn, block_turn = CHUNKS, CHUNKS + 2
    tail_turn = block_turn + 2 * chips
    events = []
    for c in range(CHUNKS):
        for i in range(len(stages)):
            events.append((c + STAGES[i], functools.partial(stages[i], c)))
    for i in range(len(expert_stages)):
        events.append((first_turn + 1 + EXPERT_STAGES[i], functools.partial(expert_stages[i], 0)))
    events.sort(key=lambda event: event[0])

    def service(turn, least, most):
        for at, event in events:
            if least <= at < most:
                if isinstance(turn, int):
                    if at == turn:
                        event()
                else:
                    pl.when(turn == at)(event)

    for i in (3, 4, 5):
        loads[i].wait()
    chunk = act.shape[1]

    def feed(c):
        units = pl.ds(pl.multiple_of(c * chunk, chunk), chunk)

        def feed_rows(i):
            rows = pl.ds(pl.multiple_of(i * TILE, TILE), TILE)
            value, slope = gelu_both(dot(hidden[rows], up[:, units], 1, 0))
            value = value.astype(LOW)
            grad = (dot(cot[rows], down[units], 1, 1) * slope).astype(LOW)
            act[rows] = value
            grad_pre[rows] = grad
            result[rows] = result[rows] + dot(value, down[units], 1, 0)
            grad_hidden[rows] = grad_hidden[rows] + dot(grad, up[:, units], 1, 1)

        loop(positions // TILE, feed_rows)
        own[2 * c] = dot(hidden_t[...], grad_pre[...], 1, 0).astype(LOW)
        own[2 * c + 1] = dot(act[...], cot[...], 0, 0).astype(LOW)
        service(c, 0, CHUNKS)

    loop(CHUNKS, feed)

    gain_two[...] = jnp.zeros(gain_two.shape, F32)

    def mix_back(i):
        rows = pl.ds(pl.multiple_of(i * TILE, TILE), TILE)
        layer_out_ref[rows] = result[rows].astype(LOW)
        hat, scale = moments(mixed[rows])
        grad, gain = norm_back(hat, scale, gain_two_ref[...], grad_hidden[rows])
        grad = grad + cot[rows].astype(F32)
        grad_mixed[rows] = grad
        grad_mixed_low[rows] = grad.astype(LOW)
        gain_two[...] = gain_two[...] + gain

    loop(positions // TILE, mix_back)

    service(first_turn, first_turn, first_turn + 1)

    shown = pick(ids, dot(out_all[...], grad_mixed_low[...], 1, 1), experts, head)
    grad_out_all = dot(gated[...], grad_mixed_low[...], 1, 0).astype(LOW)
    expert_own[0] = grad_out_all.reshape(experts, head, width)
    attended = total[16:]
    grad_gates = [
        jnp.sum(shown[c] * attended[:, c * positions : (c + 1) * positions], 0, keepdims=True)
        for c in range(2)
    ]
    gates = gates_ref[...]
    soft = [soft_ref[c : c + 1] for c in range(2)]
    kept_grad = [grad_gates[c] * kept[c : c + 1] for c in range(2)]
    inner = soft[0] * kept_grad[0] + soft[1] * kept_grad[1]
    grad_logits = onehots[0] * (soft[0] * (kept_grad[0] - inner)) + onehots[1] * (
        soft[1] * (kept_grad[1] - inner)
    )
    grad_logits_ref[...] = grad_logits
    vectors[...] = jnp.zeros(vectors.shape, F32)
    vectors[0:experts] = dot(grad_logits, normed[...].astype(F32), 1, 0, HIGH)
    vectors[experts + 1 : experts + 2] = gain_two[...]
    delta = jnp.concatenate([gates[c : c + 1] * grad_gates[c] for c in range(2)], 1)
    grad_attended = jnp.concatenate([gates[c : c + 1] * shown[c] for c in range(2)], 1)
    stacked = jnp.concatenate([blank, grad_attended], 0)
    o_aug[0 : 2 * head] = stacked.astype(LOW)
    o_aug[2 * head :] = jnp.concatenate(
        [jnp.zeros((3, count), F32)] + thirds(-delta) + [jnp.zeros((2 * head - 6, count), F32)], 0
    ).astype(LOW)
    q_rows[count:] = stacked.T.astype(LOW)

    service(first_turn + 1, first_turn + 1, block_turn)

    grad_q[...] = jnp.zeros(grad_q.shape, F32)

    def attend_back(slot):
        block, keys = key_block(slot)
        keys_t = block.T[:head]
        part[...] = jnp.zeros(part.shape, F32)

        def one_span(i):
            at = pl.ds(pl.multiple_of(i * SPAN, SPAN), SPAN)
            also = pl.ds(pl.multiple_of(count + i * SPAN, SPAN), SPAN)
            probs = jnp.exp(dot(keys, q_aug[:, at], 1, 0))
            grads = (probs * dot(keys, o_aug[:, at], 1, 0)).astype(LOW)
            grad_q[:, at] = grad_q[:, at] + dot(keys_t, grads, 1, 0)
            part[...] = (
                part[...] + dot(grads, q_rows[at], 1, 0) + dot(probs.astype(LOW), q_rows[also], 1, 0)
            )

        loop(count // SPAN, one_span)

    def pair_copy(k):
        return pltpu.make_async_remote_copy(
            src_ref=kv_out.at[k],
            dst_ref=kv_pair.at[k],
            send_sem=pair_send.at[k],
            recv_sem=pair_recv.at[k],
            device_id=sibling,
            device_id_type=MESH,
        )

    def back_copy(k):
        return pltpu.make_async_remote_copy(
            src_ref=kv_pair.at[k],
            dst_ref=kv_in.at[k],
            send_sem=back_send.at[k],
            recv_sem=back_recv.at[k],
            device_id=behind(k),
            device_id_type=MESH,
        )

    def back_chip(step):
        k = lax.rem(step + 1, chips)
        attend_back(2 * k + 1)
        kv_out[k] = part[...].astype(LOW)
        pair_copy(k).start()
        service(block_turn + 2 * step, block_turn, tail_turn)
        attend_back(2 * k)
        pair_copy(k).wait_recv()
        both = part[...] + kv_pair[k].astype(F32)

        @pl.when(k > 0)
        def _():
            kv_pair[k] = both.astype(LOW)
            back_copy(k).start()

        @pl.when(k == 0)
        def _():
            kv_own[...] = both

        service(block_turn + 2 * step + 1, block_turn, tail_turn)

    loop(chips, back_chip)

    grad_queries = grad_q[...] * SCALE
    grad_spread[...] = spread(
        ids, [grad_queries[:, :positions], grad_queries[:, positions:]], experts
    )
    grad_query_all = dot(grad_spread[...], normed[...], 1, 0).astype(LOW)
    expert_own[1] = grad_query_all.reshape(experts, head, width)
    expert_0(1)
    last_turn = max(at for at, _ in events) + 1

    def tail(turn):
        service(turn, tail_turn, last_turn)

    tail(tail_turn)

    def add_in(k):
        back_copy(k + 1).wait_recv()
        kv_own[...] = kv_own[...] + kv_in[k + 1].astype(F32)

    loop(chips - 1, add_in)
    grad_kv = kv_own[...].astype(LOW)
    kv_grad[...] = dot(normed[...], grad_kv, 0, 0).astype(LOW)
    kv_0()
    kv_in[0] = grad_kv
    expert_1(1)
    tail(tail_turn + 1)

    def token_back(i):
        rows = pl.ds(pl.multiple_of(i * TILE, TILE), TILE)
        grad = (
            dot(grad_spread[:, rows], query_all[...], 0, 0)
            + dot(kv_in[0, rows], kv_weight_ref[...], 1, 1)
            + dot(grad_logits_ref[:, rows], router_ref[...].astype(F32), 0, 0, HIGH)
        )
        hat, scale = moments(tokens[rows].astype(F32))
        grad, gain = norm_back(hat, scale, gain_one_ref[...], grad)
        grad_tokens_ref[rows] = grad + grad_mixed[rows]
        vectors[experts : experts + 1] = vectors[experts : experts + 1] + gain

    loop(positions // TILE, token_back)

    vectors_0()
    kv_1()
    tail(tail_turn + 2)
    expert_2(1)
    tail(tail_turn + 3)
    vectors_1()
    tail(tail_turn + 4)
    kv_2()
    tail(tail_turn + 5)
    expert_3(1)
    tail(tail_turn + 6)
    vectors_2()
    tail(tail_turn + 7)
    kv_3()
    expert_4(1)
    tail(tail_turn + 8)
    vectors_3()
    tail(tail_turn + 9)
    kv_4()
    expert_5(1)
    tail(tail_turn + 10)
    kv_5()
    for turn in range(tail_turn + 11, last_turn):
        tail(turn)

    for c in range(CHUNKS):
        for w in range(2):
            b = 2 * c + w
            g, i = c // each, (c % each) * 2 + w
            send_pair(b).wait_send()
            send_near(b, w).wait_send()
            send_far(b, w).wait_send()
            give_far(b, w, g, i).wait_send()
            give_near(b, w).wait_send()
            give_pair(b).wait_send()
            store(c, w).wait()

    expert_sent(0)
    expert_sent(1)
    late_sent()

    def line_sent(k):
        for g in range(groups):
            send_line(g, k + 1).wait_send()
            give_line(g, k + 1).wait_send()

    loop(chips - 1, line_sent)
    kv_copy(0, 1, sibling).wait_send()

    def sent(k):
        kv_copy(0, 2 * (k + 1), ahead(k + 1)).wait_send()
        kv_copy(2 * (k + 1), 2 * (k + 1) + 1, sibling).wait_send()
        back_copy(k + 1).wait_send()

    loop(chips - 1, sent)
    loop(chips, lambda k: pair_copy(k).wait_send())


def shards(
    tokens,
    segments,
    expert_ids,
    keep,
    gain_one,
    kv_weight,
    router_weight,
    query_weight,
    out_weight,
    gain_two,
    up_weight,
    down_weight,
    cotangent,
):
    positions, width = tokens.shape[1:]
    experts, _, head = query_weight.shape
    hidden_units = up_weight.shape[1]
    chips = lax.axis_size("expert") // 2
    chunk = hidden_units // CHUNKS
    blocks = 2 * CHUNKS
    groups = max(1, min(CHUNKS, blocks * (width // 8) // (16 * chips)))
    line_rows = blocks * (width // 8) // groups
    count = 2 * positions
    query_all = jnp.swapaxes(query_weight, 1, 2).reshape(experts * head, width)
    out_all = jnp.swapaxes(out_weight, 1, 2).reshape(experts * head, width)

    vmem = pl.BlockSpec(memory_space=pltpu.VMEM)
    hbm = pl.BlockSpec(memory_space=pl.ANY)
    dma = pltpu.SemaphoreType.DMA

    def struct(*shape_and_type):
        return jax.ShapeDtypeStruct(shape_and_type[:-1], shape_and_type[-1])

    dps = lax.axis_size("dp")
    few = experts // 2
    fine = width // chips % 128 == 0
    expert_struct = struct(few, head // 4, width, LOW)
    if fine:
        expert_struct = struct(experts, head // 4, width // chips // 2, F32)
    outs = pl.pallas_call(
        functools.partial(kernel, chips),
        out_shape=(
            struct(positions, width, LOW),
            struct(positions, width, F32),
            struct(1, width, F32),
            struct(width, 2 * head, F32),
            struct(experts, width, F32),
            expert_struct,
            expert_struct,
            struct(1, width, F32),
            struct(width, hidden_units, LOW),
            struct(hidden_units, width, LOW),
        ),
        in_specs=[hbm, vmem, vmem, vmem, vmem, vmem, vmem, hbm, hbm, vmem, hbm, hbm, hbm],
        out_specs=(vmem,) * 8 + (hbm,) * 2,
        scratch_shapes=[
            pltpu.VMEM((positions, width), LOW),
            pltpu.VMEM((positions, width), LOW),
            pltpu.VMEM((experts * head, width), LOW),
            pltpu.VMEM((experts * head, width), LOW),
            pltpu.VMEM((width, hidden_units), LOW),
            pltpu.VMEM((hidden_units, width), LOW),
            pltpu.VMEM((positions, width), LOW),
            pltpu.VMEM((2 * chips, positions + SEG_ROWS, 2 * head), LOW),
            pltpu.VMEM((4 * head, count), LOW),
            pltpu.VMEM((4 * head, count), LOW),
            pltpu.VMEM((2 * count, 2 * head), LOW),
            pltpu.VMEM((1, count), F32),
            pltpu.VMEM((16 + head, count), F32),
            pltpu.VMEM((2, positions), F32),
            pltpu.VMEM((2, positions), F32),
            pltpu.VMEM((experts * head, positions), LOW),
            pltpu.VMEM((positions, width), F32),
            pltpu.VMEM((positions, width), LOW),
            pltpu.VMEM((width, positions), LOW),
            pltpu.VMEM((positions, chunk), LOW),
            pltpu.VMEM((positions, chunk), LOW),
            pltpu.VMEM((positions, width), F32),
            pltpu.VMEM((positions, width), F32),
            pltpu.VMEM((positions, width), F32),
            pltpu.VMEM((positions, width), LOW),
            pltpu.VMEM((experts, positions), F32),
            pltpu.VMEM((head, count), F32),
            pltpu.VMEM((positions, 2 * head), F32),
            pltpu.VMEM((chips, positions, 2 * head), LOW),
            pltpu.VMEM((chips, positions, 2 * head), LOW),
            pltpu.VMEM((chips, positions, 2 * head), LOW),
            pltpu.VMEM((positions, 2 * head), F32),
            pltpu.VMEM((experts * head, positions), LOW),
            pltpu.VMEM((2, experts, head, width), LOW),
            pltpu.VMEM((2, few, head, width), LOW),
            pltpu.VMEM((2, few, head // 2, width), LOW),
            pltpu.VMEM((2, few, head // 4, width), LOW),
            pltpu.VMEM((2, chips if fine else 1, few, head // 4, width // chips), LOW),
            pltpu.VMEM((2, 2, few, head // 4, width // chips), LOW),
            pltpu.VMEM((width, 2 * head), LOW),
            pltpu.VMEM((width // 2, 2 * head), LOW),
            pltpu.VMEM((dps, width // 2 // dps, 2 * head), LOW),
            pltpu.VMEM((chips, width // 2 // dps, 2 * head), LOW),
            pltpu.VMEM((width, 2 * head), F32),
            pltpu.VMEM((1, width), F32),
            pltpu.VMEM((2 * experts, width), F32),
            pltpu.VMEM((2 * experts, width), F32),
            pltpu.VMEM((dps, 2 * experts, width), F32),
            pltpu.VMEM((chips, 2 * experts, width), F32),
            pltpu.VMEM((blocks, width, chunk), LOW),
            pltpu.VMEM((blocks, width, chunk), LOW),
            pltpu.VMEM((blocks, width // 2, chunk), LOW),
            pltpu.VMEM((blocks, width // 4, chunk), LOW),
            pltpu.VMEM((blocks, width // 8, chunk), LOW),
            pltpu.VMEM((groups, line_rows, chunk), LOW),
            pltpu.VMEM((groups, chips, line_rows // chips, chunk), LOW),
            pltpu.VMEM((groups, line_rows, chunk), LOW),
            dma((6,)),
            dma((2 * chips,)),
            dma((2 * chips,)),
            dma((chips,)),
            dma((chips,)),
            dma((chips,)),
            dma((chips,)),
            dma((6, blocks)),
            dma((6, blocks)),
            dma((2, groups, chips)),
            dma((2, groups, chips)),
            dma((blocks,)),
            dma((2, 4)),
            dma((2, 4)),
            dma((2, chips)),
            dma((2, chips)),
            dma((3,)),
            dma((3,)),
            dma((3, dps)),
            dma((3, dps)),
            dma((2, chips)),
            dma((2, chips)),
        ],
        compiler_params=pltpu.CompilerParams(
            collective_id=0, has_side_effects=True, vmem_limit_bytes=62 << 20
        ),
    )(
        tokens[0],
        segments,
        expert_ids[0].T,
        keep[0].T,
        gain_one[None],
        kv_weight,
        router_weight.T,
        query_all,
        out_all,
        gain_two[None],
        up_weight,
        down_weight,
        cotangent[0],
    )

    def own_part(reduced):
        if not fine:
            whole = jnp.zeros((2, *reduced.shape), LOW).at[lax.axis_index("expert") % 2].set(reduced)
            whole = whole.reshape(experts, head // 4, width)
            reduced = lax.psum_scatter(whole, "expert", scatter_dimension=2, tiled=True)
        return jnp.swapaxes(reduced, 1, 2).astype(F32)

    return (
        outs[0][None],
        outs[1][None],
        outs[2][0],
        outs[3],
        outs[4].T,
        own_part(outs[5]),
        own_part(outs[6]),
        outs[7][0],
        outs[8].astype(F32),
        outs[9].astype(F32),
    )


def solution(mesh):
    row = P("dp", "expert", None)
    in_specs = (row, P("dp", "expert"), row, row) + (P(),) * 8 + (row,)
    expert = P(None, "expert", "dp")
    out_specs = (row, row, P(), P(), P(), expert, expert, P(), P(), P())
    return jax.shard_map(shards, mesh=mesh, in_specs=in_specs, out_specs=out_specs, check_vma=False)
```

```python
import functools
import types

import jax
import jax.numpy as jnp
from jax import lax
from jax.experimental import pallas as pl
from jax.experimental.pallas import tpu as pltpu
from jax.sharding import PartitionSpec as P

EPS = 1e-05
SCALE = 0.125
NEGATIVE = -1e30
LOW = jnp.bfloat16
F32 = jnp.float32
HIGH = lax.Precision.HIGHEST
MESH = pl.DeviceIdType.MESH
SEG_ROWS = 16
CHUNKS = 8
FEED_PLAN = (
    (),
    (),
    ((1, 0), ),
    ((1, 1), ),
    ((1, 2), ),
    ((1, 3), ),
    ((2, 0), (1, 4), (1, 5), (2, 1), ),
    ((1, 6), (2, 2), ),
)
MIX_PLAN = ()
GATE_PLAN = ((3, 0), (2, 3), (2, 4), (1, 7), )
BLOCK_PLAN = (
    (("e1", 0), (3, 1), (2, 5), ),
    ((2, 6), (4, 0), ),
    ((3, 2), (3, 3), ),
    ((4, 1), (3, 4), ),
    ((2, 7), ),
    (),
    (("e2", 0), (4, 2), ),
    ((4, 3), (5, 0), (3, 5), (3, 6), (3, 7), ),
)
TAIL_PLAN = (
    ("q",),
    ("e3", 0),
    (4, 4),
    ("e1", 1),
    (5, 1),
    (4, 5),
    (4, 6),
    ("e2", 1),
    (4, 7),
    ("k",),
    (5, 2),
    ("t",),
    ("k1",),
    (6, 0),
    (5, 3),
    ("v1",),
    ("e4", 0),
    ("e3", 1),
    (5, 4),
    (6, 1),
    ("e5", 0),
    (5, 5),
    (5, 6),
    (7, 0),
    ("k2",),
    (5, 7),
    ("v2",),
    (6, 2),
    (6, 3),
    (7, 1),
    (8, 0),
    ("e4", 1),
    (6, 4),
    (6, 5),
    ("e5", 1),
    (6, 6),
    (8, 1),
    (7, 2),
    (7, 3),
    ("k3",),
    (9, 0),
    (6, 7),
    (7, 4),
    (7, 5),
    (7, 6),
    ("v3",),
    (10, 0),
    (9, 1),
    (8, 2),
    (7, 7),
    (8, 3),
    (10, 1),
    ("k4",),
    (8, 4),
    (8, 5),
    ("k5",),
    (8, 6),
    (9, 2),
    (8, 7),
    (10, 2),
    (9, 3),
    (9, 4),
    (10, 3),
    (9, 5),
    (10, 4),
    (9, 6),
    (10, 5),
    (9, 7),
    (10, 6),
    (10, 7),
)

def dot(left, right, left_dim, right_dim, precision=None):
    return lax.dot_general(
        left,
        right,
        (((left_dim,), (right_dim,)), ((), ())),
        preferred_element_type=F32,
        precision=precision,
    )


def loop(count, body):
    def step(i, carry):
        body(i)
        return carry

    lax.fori_loop(0, count, step, 0)


def moments(values):
    mean = jnp.mean(values, -1, keepdims=True)
    centred = values - mean
    scale = lax.rsqrt(jnp.mean(centred * centred, -1, keepdims=True) + EPS)
    return centred * scale, scale


def norm_back(hat, scale, gain, grad):
    scaled = grad * gain
    inner = jnp.mean(scaled, -1, keepdims=True) + hat * jnp.mean(scaled * hat, -1, keepdims=True)
    return scale * (scaled - inner), jnp.sum(grad * hat, 0, keepdims=True)


def spread(ids, rows, experts):
    pieces = []
    for e in range(experts):
        pieces.append(
            jnp.where(ids[0:1] == e, rows[0], 0.0) + jnp.where(ids[1:2] == e, rows[1], 0.0)
        )
    return jnp.concatenate(pieces, 0).astype(LOW)


def pick(ids, everything, experts, head):
    picked = []
    for c in range(2):
        total = jnp.zeros((head, everything.shape[1]), F32)
        for e in range(experts):
            part = everything[e * head : (e + 1) * head]
            total = total + jnp.where(ids[c : c + 1] == e, part, 0.0)
        picked.append(total)
    return picked


def thirds(values):
    first = values.astype(LOW)
    rest = values - first.astype(F32)
    second = rest.astype(LOW)
    third = (rest - second.astype(F32)).astype(LOW)
    return [first.astype(F32), second.astype(F32), third.astype(F32)]


def gelu_both(x):
    root, cubic = 0.7978845608028654, 0.7978845608028654 * 0.044715
    square = x * x
    h = 0.5 + 0.5 * jnp.tanh(x * (root + cubic * square))
    slope = h * (1.0 + (1.0 - h) * (x * (2.0 * root + 6.0 * cubic * square)))
    return x * h, slope


def low_sum(first, second):
    return (first.astype(F32) + second.astype(F32)).astype(LOW)


def cut(start, size):
    return pl.ds(pl.multiple_of(start, 16), size)


class Links:
    def __init__(self, send, recv):
        self.send, self.recv = send, recv

    def start(self, kind, place, source, target, device_id):
        pltpu.make_async_remote_copy(
            src_ref=source,
            dst_ref=target,
            send_sem=self.send.at[kind],
            recv_sem=self.recv.at[kind, place],
            device_id=device_id,
            device_id_type=MESH,
        ).start()

    def arrived(self, kind, place, ref):
        pltpu.make_async_copy(ref, ref, self.recv.at[kind, place]).wait()

    def sent(self, kind, ref):
        pltpu.make_async_copy(ref, ref, self.send.at[kind]).wait()


def kernel(chips, experts, names, *refs):
    r = types.SimpleNamespace(**dict(zip(names, refs, strict=True)))
    positions, width = r.tokens.shape
    head = r.kv_weight.shape[1] // 2
    count = 2 * positions
    dp, device = lax.axis_index("dp"), lax.axis_index("expert")
    chip, core = device // 2, device % 2
    y, x = dp // 2, dp % 2
    place = [x, y]
    sibling = (dp, chip * 2 + 1 - core)
    beside = [(2 * y + 1 - x, device), (2 * (1 - y) + x, device)]
    dp_count = r.kv_grad_dp.shape[0]
    around = [(lax.rem(dp + k, dp_count), device) for k in range(1, dp_count)]

    def ahead(k):
        return (dp, lax.rem(chip + k, chips) * 2 + core)

    def behind(k):
        return (dp, lax.rem(chip + chips - k, chips) * 2 + core)

    loads = {}
    for i, name in enumerate(LOADS):
        loads[name] = pltpu.make_async_copy(
            getattr(r, name + "_hbm"), getattr(r, name), r.load_sem.at[i]
        )
        loads[name].start()

    def loaded(*wanted):
        for name in wanted:
            loads[name].wait()

    barrier = pltpu.get_barrier_semaphore()
    for peer in [sibling] + around:
        pl.semaphore_signal(barrier, inc=1, device_id=peer, device_id_type=MESH)
    loop(
        chips - 1,
        lambda k: pl.semaphore_signal(
            barrier, inc=1, device_id=ahead(k + 1), device_id_type=MESH
        ),
    )

    loaded("tokens", "gain_one", "kv_weight", "segments")
    normed = (moments(r.tokens[...].astype(F32))[0] * r.gain_one[...]).astype(LOW)
    r.normed[...] = normed
    r.kv[0, :positions] = dot(normed, r.kv_weight[...], 1, 0).astype(LOW)
    segs = r.segments[...].astype(F32)
    lanes = 2 * head
    seg_rows = [segs[:, i * lanes : (i + 1) * lanes] for i in range(positions // lanes)]
    seg_rows.append(jnp.full((SEG_ROWS - len(seg_rows), lanes), 3.0, F32))
    r.kv[0, positions:] = jnp.concatenate(seg_rows, 0).astype(LOW)

    pl.semaphore_wait(barrier, chips + dp_count - 1)

    kv_links = Links(r.kv_send, r.kv_recv)

    def kv_copy(source, target, device_id):
        kv_links.start(0, target, r.kv.at[source], r.kv.at[target], device_id)

    kv_copy(0, 1, sibling)
    loop(chips - 1, lambda k: kv_copy(0, 2 * (k + 1), ahead(k + 1)))

    loaded("query_all", "ids", "keep", "router")
    ids = r.ids[...]
    kept = r.keep[...].astype(F32)
    queries = jnp.concatenate(
        pick(ids, dot(r.query_all[...], r.normed[...], 1, 1), experts, head), 1
    )
    queries = queries.astype(LOW).astype(F32) * SCALE
    seg_twice = jnp.concatenate([segs, segs], 1)
    others = [jnp.where(seg_twice == s, 0.0, NEGATIVE) for s in range(3)]
    blank = jnp.zeros((head, count), F32)
    r.q_aug[0 : 2 * head] = jnp.concatenate([queries, blank], 0).astype(LOW)
    r.q_aug[2 * head :] = jnp.concatenate(
        others + [jnp.zeros((2 * head - 3, count), F32)], 0
    ).astype(LOW)
    r.q_rows[0:count] = jnp.concatenate([queries, blank], 0).T.astype(LOW)
    logits = dot(r.router[...], r.normed[...], 1, 1)
    places = lax.broadcasted_iota(jnp.int32, logits.shape, 0)
    onehots = [(places == ids[c : c + 1]).astype(F32) for c in range(2)]
    chosen = [jnp.sum(onehots[c] * logits, 0, keepdims=True) for c in range(2)]
    top = jnp.maximum(chosen[0], chosen[1])
    expo = [jnp.exp(chosen[c] - top) for c in range(2)]
    r.soft[...] = jnp.concatenate([e / (expo[0] + expo[1]) for e in expo], 0)
    r.gates[...] = r.soft[...] * kept

    r.peak[...] = jnp.full(r.peak.shape, -3e38, F32)
    r.total[...] = jnp.zeros(r.total.shape, F32)

    def key_block(slot):
        block = r.kv[slot, :positions]
        seg = r.kv[slot, positions:].astype(F32)
        first = jnp.sum(jnp.where(seg < 0.5, 1.0, 0.0), keepdims=True)
        second = jnp.sum(jnp.where(seg < 1.5, 1.0, 0.0), keepdims=True)
        row = lax.broadcasted_iota(jnp.int32, (positions, lanes), 0).astype(F32)
        lane = lax.broadcasted_iota(jnp.int32, (positions, lanes), 1)
        segment = jnp.where(row < first, 0, jnp.where(row < second, 1, 2))
        extra = jnp.where((segment == lane) | ((lane >= 3) & (lane < 6)), 1.0, 0.0)
        return block, jnp.concatenate([block, extra.astype(LOW)], 1)

    def attend(slot):
        block, keys = key_block(slot)
        values_t = jnp.concatenate([jnp.ones((16, positions), LOW), block.T[head:]], 0)
        scores = dot(keys, r.q_aug[...], 1, 0)
        old = r.peak[...]
        new = jnp.maximum(old, jnp.max(scores, 0, keepdims=True))
        probs = jnp.exp(scores - new).astype(LOW)
        r.total[...] = r.total[...] * jnp.exp(old - new) + dot(values_t, probs, 1, 0)
        r.peak[...] = new

    def attend_chip(k):
        @pl.when(k > 0)
        def _():
            kv_links.arrived(0, 2 * k, r.kv.at[2 * k])
            kv_copy(2 * k, 2 * k + 1, sibling)

        attend(2 * k)
        kv_links.arrived(0, 2 * k + 1, r.kv.at[2 * k + 1])
        attend(2 * k + 1)

    loop(chips, attend_chip)

    weight = r.total[0:1]
    attended = r.total[16:] / weight
    log_total = r.peak[...] + jnp.log(weight)
    r.total[16:] = attended
    r.q_aug[2 * head :] = jnp.concatenate(
        others + thirds(-log_total) + [jnp.zeros((2 * head - 6, count), F32)], 0
    ).astype(LOW)
    halves = [attended[:, :positions], attended[:, positions:]]
    gates = r.gates[...]
    r.gated[...] = spread(ids, [halves[c] * gates[c : c + 1] for c in range(2)], experts)
    loaded("out_all", "gain_two")
    mixed = r.tokens[...].astype(F32) + dot(r.gated[...], r.out_all[...], 0, 0)
    r.mixed[...] = mixed
    r.result[...] = mixed
    hidden = (moments(mixed)[0] * r.gain_two[...]).astype(LOW)
    r.hidden[...] = hidden
    r.hidden_t[...] = hidden.T
    r.grad_hidden[...] = jnp.zeros(r.grad_hidden.shape, F32)

    groups, line_rows = r.line_sum.shape[:2]
    each = CHUNKS // groups
    near_rows = line_rows // 2
    share = line_rows // chips
    side, turn_of = chip % 2, chip // 2
    next_chip = (dp, (chip + 1 - 2 * side) * 2 + core)
    half, quarter, eighth = width // 2, width // 4, width // 8
    halving = Links(r.halving_send, r.halving_recv)
    line = Links(r.line_send, r.line_recv)

    PAIR, NEAR, FAR, FAR_BACK, NEAR_BACK, PAIR_BACK = range(6)
    NEXT, LINE, LINE_BACK, NEXT_BACK = range(4)

    def both_of(c):
        return pl.ds(2 * c, 2)

    def stage_0(c):
        for w in range(2):
            b = 2 * c + w
            source = r.own.at[b, cut((1 - core) * half, half)]
            halving.start(PAIR, c, source, r.pair_in.at[b], sibling)

    def stage_1(c):
        halving.arrived(PAIR, c, r.pair_in.at[both_of(c)])
        for w in range(2):
            b = 2 * c + w
            at = cut(core * half, half)
            r.own[b, at] = low_sum(r.own[b, at], r.pair_in[b])
            source = r.own.at[b, cut(core * half + (1 - place[w]) * quarter, quarter)]
            halving.start(NEAR, c, source, r.near_in.at[b], beside[w])

    def stage_2(c):
        halving.arrived(NEAR, c, r.near_in.at[both_of(c)])
        for w in range(2):
            b = 2 * c + w
            at = cut(core * half + place[w] * quarter, quarter)
            r.own[b, at] = low_sum(r.own[b, at], r.near_in[b])
            to = core * half + place[w] * quarter + (1 - place[1 - w]) * eighth
            source = r.own.at[b, cut(to, eighth)]
            halving.start(FAR, c, source, r.far_in.at[b], beside[1 - w])

    def stage_3(c):
        g = c // each
        halving.arrived(FAR, c, r.far_in.at[both_of(c)])
        for w in range(2):
            b = 2 * c + w
            at = cut(core * half + place[w] * quarter + place[1 - w] * eighth, eighth)
            to = (c % each * 2 + w) * eighth
            r.line_sum[g, to : to + eighth] = low_sum(r.own[b, at], r.far_in[b])
        if c % each == each - 1:
            source = r.line_sum.at[g, cut((1 - side) * near_rows, near_rows)]
            line.start(NEXT, g, source, r.next_in.at[g], next_chip)

    def at_group_end(body):
        def stage(c):
            if c % each == each - 1:
                body(c // each)

        return stage

    my_rows = cut(side * near_rows, near_rows)
    my_share = cut(side * near_rows + turn_of * share, share)
    same_side = chips // 2

    @at_group_end
    def stage_4(g):
        line.arrived(NEXT, g, r.next_in.at[g])
        r.line_sum[g, my_rows] = low_sum(r.line_sum[g, my_rows], r.next_in[g])

        def send_share(k):
            at = side * near_rows + lax.rem(turn_of + k + 1, same_side) * share
            source = r.line_sum.at[g, cut(at, share)]
            line.start(LINE, g, source, r.line_in.at[g, k], ahead(2 * (k + 1)))

        loop(same_side - 1, send_share)

    @at_group_end
    def stage_5(g):
        if same_side > 1:
            line.arrived(LINE, g, r.line_in.at[g])

        def add_line(k, sum_so_far):
            return sum_so_far + r.line_in[g, k].astype(F32)

        summed = lax.fori_loop(0, same_side - 1, add_line, r.line_sum[g, my_share].astype(F32))
        r.line_whole[g, my_share] = summed.astype(LOW)

        def give_share(k):
            ref = r.line_whole.at[g, my_share]
            line.start(LINE_BACK, g, ref, ref, ahead(2 * (k + 1)))

        loop(same_side - 1, give_share)

    @at_group_end
    def stage_6(g):
        if same_side > 1:
            line.arrived(LINE_BACK, g, r.line_in.at[g])
        ref = r.line_whole.at[g, my_rows]
        line.start(NEXT_BACK, g, ref, ref, next_chip)

    def blocks_of(g):
        for i in range(2 * each):
            yield i, i % 2, g * 2 * each + i

    def group_at(g):
        return pl.ds(g * 2 * each, 2 * each)

    @at_group_end
    def stage_7(g):
        line.arrived(NEXT_BACK, g, r.next_in.at[g])
        for i, w, b in blocks_of(g):
            at = cut(core * half + place[w] * quarter + place[1 - w] * eighth, eighth)
            r.whole[b, at] = r.line_whole[g, i * eighth : (i + 1) * eighth]
            source = r.line_whole.at[g, i * eighth : (i + 1) * eighth]
            halving.start(FAR_BACK, g, source, r.whole.at[b, at], beside[1 - w])

    @at_group_end
    def stage_8(g):
        halving.arrived(FAR_BACK, g, r.far_in.at[group_at(g)])
        for i, w, b in blocks_of(g):
            ref = r.whole.at[b, cut(core * half + place[w] * quarter, quarter)]
            halving.start(NEAR_BACK, g, ref, ref, beside[w])

    @at_group_end
    def stage_9(g):
        halving.arrived(NEAR_BACK, g, r.near_in.at[group_at(g)])
        for i, w, b in blocks_of(g):
            ref = r.whole.at[b, cut(core * half, half)]
            halving.start(PAIR_BACK, g, ref, ref, sibling)

    @at_group_end
    def stage_10(g):
        halving.arrived(PAIR_BACK, g, r.pair_in.at[group_at(g)])
        for i, w, b in blocks_of(g):
            pltpu.make_async_copy(r.whole.at[b], r.big_hbm.at[b], r.store_sem.at[0]).start()

    def big_sent():
        for kind in (PAIR, PAIR_BACK):
            halving.sent(kind, r.pair_in)
        for kind in (NEAR, NEAR_BACK):
            halving.sent(kind, r.near_in)
        for kind in (FAR, FAR_BACK):
            halving.sent(kind, r.far_in)
        for kind in (NEXT, NEXT_BACK):
            line.sent(kind, r.next_in)
        if same_side > 1:
            for kind in (LINE, LINE_BACK):
                line.sent(kind, r.line_in)
        pltpu.make_async_copy(r.whole, r.big_hbm, r.store_sem.at[0]).wait()

    few = experts // 2
    my_experts = pl.ds(core * few, few)
    fine = width // chips % 128 == 0
    expert_links = Links(r.expert_send, r.expert_recv)
    EXPERT_PAIR, EXPERT_NEAR, EXPERT_FAR, EXPERT_LINE, EXPERT_LAST = range(5)

    def expert_half(a, first, second):
        if a == 0:
            if second is None:
                return (a, my_experts, first)
            return (a, my_experts, first, second)
        if second is None:
            return (a, my_experts, slice(None), first)
        return (a, my_experts, second, first)

    order = [(y, x), (x, y)]
    sides = [(beside[1], beside[0]), (beside[0], beside[1])]

    def expert_columns(c):
        return pl.ds(pl.multiple_of(c * (width // chips), 128), width // chips)

    def expert_0(a):
        source = r.expert_own.at[a, pl.ds((1 - core) * few, few)]
        expert_links.start(EXPERT_PAIR, a, source, r.expert_pair.at[a], sibling)

    def expert_1(a):
        expert_links.arrived(EXPERT_PAIR, a, r.expert_pair.at[a])
        r.expert_own[a, my_experts] = low_sum(r.expert_own[a, my_experts], r.expert_pair[a])
        source = r.expert_own.at[expert_half(a, 1 - order[a][0], None)]
        expert_links.start(EXPERT_NEAR, a, source, r.expert_near.at[a], sides[a][0])

    def expert_2(a):
        expert_links.arrived(EXPERT_NEAR, a, r.expert_near.at[a])
        at = expert_half(a, order[a][0], None)
        r.expert_own[at] = low_sum(r.expert_own[at], r.expert_near[a])
        source = r.expert_own.at[expert_half(a, order[a][0], 1 - order[a][1])]
        expert_links.start(EXPERT_FAR, a, source, r.expert_far.at[a], sides[a][1])

    def expert_3(a):
        expert_links.arrived(EXPERT_FAR, a, r.expert_far.at[a])
        at = expert_half(a, *order[a])
        r.expert_quarter[a] = low_sum(r.expert_own[at], r.expert_far[a])

        def send_columns(k):
            source = r.expert_quarter.at[a, :, :, expert_columns(lax.rem(chip + k + 1, chips))]
            expert_links.start(EXPERT_LINE, a, source, r.expert_line.at[a, k], ahead(k + 1))

        if fine:
            loop(chips - 1, send_columns)

    def expert_4(a):
        if not fine:
            return
        expert_links.arrived(EXPERT_LINE, a, r.expert_line.at[a])

        def add_line(k, sum_so_far):
            return sum_so_far + r.expert_line[a, k].astype(F32)

        own_part = r.expert_quarter[a, :, :, expert_columns(chip)].astype(F32)
        r.expert_last[a, 0] = lax.fori_loop(0, chips - 1, add_line, own_part).astype(LOW)
        source, target = r.expert_last.at[a, 0], r.expert_last.at[a, 1]
        expert_links.start(EXPERT_LAST, a, source, target, sibling)

    def expert_5(a):
        if fine:
            expert_links.arrived(EXPERT_LAST, a, r.expert_last.at[a, 1])
            part = width // chips // 2
            mine = r.expert_last[a, 0].astype(F32)
            other = r.expert_last[a, 1].astype(F32)
            for i in range(2):
                rows = jnp.where(core == i, mine, other)
                r.expert_out[a, i * few : (i + 1) * few] = jnp.where(
                    core == 0, rows[:, :, :part], rows[:, :, part:]
                )
        else:
            r.expert_out[a] = r.expert_quarter[a]
        pltpu.make_async_copy(r.expert_out.at[a], r.experts_hbm.at[a], r.store_sem.at[1 + a]).start()

    def expert_sent():
        expert_links.sent(EXPERT_PAIR, r.expert_pair)
        expert_links.sent(EXPERT_NEAR, r.expert_near)
        expert_links.sent(EXPERT_FAR, r.expert_far)
        if fine:
            expert_links.sent(EXPERT_LINE, r.expert_line)
            expert_links.sent(EXPERT_LAST, r.expert_last.at[:, 0])
        for a in range(2):
            pltpu.make_async_copy(
                r.expert_out.at[a], r.experts_hbm.at[a], r.store_sem.at[1 + a]
            ).wait()

    late = Links(r.late_send, r.late_recv)
    KV_PAIR, KV_DP, KV_LINE, KV_DP_BACK, KV_PAIR_BACK, VEC_PAIR, VEC_DP, VEC_LINE = range(8)
    kv_half = width // 2
    kv_part = kv_half // dp_count
    others_dp = range(1, dp_count)
    kv_mine = cut(core * kv_half, kv_half)
    kv_share = cut(core * kv_half + dp * kv_part, kv_part)

    def kv_0():
        source = r.kv_grad.at[cut((1 - core) * kv_half, kv_half)]
        late.start(KV_PAIR, 0, source, r.kv_grad_pair, sibling)

    def kv_1():
        late.arrived(KV_PAIR, 0, r.kv_grad_pair)
        r.kv_grad[kv_mine] = low_sum(r.kv_grad[kv_mine], r.kv_grad_pair[...])
        for k in others_dp:
            at = cut(core * kv_half + lax.rem(dp + k, dp_count) * kv_part, kv_part)
            late.start(KV_DP, 0, r.kv_grad.at[at], r.kv_grad_dp.at[k], around[k - 1])

    def to_line(kind, buffer, value):
        buffer[chip] = value.astype(LOW)
        ref = buffer.at[chip]
        loop(chips - 1, lambda k: late.start(kind, 0, ref, ref, ahead(k + 1)))

    def from_line(kind, buffer):
        late.arrived(kind, 0, buffer.at[1:])

        def add(k, sum_so_far):
            return sum_so_far + buffer[k].astype(F32)

        return lax.fori_loop(1, chips, add, buffer[0].astype(F32))

    def kv_2():
        late.arrived(KV_DP, 0, r.kv_grad_dp.at[1:])
        summed = r.kv_grad[kv_share].astype(F32)
        for k in others_dp:
            summed = summed + r.kv_grad_dp[k].astype(F32)
        to_line(KV_LINE, r.kv_grad_line, summed)

    def kv_3():
        r.kv_grad_whole[kv_share] = from_line(KV_LINE, r.kv_grad_line).astype(LOW)
        ref = r.kv_grad_whole.at[kv_share]
        for k in others_dp:
            late.start(KV_DP_BACK, 0, ref, ref, around[k - 1])

    def kv_4():
        late.arrived(KV_DP_BACK, 0, r.kv_grad_dp.at[1:])
        ref = r.kv_grad_whole.at[kv_mine]
        late.start(KV_PAIR_BACK, 0, ref, ref, sibling)

    def kv_store():
        return pltpu.make_async_copy(r.kv_grad_whole, r.kv_hbm, r.out_sem.at[2])

    def kv_5():
        late.arrived(KV_PAIR_BACK, 0, r.kv_grad_pair)
        kv_store().start()

    def vectors_store():
        return pltpu.make_async_copy(r.vectors_whole, r.vectors_hbm, r.out_sem.at[3])

    def vectors_0():
        late.start(VEC_PAIR, 0, r.vectors, r.vectors_pair, sibling)

    def vectors_1():
        late.arrived(VEC_PAIR, 0, r.vectors_pair)
        r.vectors_dp[dp] = low_sum(r.vectors[...], r.vectors_pair[...])
        ref = r.vectors_dp.at[dp]
        for k in others_dp:
            late.start(VEC_DP, 0, ref, ref, around[k - 1])

    def vectors_2():
        late.arrived(VEC_DP, 0, r.vectors_dp.at[1:])
        summed = r.vectors_dp[0].astype(F32)
        for k in others_dp:
            summed = summed + r.vectors_dp[k].astype(F32)
        to_line(VEC_LINE, r.vectors_line, summed)

    def vectors_3():
        r.vectors_whole[...] = from_line(VEC_LINE, r.vectors_line)
        vectors_store().start()

    def late_sent():
        late.sent(KV_PAIR, r.kv_grad_pair)
        late.sent(KV_PAIR_BACK, r.kv_grad_pair)
        late.sent(VEC_PAIR, r.vectors_pair)
        late.sent(KV_DP, r.kv_grad_dp.at[1:])
        late.sent(KV_DP_BACK, r.kv_grad_dp.at[1:])
        late.sent(VEC_DP, r.vectors_dp.at[1:])
        late.sent(KV_LINE, r.kv_grad_line.at[1:])
        late.sent(VEC_LINE, r.vectors_line.at[1:])
        kv_store().wait()
        vectors_store().wait()

    stages = {
        "e1": expert_1,
        "e2": expert_2,
        "e3": expert_3,
        "e4": expert_4,
        "e5": expert_5,
        "k1": kv_1,
        "k2": kv_2,
        "k3": kv_3,
        "k4": kv_4,
        "k5": kv_5,
        "v1": vectors_1,
        "v2": vectors_2,
        "v3": vectors_3,
    }
    for i, stage in enumerate(
        [stage_1, stage_2, stage_3, stage_4, stage_5, stage_6, stage_7, stage_8, stage_9, stage_10]
    ):
        stages[i + 1] = stage

    def do(event):
        stages[event[0]](*event[1:])

    def service(plan, turn):
        for at, events in enumerate(plan):
            for event in events:
                pl.when(turn == at)(functools.partial(do, event))

    loaded("up", "cot", "down")
    chunk = r.own.shape[2]

    def feed(c):
        units = pl.ds(pl.multiple_of(c * chunk, chunk), chunk)
        value, slope = gelu_both(dot(r.hidden[...], r.up[:, units], 1, 0))
        value = value.astype(LOW)
        grad = (dot(r.cot[...], r.down[units], 1, 1) * slope).astype(LOW)
        r.own[2 * c] = dot(r.hidden_t[...], grad, 1, 0).astype(LOW)
        down_grad = dot(value, r.cot[...], 0, 0).astype(LOW)
        for i in range(width // chunk):
            at = slice(i * chunk, (i + 1) * chunk)
            r.own[2 * c + 1, at] = down_grad[:, at]
        stage_0(c)
        r.result[...] = r.result[...] + dot(value, r.down[units], 1, 0)
        r.grad_hidden[...] = r.grad_hidden[...] + dot(grad, r.up[:, units], 1, 1)
        service(FEED_PLAN, c)

    loop(CHUNKS, feed)

    r.layer_out[...] = r.result[...].astype(LOW)
    layer_store = pltpu.make_async_copy(r.layer_out, r.layer_hbm, r.out_sem.at[0])
    layer_store.start()
    hat, scale = moments(r.mixed[...])
    grad, gain = norm_back(hat, scale, r.gain_two[...], r.grad_hidden[...])
    grad = grad + r.cot[...].astype(F32)
    r.grad_mixed[...] = grad
    r.grad_mixed_low[...] = grad.astype(LOW)
    r.gain_grad[...] = gain
    for event in MIX_PLAN:
        do(event)

    shown = pick(ids, dot(r.out_all[...], r.grad_mixed_low[...], 1, 1), experts, head)
    expert_shape = r.expert_own.shape[1:]
    r.expert_own[0] = dot(r.gated[...], r.grad_mixed_low[...], 1, 0).astype(LOW).reshape(expert_shape)
    expert_0(0)
    attended = r.total[16:]
    grad_gates = [
        jnp.sum(shown[c] * attended[:, c * positions : (c + 1) * positions], 0, keepdims=True)
        for c in range(2)
    ]
    gates = r.gates[...]
    soft = [r.soft[c : c + 1] for c in range(2)]
    kept_grad = [grad_gates[c] * kept[c : c + 1] for c in range(2)]
    inner = soft[0] * kept_grad[0] + soft[1] * kept_grad[1]
    grad_logits = onehots[0] * (soft[0] * (kept_grad[0] - inner)) + onehots[1] * (
        soft[1] * (kept_grad[1] - inner)
    )
    r.grad_logits[...] = grad_logits
    r.router_grad[...] = dot(grad_logits, r.normed[...].astype(F32), 1, 0, HIGH)
    delta = jnp.concatenate([gates[c : c + 1] * grad_gates[c] for c in range(2)], 1)
    grad_attended = jnp.concatenate([gates[c : c + 1] * shown[c] for c in range(2)], 1)
    stacked = jnp.concatenate([blank, grad_attended], 0)
    r.o_aug[0 : 2 * head] = stacked.astype(LOW)
    r.o_aug[2 * head :] = jnp.concatenate(
        [jnp.zeros((3, count), F32)] + thirds(-delta) + [jnp.zeros((2 * head - 6, count), F32)], 0
    ).astype(LOW)
    r.q_rows[count:] = stacked.T.astype(LOW)
    for event in GATE_PLAN:
        do(event)

    r.grad_q[...] = jnp.zeros(r.grad_q.shape, F32)

    def attend_back(slot):
        block, keys = key_block(slot)
        probs = jnp.exp(dot(keys, r.q_aug[...], 1, 0))
        grads = (probs * dot(keys, r.o_aug[...], 1, 0)).astype(LOW)
        r.grad_q[...] = r.grad_q[...] + dot(block.T[:head], grads, 1, 0)
        return dot(grads, r.q_rows[0:count], 1, 0) + dot(
            probs.astype(LOW), r.q_rows[count:], 1, 0
        )

    back_links = Links(r.back_send, r.back_recv)
    BACK_PAIR, BACK = range(2)

    def back_chip(step):
        k = lax.rem(step + 1, chips)
        r.kv_out[k] = attend_back(2 * k + 1).astype(LOW)
        back_links.start(BACK_PAIR, k, r.kv_out.at[k], r.kv_pair.at[k], sibling)
        service(BLOCK_PLAN, 2 * step)
        mine = attend_back(2 * k)
        back_links.arrived(BACK_PAIR, k, r.kv_pair.at[k])
        both = mine + r.kv_pair[k].astype(F32)

        @pl.when(k > 0)
        def _():
            r.kv_pair[k] = both.astype(LOW)
            back_links.start(BACK, 0, r.kv_pair.at[k], r.kv_in.at[k], behind(k))

        @pl.when(k == 0)
        def _():
            r.kv_own[...] = both

        service(BLOCK_PLAN, 2 * step + 1)

    loop(chips, back_chip)
    for events in BLOCK_PLAN[2 * chips :]:
        for event in events:
            do(event)

    def query_grads():
        grad_queries = r.grad_q[...] * SCALE
        r.grad_spread[...] = spread(
            ids, [grad_queries[:, :positions], grad_queries[:, positions:]], experts
        )
        grads = dot(r.grad_spread[...], r.normed[...], 1, 0).astype(LOW)
        r.expert_own[1] = grads.reshape(expert_shape)
        expert_0(1)

    def kv_grads():
        back_links.arrived(BACK, 0, r.kv_in.at[1:])

        def add_in(k, sum_so_far):
            return sum_so_far + r.kv_in[k].astype(F32)

        grad_kv = lax.fori_loop(1, chips, add_in, r.kv_own[...]).astype(LOW)
        r.kv_grad[...] = dot(r.normed[...], grad_kv, 0, 0).astype(LOW)
        kv_0()
        r.kv_in[0] = grad_kv

    def token_grads():
        grad = (
            dot(r.grad_spread[...], r.query_all[...], 0, 0)
            + dot(r.kv_in[0], r.kv_weight[...], 1, 1)
            + dot(r.grad_logits[...], r.router[...].astype(F32), 0, 0, HIGH)
        )
        hat, scale = moments(r.tokens[...].astype(F32))
        grad, gain = norm_back(hat, scale, r.gain_one[...], grad)
        rest = jnp.zeros((r.vectors.shape[0] - experts - 2, width), F32)
        r.vectors[...] = jnp.concatenate(
            [r.router_grad[...], gain, r.gain_grad[...], rest], 0
        ).astype(LOW)
        vectors_0()
        r.grad_mixed[...] = grad + r.grad_mixed[...]
        tokens_store.start()

    tokens_store = pltpu.make_async_copy(r.grad_mixed, r.grad_tokens_hbm, r.out_sem.at[1])
    stages.update(q=query_grads, k=kv_grads, t=token_grads)
    for event in TAIL_PLAN:
        do(event)

    big_sent()
    expert_sent()
    late_sent()
    layer_store.wait()
    tokens_store.wait()
    kv_links.sent(0, r.kv.at[1:])
    back_links.sent(BACK_PAIR, r.kv_out)
    back_links.sent(BACK, r.kv_in.at[1:])


LOADS = (
    "tokens",
    "gain_one",
    "kv_weight",
    "segments",
    "query_all",
    "ids",
    "keep",
    "router",
    "out_all",
    "gain_two",
    "up",
    "cot",
    "down",
)


def finish(names, fine, *refs):
    r = types.SimpleNamespace(**dict(zip(names, refs, strict=True)))
    blocks, width, chunk = r.big.shape
    experts = r.grad_router.shape[0]
    sources = [r.layer, r.tokens, r.vectors, r.kv]
    held = [r.layer_held, r.tokens_held, r.vectors_held, r.kv_low]
    if fine:
        sources.append(r.experts)
        held.append(r.experts_held)
    loads = [
        pltpu.make_async_copy(r.big.at[b], r.big_low.at[b], r.load_sem.at[b]) for b in range(blocks)
    ]
    small = [
        pltpu.make_async_copy(a, b, r.small_sem.at[i])
        for i, (a, b) in enumerate(zip(sources, held, strict=True))
    ]
    for load in loads + small:
        load.start()
    started = []

    def store(source, target):
        copy = pltpu.make_async_copy(source, target, r.store_sem.at[len(started)])
        copy.start()
        started.append(copy)

    def store_block(source, target):
        pltpu.make_async_copy(source, target, r.block_sem.at[0]).start()

    for b in range(blocks):
        loads[b].wait()
        r.big_full[b] = r.big_low[b].astype(F32)
        c = b // 2
        at = slice(c * chunk, (c + 1) * chunk)
        if b % 2 == 0:
            store_block(r.big_full.at[b], r.grad_up.at[:, at])
        else:
            for i in range(width // chunk):
                part = slice(i * chunk, (i + 1) * chunk)
                store_block(r.big_full.at[b, part], r.grad_down.at[at, part])
    for load in small:
        load.wait()
    r.kv_full[...] = r.kv_low[...].astype(F32)
    store(r.kv_full, r.grad_kv_weight)
    store(r.layer_held, r.layer_out)
    store(r.tokens_held, r.grad_tokens)
    store(r.vectors_held.at[0:experts], r.grad_router)
    store(r.vectors_held.at[experts : experts + 1], r.grad_gain_one)
    store(r.vectors_held.at[experts + 1 : experts + 2], r.grad_gain_two)
    if fine:
        store(r.experts_held.at[0], r.grad_out)
        store(r.experts_held.at[1], r.grad_query)
    for copy in started:
        copy.wait()
    pltpu.make_async_copy(r.big_full, r.big_full, r.block_sem.at[0]).wait()


def shards(
    tokens,
    segments,
    expert_ids,
    keep,
    gain_one,
    kv_weight,
    router_weight,
    query_weight,
    out_weight,
    gain_two,
    up_weight,
    down_weight,
    cotangent,
):
    positions, width = tokens.shape[1:]
    experts, _, head = query_weight.shape
    hidden_units = up_weight.shape[1]
    dps, chips = lax.axis_size("dp"), lax.axis_size("expert") // 2
    chunk = hidden_units // CHUNKS
    blocks = 2 * CHUNKS
    groups = max(1, min(CHUNKS, blocks * (width // 8) // (16 * chips)))
    line_rows = blocks * (width // 8) // groups
    count = 2 * positions
    few = experts // 2
    fine = width // chips % 128 == 0
    part = width // chips if fine else 128
    rows = 2 * experts

    inputs = dict(
        tokens=tokens[0],
        gain_one=gain_one[None],
        kv_weight=kv_weight,
        segments=segments,
        query_all=jnp.swapaxes(query_weight, 1, 2).reshape(experts * head, width),
        ids=expert_ids[0].T,
        keep=keep[0].T,
        router=router_weight.T,
        out_all=jnp.swapaxes(out_weight, 1, 2).reshape(experts * head, width),
        gain_two=gain_two[None],
        up=up_weight,
        cot=cotangent[0],
        down=down_weight,
    )
    inputs = {name: inputs[name] for name in LOADS}
    hbm = pl.BlockSpec(memory_space=pl.ANY)

    def struct(*shape_and_type):
        return jax.ShapeDtypeStruct(shape_and_type[:-1], shape_and_type[-1])

    def vmem(*shape_and_type):
        return pltpu.VMEM(shape_and_type[:-1], shape_and_type[-1])

    def dma(*shape):
        return pltpu.SemaphoreType.DMA(shape)

    expert_out = (few, head // 4, width, LOW)
    if fine:
        expert_out = (experts, head // 4, part // 2, F32)
    outputs = dict(
        layer_hbm=struct(positions, width, LOW),
        grad_tokens_hbm=struct(positions, width, F32),
        kv_hbm=struct(width, 2 * head, LOW),
        vectors_hbm=struct(rows, width, F32),
        experts_hbm=struct(2, *expert_out),
        big_hbm=struct(blocks, width, chunk, LOW),
    )
    scratch = {name: vmem(*value.shape, value.dtype) for name, value in inputs.items()}
    scratch.update(
        normed=vmem(positions, width, LOW),
        kv=vmem(2 * chips, positions + SEG_ROWS, 2 * head, LOW),
        q_aug=vmem(4 * head, count, LOW),
        o_aug=vmem(4 * head, count, LOW),
        q_rows=vmem(2 * count, 2 * head, LOW),
        peak=vmem(1, count, F32),
        total=vmem(16 + head, count, F32),
        gates=vmem(2, positions, F32),
        soft=vmem(2, positions, F32),
        gated=vmem(experts * head, positions, LOW),
        mixed=vmem(positions, width, F32),
        hidden=vmem(positions, width, LOW),
        hidden_t=vmem(width, positions, LOW),
        result=vmem(positions, width, F32),
        layer_out=vmem(positions, width, LOW),
        grad_hidden=vmem(positions, width, F32),
        grad_mixed=vmem(positions, width, F32),
        grad_mixed_low=vmem(positions, width, LOW),
        grad_logits=vmem(experts, positions, F32),
        router_grad=vmem(experts, width, F32),
        gain_grad=vmem(1, width, F32),
        grad_q=vmem(head, count, F32),
        kv_pair=vmem(chips, positions, 2 * head, LOW),
        kv_out=vmem(chips, positions, 2 * head, LOW),
        kv_in=vmem(chips, positions, 2 * head, LOW),
        kv_own=vmem(positions, 2 * head, F32),
        grad_spread=vmem(experts * head, positions, LOW),
        expert_own=vmem(2, experts, 2, 2, head // 4, width, LOW),
        expert_pair=vmem(2, few, 2, 2, head // 4, width, LOW),
        expert_near=vmem(2, few, 2, head // 4, width, LOW),
        expert_far=vmem(2, few, head // 4, width, LOW),
        expert_quarter=vmem(2, few, head // 4, width, LOW),
        expert_line=vmem(2, chips - 1 if fine else 1, few, head // 4, part, LOW),
        expert_last=vmem(2, 2, few, head // 4, part, LOW),
        expert_out=vmem(2, *expert_out),
        kv_grad=vmem(width, 2 * head, LOW),
        kv_grad_pair=vmem(width // 2, 2 * head, LOW),
        kv_grad_dp=vmem(dps, width // 2 // dps, 2 * head, LOW),
        kv_grad_line=vmem(chips, width // 2 // dps, 2 * head, LOW),
        kv_grad_whole=vmem(width, 2 * head, LOW),
        vectors=vmem(rows, width, LOW),
        vectors_pair=vmem(rows, width, LOW),
        vectors_dp=vmem(dps, rows, width, LOW),
        vectors_line=vmem(chips, rows, width, LOW),
        vectors_whole=vmem(rows, width, F32),
        own=vmem(blocks, width, chunk, LOW),
        whole=vmem(blocks, width, chunk, LOW),
        pair_in=vmem(blocks, width // 2, chunk, LOW),
        near_in=vmem(blocks, width // 4, chunk, LOW),
        far_in=vmem(blocks, width // 8, chunk, LOW),
        line_sum=vmem(groups, line_rows, chunk, LOW),
        next_in=vmem(groups, line_rows // 2, chunk, LOW),
        line_in=vmem(groups, max(1, chips // 2 - 1), line_rows // chips, chunk, LOW),
        line_whole=vmem(groups, line_rows, chunk, LOW),
        load_sem=dma(len(LOADS)),
        out_sem=dma(4),
        store_sem=dma(3),
        kv_send=dma(1),
        kv_recv=dma(1, 2 * chips),
        back_send=dma(2),
        back_recv=dma(2, chips),
        halving_send=dma(6),
        halving_recv=dma(6, CHUNKS),
        line_send=dma(4),
        line_recv=dma(4, groups),
        expert_send=dma(5),
        expert_recv=dma(5, 2),
        late_send=dma(8),
        late_recv=dma(8, 1),
    )
    names = [name + "_hbm" for name in LOADS] + list(outputs) + list(scratch)
    reduced = pl.pallas_call(
        functools.partial(kernel, chips, experts, names),
        out_shape=tuple(outputs.values()),
        in_specs=[hbm] * len(LOADS),
        out_specs=(hbm,) * len(outputs),
        scratch_shapes=list(scratch.values()),
        compiler_params=pltpu.CompilerParams(
            collective_id=0, has_side_effects=True, vmem_limit_bytes=62 << 20
        ),
    )(*inputs.values())

    results = dict(
        layer_out=struct(positions, width, LOW),
        grad_tokens=struct(positions, width, F32),
        grad_gain_one=struct(1, width, F32),
        grad_kv_weight=struct(width, 2 * head, F32),
        grad_router=struct(experts, width, F32),
        grad_gain_two=struct(1, width, F32),
        grad_up=struct(width, hidden_units, F32),
        grad_down=struct(hidden_units, width, F32),
    )
    if fine:
        results.update(grad_out=struct(*expert_out), grad_query=struct(*expert_out))
    scratch = dict(
        big_low=vmem(blocks, width, chunk, LOW),
        big_full=vmem(blocks, width, chunk, F32),
        kv_low=vmem(width, 2 * head, LOW),
        kv_full=vmem(width, 2 * head, F32),
        layer_held=vmem(positions, width, LOW),
        tokens_held=vmem(positions, width, F32),
        vectors_held=vmem(rows, width, F32),
        experts_held=vmem(2, *expert_out),
        load_sem=dma(blocks),
        small_sem=dma(5),
        store_sem=dma(len(results)),
        block_sem=dma(1),
    )
    names = ["layer", "tokens", "kv", "vectors", "experts", "big"] + list(results) + list(scratch)
    finished = pl.pallas_call(
        functools.partial(finish, names, fine),
        out_shape=tuple(results.values()),
        in_specs=[hbm] * len(reduced),
        out_specs=(hbm,) * len(results),
        scratch_shapes=list(scratch.values()),
        compiler_params=pltpu.CompilerParams(vmem_limit_bytes=62 << 20),
    )(*reduced)
    r = types.SimpleNamespace(**dict(zip(results, finished, strict=True)))

    def own_part(a):
        if fine:
            return jnp.swapaxes((r.grad_out, r.grad_query)[a], 1, 2)
        whole = jnp.zeros((2, few, head // 4, width), LOW)
        whole = whole.at[lax.axis_index("expert") % 2].set(reduced[4][a])
        whole = whole.reshape(experts, head // 4, width)
        whole = lax.psum_scatter(whole, "expert", scatter_dimension=2, tiled=True)
        return jnp.swapaxes(whole, 1, 2).astype(F32)

    return (
        r.layer_out[None],
        r.grad_tokens[None],
        r.grad_gain_one[0],
        r.grad_kv_weight,
        r.grad_router.T,
        own_part(1),
        own_part(0),
        r.grad_gain_two[0],
        r.grad_up,
        r.grad_down,
    )


def solution(mesh):
    row = P("dp", "expert", None)
    in_specs = (row, P("dp", "expert"), row, row) + (P(),) * 8 + (row,)
    expert = P(None, "expert", "dp")
    out_specs = (row, row, P(), P(), P(), expert, expert, P(), P(), P())
    return jax.shard_map(shards, mesh=mesh, in_specs=in_specs, out_specs=out_specs, check_vma=False)
```

```python
import functools
import types

import jax
import jax.numpy as jnp
from jax import lax
from jax.experimental import pallas as pl
from jax.experimental.pallas import tpu as pltpu
from jax.sharding import PartitionSpec as P

EPS = 1e-05
SCALE = 0.125
NEGATIVE = -1e30
LOW = jnp.bfloat16
F32 = jnp.float32
MESH = pl.DeviceIdType.MESH
LIMIT = 48
SPANS = 4
SEG_ROWS = 16
CHUNKS = 8
FEED_PLAN = (
    (),
    (),
    ((1, 0), ),
    ((1, 1), ),
    ((1, 2), ),
    ((1, 3), (2, 0), ),
    (),
    ((2, 1), (1, 4), ),
)
MIX_PLAN = ()
GATE_PLAN = ((2, 2), (3, 0), )
BLOCK_PLAN = (
    ((1, 7), (3, 1), (2, 3), ),
    ((2, 4), (3, 2), (1, 6), ),
    ((4, 0), ),
    ((3, 3), (4, 1), (2, 7), ),
    ((3, 4), (1, 5), ),
    ((4, 2), (5, 0), ),
    (),
    ((4, 3), (2, 5), (3, 7), (5, 1), ),
    ((6, 0), ),
    (),
    ((4, 4), (3, 5), (5, 2), ),
    ((5, 3), (4, 7), ),
    ((2, 6), (6, 1), ("r",), ),
    ((6, 2), ),
    (),
    ((6, 3), ),
)
TAIL_PLAN = (
    ("q",),
    (3, 6),
    (5, 4),
    (5, 7),
    (7, 0),
    ("u",),
    ("x",),
    (4, 5),
    ("e1", 0),
    ("e1", 1),
    ("k",),
    ("t",),
    ("k1",),
    (4, 6),
    (6, 4),
    (5, 5),
    (7, 1),
    ("e2", 0),
    (7, 3),
    ("e2", 1),
    ("k2",),
    ("v1",),
    (7, 2),
    (5, 6),
    (7, 4),
    (6, 7),
    ("o",),
    ("e3", 0),
    ("e3", 1),
    (6, 5),
    (8, 2),
    (6, 6),
    (7, 7),
    ("v2",),
    ("k3",),
    (7, 5),
    (7, 6),
    (8, 4),
    (8, 1),
    (8, 7),
    (8, 3),
    (8, 5),
    ("e4", 0),
    (8, 0),
    ("e4", 1),
    ("k4",),
    (8, 6),
    ("e5", 0),
    ("e5", 1),
    ("v3",),
    ("k5",),
)

def dot(left, right, left_dim, right_dim):
    return lax.dot_general(
        left, right, (((left_dim,), (right_dim,)), ((), ())), preferred_element_type=F32
    )


def loop(count, body):
    def step(i, carry):
        body(i)
        return carry

    lax.fori_loop(0, count, step, 0)


def moments(values):
    mean = jnp.mean(values, -1, keepdims=True)
    centred = values - mean
    scale = lax.rsqrt(jnp.mean(centred * centred, -1, keepdims=True) + EPS)
    return centred * scale, scale


def norm_back(hat, scale, gain, grad):
    scaled = grad * gain
    inner = jnp.mean(scaled, -1, keepdims=True) + hat * jnp.mean(scaled * hat, -1, keepdims=True)
    return scale * (scaled - inner), jnp.sum(grad * hat, 0, keepdims=True)


def spread(ids, rows, experts):
    pieces = []
    for e in range(experts):
        pieces.append(
            jnp.where(ids[0:1] == e, rows[0], 0.0) + jnp.where(ids[1:2] == e, rows[1], 0.0)
        )
    return jnp.concatenate(pieces, 0).astype(LOW)


def pick(ids, everything, experts, head):
    picked = []
    for c in range(2):
        total = jnp.zeros((head, everything.shape[1]), F32)
        for e in range(experts):
            part = everything[e * head : (e + 1) * head]
            total = total + jnp.where(ids[c : c + 1] == e, part, 0.0)
        picked.append(total)
    return picked


def thirds(values):
    first = values.astype(LOW)
    rest = values - first.astype(F32)
    second = rest.astype(LOW)
    third = (rest - second.astype(F32)).astype(LOW)
    return [first.astype(F32), second.astype(F32), third.astype(F32)]


def gelu_both(x):
    root, cubic = 0.7978845608028654, 0.7978845608028654 * 0.044715
    square = x * x
    h = 0.5 + 0.5 * jnp.tanh(x * (root + cubic * square))
    slope = h * (1.0 + (1.0 - h) * (x * (2.0 * root + 6.0 * cubic * square)))
    return x * h, slope


def low_sum(first, second):
    return (first.astype(F32) + second.astype(F32)).astype(LOW)


def cut(start, size):
    return pl.ds(pl.multiple_of(start, 16), size)


class Links:
    def __init__(self, send, recv):
        self.send, self.recv = send, recv

    def start(self, kind, place, source, target, device_id):
        pltpu.make_async_remote_copy(
            src_ref=source,
            dst_ref=target,
            send_sem=self.send.at[kind],
            recv_sem=self.recv.at[kind, place],
            device_id=device_id,
            device_id_type=MESH,
        ).start()

    def arrived(self, kind, place, ref):
        pltpu.make_async_copy(ref, ref, self.recv.at[kind, place]).wait()

    def sent(self, kind, ref):
        pltpu.make_async_copy(ref, ref, self.send.at[kind]).wait()


def kernel(chips, experts, held, names, *refs):
    r = types.SimpleNamespace(**dict(zip(names, refs, strict=True)))
    positions, width = r.tokens.shape
    head = r.kv_weight.shape[1] // 2
    count = 2 * positions
    dp, device = lax.axis_index("dp"), lax.axis_index("expert")
    chip, core = device // 2, device % 2
    y, x = dp // 2, dp % 2
    place = [x, y]
    sibling = (dp, chip * 2 + 1 - core)
    beside = [(2 * y + 1 - x, device), (2 * (1 - y) + x, device)]
    dp_count = r.kv_grad_dp.shape[0]
    around = [(lax.rem(dp + k, dp_count), device) for k in range(1, dp_count)]

    def store(slot, source, target):
        if held:
            target[...] = source[...].astype(target.dtype)
        else:
            pltpu.make_async_copy(source, target, r.out_sem.at[slot]).start()
            stored.append((slot, source, target))

    stored = []

    def ahead(k):
        return (dp, lax.rem(chip + k, chips) * 2 + core)

    loads = {}
    for i, name in enumerate(LOADS):
        loads[name] = pltpu.make_async_copy(
            getattr(r, name + "_hbm"), getattr(r, name), r.load_sem.at[i]
        )
        loads[name].start()

    def loaded(*wanted):
        for name in wanted:
            loads[name].wait()

    barrier = pltpu.get_barrier_semaphore()
    for peer in [sibling] + around:
        pl.semaphore_signal(barrier, inc=1, device_id=peer, device_id_type=MESH)
    loop(
        chips - 1,
        lambda k: pl.semaphore_signal(
            barrier, inc=1, device_id=ahead(k + 1), device_id_type=MESH
        ),
    )

    loaded("tokens", "gain_one", "kv_weight", "segments")
    normed = (moments(r.tokens[...].astype(F32))[0] * r.gain_one[...]).astype(LOW)
    r.normed[...] = normed
    r.kv[0, :positions] = dot(normed, r.kv_weight[...], 1, 0).astype(LOW)
    segs = r.segments[...].astype(F32)
    lanes = 2 * head
    seg_rows = [segs[:, i * lanes : (i + 1) * lanes] for i in range(positions // lanes)]
    seg_rows.append(jnp.full((SEG_ROWS - len(seg_rows), lanes), 3.0, F32))
    r.kv[0, positions:] = jnp.concatenate(seg_rows, 0).astype(LOW)

    pl.semaphore_wait(barrier, chips + dp_count - 1)

    kv_links = Links(r.kv_send, r.kv_recv)

    def kv_copy(source, target, device_id):
        kv_links.start(0, target, r.kv.at[source], r.kv.at[target], device_id)

    kv_copy(0, 1, sibling)
    loop(chips - 1, lambda k: kv_copy(0, 2 * (k + 1), ahead(k + 1)))

    loaded("query_all", "ids", "keep", "router")
    ids = r.ids[...]
    kept = r.keep[...].astype(F32)
    queries = jnp.concatenate(
        pick(ids, dot(r.query_all[...], r.normed[...], 1, 1), experts, head), 1
    )
    queries = queries.astype(LOW).astype(F32) * SCALE
    seg_twice = jnp.concatenate([segs, segs], 1)
    others = [jnp.where(seg_twice == s, 0.0, NEGATIVE) for s in range(3)]
    blank = jnp.zeros((head, count), F32)
    r.q_aug[0 : 2 * head] = jnp.concatenate([queries, blank], 0).astype(LOW)
    r.q_aug[2 * head :] = jnp.concatenate(
        others + [jnp.zeros((2 * head - 3, count), F32)], 0
    ).astype(LOW)
    r.q_rows[0:count] = jnp.concatenate([queries, blank], 0).T.astype(LOW)
    logits = dot(r.router[...], r.normed[...], 1, 1)
    places = lax.broadcasted_iota(jnp.int32, logits.shape, 0)
    onehots = [(places == ids[c : c + 1]).astype(F32) for c in range(2)]
    chosen = [jnp.sum(onehots[c] * logits, 0, keepdims=True) for c in range(2)]
    top = jnp.maximum(chosen[0], chosen[1])
    expo = [jnp.exp(chosen[c] - top) for c in range(2)]
    r.soft[...] = jnp.concatenate([e / (expo[0] + expo[1]) for e in expo], 0)
    r.gates[...] = r.soft[...] * kept

    r.peak[...] = jnp.full(r.peak.shape, -3e38, F32)
    r.total[...] = jnp.zeros(r.total.shape, F32)

    def key_block(slot):
        block = r.kv[slot, :positions]
        seg = r.kv[slot, positions:].astype(F32)
        first = jnp.sum(jnp.where(seg < 0.5, 1.0, 0.0), keepdims=True)
        second = jnp.sum(jnp.where(seg < 1.5, 1.0, 0.0), keepdims=True)
        row = lax.broadcasted_iota(jnp.int32, (positions, lanes), 0).astype(F32)
        lane = lax.broadcasted_iota(jnp.int32, (positions, lanes), 1)
        segment = jnp.where(row < first, 0, jnp.where(row < second, 1, 2))
        extra = jnp.where((segment == lane) | ((lane >= 3) & (lane < 6)), 1.0, 0.0)
        return block, jnp.concatenate([block, extra.astype(LOW)], 1)

    def attend(slot):
        block, keys = key_block(slot)
        values_t = jnp.concatenate([jnp.ones((16, positions), LOW), block.T[head:]], 0)
        scores = dot(keys, r.q_aug[...], 1, 0)
        old = r.peak[...]
        new = jnp.maximum(old, jnp.max(scores, 0, keepdims=True))
        probs = jnp.exp(scores - new).astype(LOW)
        r.total[...] = r.total[...] * jnp.exp(old - new) + dot(values_t, probs, 1, 0)
        r.peak[...] = new

    def attend_chip(k):
        @pl.when(k > 0)
        def _():
            kv_links.arrived(0, 2 * k, r.kv.at[2 * k])
            kv_copy(2 * k, 2 * k + 1, sibling)

        attend(2 * k)
        kv_links.arrived(0, 2 * k + 1, r.kv.at[2 * k + 1])
        attend(2 * k + 1)

    loop(chips, attend_chip)

    weight = r.total[0:1]
    attended = r.total[16:] / weight
    log_total = r.peak[...] + jnp.log(weight)
    r.total[16:] = attended
    r.q_aug[2 * head :] = jnp.concatenate(
        others + thirds(-log_total) + [jnp.zeros((2 * head - 6, count), F32)], 0
    ).astype(LOW)
    halves = [attended[:, :positions], attended[:, positions:]]
    gates = r.gates[...]
    r.gated[...] = spread(ids, [halves[c] * gates[c : c + 1] for c in range(2)], experts)
    loaded("out_all", "gain_two")
    mixed = r.tokens[...].astype(F32) + dot(r.gated[...], r.out_all[...], 0, 0)
    r.mixed[...] = mixed
    hidden = (moments(mixed)[0] * r.gain_two[...]).astype(LOW)
    r.hidden[...] = hidden
    r.hidden_t[...] = hidden.T

    groups, line_rows = r.line_sum.shape[:2]
    each = CHUNKS // groups
    share = line_rows // chips
    half, quarter, eighth = width // 2, width // 4, width // 8
    halving = Links(r.halving_send, r.halving_recv)
    line = Links(r.line_send, r.line_recv)

    PAIR, NEAR, FAR, FAR_BACK, NEAR_BACK, PAIR_BACK = range(6)
    LINE, LINE_BACK = range(2)

    def both_of(c):
        return pl.ds(2 * c, 2)

    def stage_0(c):
        for w in range(2):
            b = 2 * c + w
            source = r.own.at[b, cut((1 - core) * half, half)]
            halving.start(PAIR, c, source, r.pair_in.at[b], sibling)

    def stage_1(c):
        halving.arrived(PAIR, c, r.pair_in.at[both_of(c)])
        for w in range(2):
            b = 2 * c + w
            at = cut(core * half, half)
            r.own[b, at] = low_sum(r.own[b, at], r.pair_in[b])
            source = r.own.at[b, cut(core * half + (1 - place[w]) * quarter, quarter)]
            halving.start(NEAR, c, source, r.near_in.at[b], beside[w])

    def stage_2(c):
        halving.arrived(NEAR, c, r.near_in.at[both_of(c)])
        for w in range(2):
            b = 2 * c + w
            at = cut(core * half + place[w] * quarter, quarter)
            r.own[b, at] = low_sum(r.own[b, at], r.near_in[b])
            to = core * half + place[w] * quarter + (1 - place[1 - w]) * eighth
            source = r.own.at[b, cut(to, eighth)]
            halving.start(FAR, c, source, r.far_in.at[b], beside[1 - w])

    def stage_3(c):
        g = c // each
        halving.arrived(FAR, c, r.far_in.at[both_of(c)])
        for w in range(2):
            b = 2 * c + w
            at = cut(core * half + place[w] * quarter + place[1 - w] * eighth, eighth)
            to = (c % each * 2 + w) * eighth
            r.line_sum[g, to : to + eighth] = low_sum(r.own[b, at], r.far_in[b])
        if c % each == each - 1:

            def send_share(k):
                source = r.line_sum.at[g, cut(lax.rem(chip + k + 1, chips) * share, share)]
                line.start(LINE, g, source, r.line_in.at[g, k], ahead(k + 1))

            loop(chips - 1, send_share)

    def at_group_end(body):
        def stage(c):
            if c % each == each - 1:
                body(c // each)

        return stage

    my_share = cut(chip * share, share)

    @at_group_end
    def stage_4(g):
        line.arrived(LINE, g, r.line_in.at[g])

        def add_line(k, sum_so_far):
            return sum_so_far + r.line_in[g, k].astype(F32)

        summed = lax.fori_loop(0, chips - 1, add_line, r.line_sum[g, my_share].astype(F32))
        r.line_whole[g, my_share] = summed.astype(LOW)
        ref = r.line_whole.at[g, my_share]
        loop(chips - 1, lambda k: line.start(LINE_BACK, g, ref, ref, ahead(k + 1)))

    def blocks_of(g):
        for i in range(2 * each):
            yield i, i % 2, g * 2 * each + i

    def group_at(g):
        return pl.ds(g * 2 * each, 2 * each)

    @at_group_end
    def stage_5(g):
        line.arrived(LINE_BACK, g, r.line_in.at[g])
        for i, w, b in blocks_of(g):
            at = cut(core * half + place[w] * quarter + place[1 - w] * eighth, eighth)
            r.whole[b, at] = r.line_whole[g, i * eighth : (i + 1) * eighth]
            source = r.line_whole.at[g, i * eighth : (i + 1) * eighth]
            halving.start(FAR_BACK, g, source, r.whole.at[b, at], beside[1 - w])

    @at_group_end
    def stage_6(g):
        halving.arrived(FAR_BACK, g, r.far_in.at[group_at(g)])
        for i, w, b in blocks_of(g):
            ref = r.whole.at[b, cut(core * half + place[w] * quarter, quarter)]
            halving.start(NEAR_BACK, g, ref, ref, beside[w])

    @at_group_end
    def stage_7(g):
        halving.arrived(NEAR_BACK, g, r.near_in.at[group_at(g)])
        for i, w, b in blocks_of(g):
            ref = r.whole.at[b, cut(core * half, half)]
            halving.start(PAIR_BACK, g, ref, ref, sibling)

    @at_group_end
    def stage_8(g):
        halving.arrived(PAIR_BACK, g, r.pair_in.at[group_at(g)])
        for i, w, b in blocks_of(g):
            if held:
                r.big_out[b] = r.whole[b].astype(F32)
            else:
                pltpu.make_async_copy(r.whole.at[b], r.big_out.at[b], r.store_sem.at[0]).start()

    def big_sent():
        for kind in (PAIR, PAIR_BACK):
            halving.sent(kind, r.pair_in)
        for kind in (NEAR, NEAR_BACK):
            halving.sent(kind, r.near_in)
        for kind in (FAR, FAR_BACK):
            halving.sent(kind, r.far_in)
        for kind in (LINE, LINE_BACK):
            line.sent(kind, r.line_in)
        if not held:
            pltpu.make_async_copy(r.whole, r.big_out, r.store_sem.at[0]).wait()

    few = experts // 2
    my_experts = pl.ds(core * few, few)
    fine = width // chips % 128 == 0
    expert_links = Links(r.expert_send, r.expert_recv)
    EXPERT_PAIR, EXPERT_NEAR, EXPERT_FAR, EXPERT_LINE, EXPERT_LAST = range(5)

    def expert_half(a, first, second):
        if a == 0:
            if second is None:
                return (a, my_experts, first)
            return (a, my_experts, first, second)
        if second is None:
            return (a, my_experts, slice(None), first)
        return (a, my_experts, second, first)

    order = [(y, x), (x, y)]
    sides = [(beside[1], beside[0]), (beside[0], beside[1])]

    def expert_columns(c):
        return pl.ds(pl.multiple_of(c * (width // chips), 128), width // chips)

    def expert_0(a):
        source = r.expert_own.at[a, pl.ds((1 - core) * few, few)]
        expert_links.start(EXPERT_PAIR, a, source, r.expert_pair.at[a], sibling)

    def expert_1(a):
        expert_links.arrived(EXPERT_PAIR, a, r.expert_pair.at[a])
        r.expert_own[a, my_experts] = low_sum(r.expert_own[a, my_experts], r.expert_pair[a])
        source = r.expert_own.at[expert_half(a, 1 - order[a][0], None)]
        expert_links.start(EXPERT_NEAR, a, source, r.expert_near.at[a], sides[a][0])

    def expert_2(a):
        expert_links.arrived(EXPERT_NEAR, a, r.expert_near.at[a])
        at = expert_half(a, order[a][0], None)
        r.expert_own[at] = low_sum(r.expert_own[at], r.expert_near[a])
        source = r.expert_own.at[expert_half(a, order[a][0], 1 - order[a][1])]
        expert_links.start(EXPERT_FAR, a, source, r.expert_far.at[a], sides[a][1])

    def expert_3(a):
        expert_links.arrived(EXPERT_FAR, a, r.expert_far.at[a])
        at = expert_half(a, *order[a])
        r.expert_quarter[a] = low_sum(r.expert_own[at], r.expert_far[a])

        def send_columns(k):
            source = r.expert_quarter.at[a, :, :, expert_columns(lax.rem(chip + k + 1, chips))]
            expert_links.start(EXPERT_LINE, a, source, r.expert_line.at[a, k], ahead(k + 1))

        if fine:
            loop(chips - 1, send_columns)

    def expert_4(a):
        if not fine:
            return
        expert_links.arrived(EXPERT_LINE, a, r.expert_line.at[a])

        def add_line(k, sum_so_far):
            return sum_so_far + r.expert_line[a, k].astype(F32)

        own_part = r.expert_quarter[a, :, :, expert_columns(chip)].astype(F32)
        r.expert_last[a, 0] = lax.fori_loop(0, chips - 1, add_line, own_part).astype(LOW)
        source, target = r.expert_last.at[a, 0], r.expert_last.at[a, 1]
        expert_links.start(EXPERT_LAST, a, source, target, sibling)

    def expert_5(a):
        if fine:
            expert_links.arrived(EXPERT_LAST, a, r.expert_last.at[a, 1])
            part = width // chips // 2
            mine = r.expert_last[a, 0].astype(F32)
            other = r.expert_last[a, 1].astype(F32)
            for i in range(2):
                rows = jnp.where(core == i, mine, other)
                r.expert_out[a, i * few : (i + 1) * few] = jnp.where(
                    core == 0, rows[:, :, :part], rows[:, :, part:]
                )
        else:
            r.expert_out[a] = r.expert_quarter[a]
        store(a, r.expert_out.at[a], r.experts_out.at[a])

    def expert_sent():
        expert_links.sent(EXPERT_PAIR, r.expert_pair)
        expert_links.sent(EXPERT_NEAR, r.expert_near)
        expert_links.sent(EXPERT_FAR, r.expert_far)
        if fine:
            expert_links.sent(EXPERT_LINE, r.expert_line)
            expert_links.sent(EXPERT_LAST, r.expert_last.at[:, 0])

    late = Links(r.late_send, r.late_recv)
    KV_PAIR, KV_DP, KV_LINE, KV_DP_BACK, KV_PAIR_BACK, VEC_PAIR, VEC_DP, VEC_LINE = range(8)
    kv_half = width // 2
    kv_part = kv_half // dp_count
    others_dp = range(1, dp_count)
    kv_mine = cut(core * kv_half, kv_half)
    kv_share = cut(core * kv_half + dp * kv_part, kv_part)

    def kv_0():
        source = r.kv_grad.at[cut((1 - core) * kv_half, kv_half)]
        late.start(KV_PAIR, 0, source, r.kv_grad_pair, sibling)

    def kv_1():
        late.arrived(KV_PAIR, 0, r.kv_grad_pair)
        r.kv_grad[kv_mine] = low_sum(r.kv_grad[kv_mine], r.kv_grad_pair[...])
        for k in others_dp:
            at = cut(core * kv_half + lax.rem(dp + k, dp_count) * kv_part, kv_part)
            late.start(KV_DP, 0, r.kv_grad.at[at], r.kv_grad_dp.at[k], around[k - 1])

    def to_line(kind, buffer, value):
        buffer[chip] = value.astype(LOW)
        ref = buffer.at[chip]
        loop(chips - 1, lambda k: late.start(kind, 0, ref, ref, ahead(k + 1)))

    def from_line(kind, buffer):
        late.arrived(kind, 0, buffer.at[1:])

        def add(k, sum_so_far):
            return sum_so_far + buffer[k].astype(F32)

        return lax.fori_loop(1, chips, add, buffer[0].astype(F32))

    def kv_2():
        late.arrived(KV_DP, 0, r.kv_grad_dp.at[1:])
        summed = r.kv_grad[kv_share].astype(F32)
        for k in others_dp:
            summed = summed + r.kv_grad_dp[k].astype(F32)
        to_line(KV_LINE, r.kv_grad_line, summed)

    def kv_3():
        r.kv_grad_whole[kv_share] = from_line(KV_LINE, r.kv_grad_line).astype(LOW)
        ref = r.kv_grad_whole.at[kv_share]
        for k in others_dp:
            late.start(KV_DP_BACK, 0, ref, ref, around[k - 1])

    def kv_4():
        late.arrived(KV_DP_BACK, 0, r.kv_grad_dp.at[1:])
        ref = r.kv_grad_whole.at[kv_mine]
        late.start(KV_PAIR_BACK, 0, ref, ref, sibling)

    def kv_5():
        late.arrived(KV_PAIR_BACK, 0, r.kv_grad_pair)
        store(2, r.kv_grad_whole, r.kv_out_whole)

    def vectors_0():
        late.start(VEC_PAIR, 0, r.vectors, r.vectors_pair, sibling)

    def vectors_1():
        late.arrived(VEC_PAIR, 0, r.vectors_pair)
        r.vectors_dp[dp] = low_sum(r.vectors[...], r.vectors_pair[...])
        ref = r.vectors_dp.at[dp]
        for k in others_dp:
            late.start(VEC_DP, 0, ref, ref, around[k - 1])

    def vectors_2():
        late.arrived(VEC_DP, 0, r.vectors_dp.at[1:])
        summed = r.vectors_dp[0].astype(F32)
        for k in others_dp:
            summed = summed + r.vectors_dp[k].astype(F32)
        to_line(VEC_LINE, r.vectors_line, summed)

    def vectors_3():
        r.vectors_whole[...] = from_line(VEC_LINE, r.vectors_line)
        store(3, r.vectors_whole, r.vectors_out)

    def late_sent():
        late.sent(KV_PAIR, r.kv_grad_pair)
        late.sent(KV_PAIR_BACK, r.kv_grad_pair)
        late.sent(VEC_PAIR, r.vectors_pair)
        late.sent(KV_DP, r.kv_grad_dp.at[1:])
        late.sent(KV_DP_BACK, r.kv_grad_dp.at[1:])
        late.sent(VEC_DP, r.vectors_dp.at[1:])
        late.sent(KV_LINE, r.kv_grad_line.at[1:])
        late.sent(VEC_LINE, r.vectors_line.at[1:])

    stages = {
        "e1": expert_1,
        "e2": expert_2,
        "e3": expert_3,
        "e4": expert_4,
        "e5": expert_5,
        "k1": kv_1,
        "k2": kv_2,
        "k3": kv_3,
        "k4": kv_4,
        "k5": kv_5,
        "v1": vectors_1,
        "v2": vectors_2,
        "v3": vectors_3,
    }
    for i, stage in enumerate(
        [stage_1, stage_2, stage_3, stage_4, stage_5, stage_6, stage_7, stage_8]
    ):
        stages[i + 1] = stage

    def do(event):
        stages[event[0]](*event[1:])

    def service(plan, turn):
        for at, events in enumerate(plan):
            for event in events:
                pl.when(turn == at)(functools.partial(do, event))

    loaded("up", "cot", "down")
    chunk = r.own.shape[2]

    def layer_output():
        out = r.mixed[...] + dot(r.act[...], r.down[...], 1, 0)
        r.layer_low[...] = out.astype(LOW)
        store(4, r.layer_low, r.layer_out)

    stages["o"] = layer_output

    def feed(c):
        units = pl.ds(pl.multiple_of(c * chunk, chunk), chunk)
        value, slope = gelu_both(dot(r.hidden[...], r.up[:, units], 1, 0))
        value = value.astype(LOW)
        grad = (dot(r.cot[...], r.down[units], 1, 1) * slope).astype(LOW)
        r.act[:, units] = value
        r.grad_pre[:, units] = grad
        r.own[2 * c] = dot(r.hidden_t[...], grad, 1, 0).astype(LOW)
        down_grad = dot(value, r.cot[...], 0, 0).astype(LOW)
        for i in range(width // chunk):
            at = slice(i * chunk, (i + 1) * chunk)
            r.own[2 * c + 1, at] = down_grad[:, at]
        stage_0(c)
        service(FEED_PLAN, c)

    loop(CHUNKS, feed)

    hat, scale = moments(r.mixed[...])
    grad = dot(r.grad_pre[...], r.up[...], 1, 1)
    grad, gain = norm_back(hat, scale, r.gain_two[...], grad)
    grad = grad + r.cot[...].astype(F32)
    r.grad_mixed[...] = grad
    r.grad_mixed_low[...] = grad.astype(LOW)
    r.gain_grad[...] = gain
    for event in MIX_PLAN:
        do(event)

    shown = pick(ids, dot(r.out_all[...], r.grad_mixed_low[...], 1, 1), experts, head)
    expert_shape = r.expert_own.shape[1:]
    r.expert_own[0] = dot(r.gated[...], r.grad_mixed_low[...], 1, 0).astype(LOW).reshape(expert_shape)
    expert_0(0)
    attended = r.total[16:]
    grad_gates = [
        jnp.sum(shown[c] * attended[:, c * positions : (c + 1) * positions], 0, keepdims=True)
        for c in range(2)
    ]
    gates = r.gates[...]
    soft = [r.soft[c : c + 1] for c in range(2)]
    kept_grad = [grad_gates[c] * kept[c : c + 1] for c in range(2)]
    inner = soft[0] * kept_grad[0] + soft[1] * kept_grad[1]
    grad_logits = onehots[0] * (soft[0] * (kept_grad[0] - inner)) + onehots[1] * (
        soft[1] * (kept_grad[1] - inner)
    )
    r.grad_logits[...] = jnp.concatenate(thirds(grad_logits), 0).astype(LOW)
    in_thirds = dot(r.grad_logits[...], r.normed[...], 1, 0)
    r.router_grad[...] = (
        in_thirds[:experts] + in_thirds[experts : 2 * experts] + in_thirds[2 * experts :]
    )
    delta = jnp.concatenate([gates[c : c + 1] * grad_gates[c] for c in range(2)], 1)
    grad_attended = jnp.concatenate([gates[c : c + 1] * shown[c] for c in range(2)], 1)
    stacked = jnp.concatenate([blank, grad_attended], 0)
    r.o_aug[0 : 2 * head] = stacked.astype(LOW)
    r.o_aug[2 * head :] = jnp.concatenate(
        [jnp.zeros((3, count), F32)] + thirds(-delta) + [jnp.zeros((2 * head - 6, count), F32)], 0
    ).astype(LOW)
    r.q_rows[count:] = stacked.T.astype(LOW)
    for event in GATE_PLAN:
        do(event)

    r.grad_q[...] = jnp.zeros(r.grad_q.shape, F32)
    back_links = Links(r.back_send, r.back_recv)
    BACK_PAIR, BACK_NEXT, BACK_LINE = range(3)
    span = count // SPANS
    side, turn_of, same_side = chip % 2, chip // 2, chips // 2
    next_chip = (dp, (chip + 1 - 2 * side) * 2 + core)

    def target_chip(step):
        back = lax.rem(step + 1, same_side)
        at = 2 * lax.rem(turn_of + same_side - back, same_side)
        at = at + jnp.where(step < same_side, 1 - side, side)
        return back, lax.rem(chip + chips - at, chips)

    def back_keys(k):
        for i in range(2):
            at = slice(i * positions, (i + 1) * positions)
            block, keys = key_block(2 * k + i)
            r.keys[at] = keys
            r.keys_t[:, at] = block.T[:head]

    def back_pair(step):
        back, _ = target_chip(step)
        back_links.arrived(BACK_PAIR, step, r.kv_pair.at[step])
        both = r.part[lax.rem(step, 2), :positions] + r.kv_pair[step].astype(F32)
        r.kv_pair[step] = both.astype(LOW)

        @pl.when(step < same_side)
        def _():
            back_links.start(BACK_NEXT, back, r.kv_pair.at[step], r.kv_next.at[back], next_chip)

        @pl.when(step == chips - 1)
        def _():
            r.kv_own[...] = both

    def back_line():
        def send(s):
            back, step = s + 1, same_side + s
            back_links.arrived(BACK_NEXT, back, r.kv_next.at[back])
            r.kv_pair[step] = low_sum(r.kv_pair[step], r.kv_next[back])
            target = (dp, lax.rem(chip + chips - 2 * back, chips) * 2 + core)
            back_links.start(BACK_LINE, 0, r.kv_pair.at[step], r.kv_line.at[s], target)

        loop(same_side - 1, send)

    stages["x"] = lambda: back_pair(chips - 1)
    stages["r"] = back_line

    def back_turn(turn):
        step, at_span = turn // SPANS, lax.rem(turn, SPANS)
        (_, k), now = target_chip(step), lax.rem(step, 2)

        @pl.when(at_span == 0)
        def _():
            back_keys(k)
            r.part[now] = jnp.zeros(r.part.shape[1:], F32)

        at = pl.ds(pl.multiple_of(at_span * span, span), span)
        also = pl.ds(pl.multiple_of(count + at_span * span, span), span)
        keys = r.keys[...]
        probs = jnp.exp(dot(keys, r.q_aug[:, at], 1, 0))
        grads = (probs * dot(keys, r.o_aug[:, at], 1, 0)).astype(LOW)
        r.grad_q[:, at] = r.grad_q[:, at] + dot(r.keys_t[...], grads, 1, 0)
        r.part[now] = (
            r.part[now] + dot(grads, r.q_rows[at], 1, 0) + dot(probs.astype(LOW), r.q_rows[also], 1, 0)
        )

        @pl.when(at_span == SPANS - 1)
        def _():
            r.kv_out[step] = r.part[now, positions:].astype(LOW)
            back_links.start(BACK_PAIR, step, r.kv_out.at[step], r.kv_pair.at[step], sibling)

        @pl.when((at_span == 0) & (step > 0))
        def _():
            back_pair(step - 1)

        service(block_plan, turn)

    block_plan, line_first = BLOCK_PLAN, False
    if chips != 4:
        line_first = any(("r",) in events for events in BLOCK_PLAN)
        block_plan = [[event for event in events if event != ("r",)] for events in BLOCK_PLAN]
    loop(SPANS * chips, back_turn)
    for events in block_plan[SPANS * chips :]:
        for event in events:
            do(event)

    def query_grads():
        grad_queries = r.grad_q[...] * SCALE
        r.grad_spread[...] = spread(
            ids, [grad_queries[:, :positions], grad_queries[:, positions:]], experts
        )
        grads = dot(r.grad_spread[...], r.normed[...], 1, 0).astype(LOW)
        r.expert_own[1] = grads.reshape(expert_shape)
        expert_0(1)

    def token_sum():
        routers = jnp.concatenate([r.router[...].astype(F32)] * 3, 0).astype(LOW)
        r.grad_normed[...] = dot(r.grad_spread[...], r.query_all[...], 0, 0) + dot(
            r.grad_logits[...], routers, 0, 0
        )

    def kv_grads():
        back_links.arrived(BACK_NEXT, 0, r.kv_next.at[0])
        if same_side > 1:
            back_links.arrived(BACK_LINE, 0, r.kv_line)

        def add_in(k, sum_so_far):
            return sum_so_far + r.kv_line[k].astype(F32)

        summed = r.kv_own[...] + r.kv_next[0].astype(F32)
        grad_kv = lax.fori_loop(0, same_side - 1, add_in, summed).astype(LOW)
        r.kv_grad_own[...] = grad_kv
        r.kv_grad[...] = dot(r.normed[...], grad_kv, 0, 0).astype(LOW)
        kv_0()

    def token_grads():
        grad = r.grad_normed[...] + dot(r.kv_grad_own[...], r.kv_weight[...], 1, 1)
        hat, scale = moments(r.tokens[...].astype(F32))
        grad, gain = norm_back(hat, scale, r.gain_one[...], grad)
        rest = jnp.zeros((r.vectors.shape[0] - experts - 2, width), F32)
        r.vectors[...] = jnp.concatenate(
            [r.router_grad[...], gain, r.gain_grad[...], rest], 0
        ).astype(LOW)
        vectors_0()
        r.grad_mixed[...] = grad + r.grad_mixed[...]
        store(5, r.grad_mixed, r.tokens_out)

    stages.update(q=query_grads, u=token_sum, k=kv_grads, t=token_grads)
    for event in TAIL_PLAN:
        do(event)
        if event == ("x",) and line_first:
            back_line()

    big_sent()
    expert_sent()
    late_sent()
    for slot, source, target in stored:
        pltpu.make_async_copy(source, target, r.out_sem.at[slot]).wait()
    kv_links.sent(0, r.kv.at[1:])
    back_links.sent(BACK_PAIR, r.kv_out)
    back_links.sent(BACK_NEXT, r.kv_next)
    if same_side > 1:
        back_links.sent(BACK_LINE, r.kv_line)


LOADS = (
    "tokens",
    "gain_one",
    "kv_weight",
    "segments",
    "query_all",
    "ids",
    "keep",
    "router",
    "out_all",
    "gain_two",
    "up",
    "cot",
    "down",
)


def finish(names, held, *refs):
    r = types.SimpleNamespace(**dict(zip(names, refs, strict=True)))
    blocks, width, chunk = r.big_out.shape
    experts = r.grad_router.shape[0]
    sources = [r.layer_out, r.tokens_out, r.vectors_out, r.kv_out_whole]
    started = []

    def store(source, target):
        copy = pltpu.make_async_copy(source, target, r.store_sem.at[len(started)])
        copy.start()
        started.append(copy)

    def store_block(b, source):
        c = b // 2
        at = slice(c * chunk, (c + 1) * chunk)
        if b % 2 == 0:
            pltpu.make_async_copy(source, r.grad_up.at[:, at], r.block_sem.at[0]).start()
            return
        for i in range(width // chunk):
            part = slice(i * chunk, (i + 1) * chunk)
            target = r.grad_down.at[at, part]
            pltpu.make_async_copy(source.at[part], target, r.block_sem.at[0]).start()

    if held:
        for b in range(blocks):
            store_block(b, r.big_out.at[b])
        layer, tokens, vectors, kv = sources
        full = r.big_out
    else:
        loads = [
            pltpu.make_async_copy(r.big_out.at[b], r.big_low.at[b], r.load_sem.at[b])
            for b in range(blocks)
        ]
        arrays = [r.layer_held, r.tokens_held, r.vectors_held, r.kv_held]
        small = [
            pltpu.make_async_copy(a, b, r.small_sem.at[i])
            for i, (a, b) in enumerate(zip(sources, arrays, strict=True))
        ]
        for load in loads + small:
            load.start()
        for b in range(blocks):
            loads[b].wait()
            r.big_full[b] = r.big_low[b].astype(F32)
            store_block(b, r.big_full.at[b])
        for load in small:
            load.wait()
        r.kv_full[...] = r.kv_held[...].astype(F32)
        layer, tokens, vectors, kv = arrays[:3] + [r.kv_full]
        full = r.big_full
    store(layer, r.layer)
    store(tokens, r.grad_tokens)
    store(kv, r.grad_kv_weight)
    store(vectors.at[0:experts], r.grad_router)
    store(vectors.at[experts : experts + 1], r.grad_gain_one)
    store(vectors.at[experts + 1 : experts + 2], r.grad_gain_two)
    if held:
        store(r.experts_out.at[0], r.grad_out)
        store(r.experts_out.at[1], r.grad_query)
    for copy in started:
        copy.wait()
    pltpu.make_async_copy(full, full, r.block_sem.at[0]).wait()


def shards(
    tokens,
    segments,
    expert_ids,
    keep,
    gain_one,
    kv_weight,
    router_weight,
    query_weight,
    out_weight,
    gain_two,
    up_weight,
    down_weight,
    cotangent,
):
    positions, width = tokens.shape[1:]
    experts, _, head = query_weight.shape
    hidden_units = up_weight.shape[1]
    dps, chips = lax.axis_size("dp"), lax.axis_size("expert") // 2
    chunk = hidden_units // CHUNKS
    blocks = 2 * CHUNKS
    groups = max(1, min(CHUNKS, blocks * (width // 8) // (16 * chips)))
    line_rows = blocks * (width // 8) // groups
    count = 2 * positions
    few = experts // 2
    fine = width // chips % 128 == 0
    part = width // chips if fine else 128
    rows = 2 * experts

    inputs = dict(
        tokens=tokens[0],
        gain_one=gain_one[None],
        kv_weight=kv_weight,
        segments=segments,
        query_all=jnp.swapaxes(query_weight, 1, 2).reshape(experts * head, width),
        ids=expert_ids[0].T,
        keep=keep[0].T,
        router=router_weight.T,
        out_all=jnp.swapaxes(out_weight, 1, 2).reshape(experts * head, width),
        gain_two=gain_two[None],
        up=up_weight,
        cot=cotangent[0],
        down=down_weight,
    )
    inputs = {name: inputs[name] for name in LOADS}
    hbm = pl.BlockSpec(memory_space=pl.ANY)

    def struct(*shape_and_type):
        return jax.ShapeDtypeStruct(shape_and_type[:-1], shape_and_type[-1])

    def vmem(*shape_and_type):
        return pltpu.VMEM(shape_and_type[:-1], shape_and_type[-1])

    def dma(*shape):
        return pltpu.SemaphoreType.DMA(shape)

    expert_out = (few, head // 4, width, LOW)
    if fine:
        expert_out = (experts, head // 4, part // 2, F32)
    held = fine
    outputs = dict(
        layer_out=(positions, width, LOW),
        tokens_out=(positions, width, F32),
        kv_out_whole=(width, 2 * head, F32 if held else LOW),
        vectors_out=(rows, width, F32),
        experts_out=(2, *expert_out),
        big_out=(blocks, width, chunk, F32 if held else LOW),
    )
    between = vmem if held else struct
    outputs = {name: between(*value) for name, value in outputs.items()}
    vmem_spec = pl.BlockSpec(memory_space=pltpu.VMEM)
    passed = vmem_spec if held else hbm
    scratch = {name: vmem(*value.shape, value.dtype) for name, value in inputs.items()}
    scratch.update(
        normed=vmem(positions, width, LOW),
        kv=vmem(2 * chips, positions + SEG_ROWS, 2 * head, LOW),
        q_aug=vmem(4 * head, count, LOW),
        o_aug=vmem(4 * head, count, LOW),
        q_rows=vmem(2 * count, 2 * head, LOW),
        peak=vmem(1, count, F32),
        total=vmem(16 + head, count, F32),
        gates=vmem(2, positions, F32),
        soft=vmem(2, positions, F32),
        gated=vmem(experts * head, positions, LOW),
        mixed=vmem(positions, width, F32),
        hidden=vmem(positions, width, LOW),
        hidden_t=vmem(width, positions, LOW),
        act=vmem(positions, hidden_units, LOW),
        grad_pre=vmem(positions, hidden_units, LOW),
        layer_low=vmem(positions, width, LOW),
        grad_normed=vmem(positions, width, F32),
        grad_mixed=vmem(positions, width, F32),
        grad_mixed_low=vmem(positions, width, LOW),
        grad_logits=vmem(3 * experts, positions, LOW),
        router_grad=vmem(experts, width, F32),
        gain_grad=vmem(1, width, F32),
        grad_q=vmem(head, count, F32),
        kv_pair=vmem(chips, positions, 2 * head, LOW),
        kv_out=vmem(chips, positions, 2 * head, LOW),
        kv_next=vmem(max(1, chips // 2), positions, 2 * head, LOW),
        kv_line=vmem(max(1, chips // 2 - 1), positions, 2 * head, LOW),
        part=vmem(2, 2 * positions, 2 * head, F32),
        keys=vmem(2 * positions, 4 * head, LOW),
        keys_t=vmem(head, 2 * positions, LOW),
        kv_grad_own=vmem(positions, 2 * head, LOW),
        kv_own=vmem(positions, 2 * head, F32),
        grad_spread=vmem(experts * head, positions, LOW),
        expert_own=vmem(2, experts, 2, 2, head // 4, width, LOW),
        expert_pair=vmem(2, few, 2, 2, head // 4, width, LOW),
        expert_near=vmem(2, few, 2, head // 4, width, LOW),
        expert_far=vmem(2, few, head // 4, width, LOW),
        expert_quarter=vmem(2, few, head // 4, width, LOW),
        expert_line=vmem(2, chips - 1 if fine else 1, few, head // 4, part, LOW),
        expert_last=vmem(2, 2, few, head // 4, part, LOW),
        expert_out=vmem(2, *expert_out),
        kv_grad=vmem(width, 2 * head, LOW),
        kv_grad_pair=vmem(width // 2, 2 * head, LOW),
        kv_grad_dp=vmem(dps, width // 2 // dps, 2 * head, LOW),
        kv_grad_line=vmem(chips, width // 2 // dps, 2 * head, LOW),
        kv_grad_whole=vmem(width, 2 * head, LOW),
        vectors=vmem(rows, width, LOW),
        vectors_pair=vmem(rows, width, LOW),
        vectors_dp=vmem(dps, rows, width, LOW),
        vectors_line=vmem(chips, rows, width, LOW),
        vectors_whole=vmem(rows, width, F32),
        own=vmem(blocks, width, chunk, LOW),
        whole=vmem(blocks, width, chunk, LOW),
        pair_in=vmem(blocks, width // 2, chunk, LOW),
        near_in=vmem(blocks, width // 4, chunk, LOW),
        far_in=vmem(blocks, width // 8, chunk, LOW),
        line_sum=vmem(groups, line_rows, chunk, LOW),
        line_in=vmem(groups, chips - 1, line_rows // chips, chunk, LOW),
        line_whole=vmem(groups, line_rows, chunk, LOW),
        load_sem=dma(len(LOADS)),
        out_sem=dma(6),
        store_sem=dma(1),
        kv_send=dma(1),
        kv_recv=dma(1, 2 * chips),
        back_send=dma(3),
        back_recv=dma(3, chips),
        halving_send=dma(6),
        halving_recv=dma(6, CHUNKS),
        line_send=dma(2),
        line_recv=dma(2, groups),
        expert_send=dma(5),
        expert_recv=dma(5, 2),
        late_send=dma(8),
        late_recv=dma(8, 1),
    )
    names = [name + "_hbm" for name in LOADS] + list(outputs) + list(scratch)
    reduced = pl.pallas_call(
        functools.partial(kernel, chips, experts, held, names),
        out_shape=tuple(outputs.values()),
        in_specs=[hbm] * len(LOADS),
        out_specs=(passed,) * len(outputs),
        scratch_shapes=list(scratch.values()),
        compiler_params=pltpu.CompilerParams(
            collective_id=0, has_side_effects=True, vmem_limit_bytes=(LIMIT if held else 62) << 20
        ),
    )(*inputs.values())

    results = dict(
        layer=struct(positions, width, LOW),
        grad_tokens=struct(positions, width, F32),
        grad_gain_one=struct(1, width, F32),
        grad_kv_weight=struct(width, 2 * head, F32),
        grad_router=struct(experts, width, F32),
        grad_gain_two=struct(1, width, F32),
        grad_up=struct(width, hidden_units, F32),
        grad_down=struct(hidden_units, width, F32),
    )
    if fine:
        results.update(grad_out=struct(*expert_out), grad_query=struct(*expert_out))
    scratch = dict(store_sem=dma(len(results)), block_sem=dma(1))
    if not held:
        scratch.update(
            big_low=vmem(blocks, width, chunk, LOW),
            big_full=vmem(blocks, width, chunk, F32),
            kv_held=vmem(width, 2 * head, LOW),
            kv_full=vmem(width, 2 * head, F32),
            layer_held=vmem(positions, width, LOW),
            tokens_held=vmem(positions, width, F32),
            vectors_held=vmem(rows, width, F32),
            load_sem=dma(blocks),
            small_sem=dma(4),
        )
    names = list(outputs) + list(results) + list(scratch)
    finished = pl.pallas_call(
        functools.partial(finish, names, held),
        out_shape=tuple(results.values()),
        in_specs=[passed] * len(reduced),
        out_specs=(hbm,) * len(results),
        scratch_shapes=list(scratch.values()),
        compiler_params=pltpu.CompilerParams(vmem_limit_bytes=(4 if held else 62) << 20),
    )(*reduced)
    r = types.SimpleNamespace(**dict(zip(results, finished, strict=True)))

    def own_part(a):
        if fine:
            return jnp.swapaxes((r.grad_out, r.grad_query)[a], 1, 2)
        whole = jnp.zeros((2, few, head // 4, width), LOW)
        whole = whole.at[lax.axis_index("expert") % 2].set(reduced[4][a])
        whole = whole.reshape(experts, head // 4, width)
        whole = lax.psum_scatter(whole, "expert", scatter_dimension=2, tiled=True)
        return jnp.swapaxes(whole, 1, 2).astype(F32)

    return (
        r.layer[None],
        r.grad_tokens[None],
        r.grad_gain_one[0],
        r.grad_kv_weight,
        r.grad_router.T,
        own_part(1),
        own_part(0),
        r.grad_gain_two[0],
        r.grad_up,
        r.grad_down,
    )


def solution(mesh):
    row = P("dp", "expert", None)
    in_specs = (row, P("dp", "expert"), row, row) + (P(),) * 8 + (row,)
    expert = P(None, "expert", "dp")
    out_specs = (row, row, P(), P(), P(), expert, expert, P(), P(), P())
    return jax.shard_map(shards, mesh=mesh, in_specs=in_specs, out_specs=out_specs, check_vma=False)
```

```python
import functools
import types

import jax
import jax.numpy as jnp
from jax import lax
from jax.experimental import pallas as pl
from jax.experimental.pallas import tpu as pltpu
from jax.sharding import PartitionSpec as P

EPS = 1e-05
SCALE = 0.125
NEGATIVE = -1e30
LOW = jnp.bfloat16
F32 = jnp.float32
MESH = pl.DeviceIdType.MESH
LIMIT = 48
SPANS = 4
SEG_ROWS = 16
CHUNKS = 8
FEED_PLAN = (
    (),
    (),
    ((1, 0), ),
    ((1, 1), ),
    ((1, 2), ),
    (),
    ((2, 0), (1, 3), ),
    (),
)
MIX_PLAN = ((2, 2), )
GATE_PLAN = ((2, 1), (1, 5), (3, 0), )
BLOCK_PLAN = (
    (),
    ((2, 3), (3, 2), (1, 4), ),
    (),
    ((1, 7), (3, 1), ),
    ((3, 3), ),
    ((4, 0), (4, 2), (2, 4), (2, 5), ),
    (("e1", 0), ),
    (),
    ((1, 6), (4, 1), (4, 3), ),
    (),
    (),
    ((3, 5), ),
    ((3, 4), (5, 2), (2, 7), ),
    (("r",), (5, 0), (2, 6), ),
    ((5, 1), (5, 3), (6, 2), ),
    (),
    ((6, 0), ),
)
TAIL_PLAN = (
    ("q",),
    (3, 6),
    (6, 3),
    ("u",),
    (4, 4),
    ("e1", 1),
    (3, 7),
    ("x",),
    ("k",),
    ("t",),
    (4, 5),
    ("k1",),
    ("v1",),
    (4, 6),
    (6, 1),
    (5, 4),
    (4, 7),
    (7, 0),
    ("e2", 1),
    ("e2", 0),
    (7, 3),
    (5, 5),
    ("k2",),
    (5, 6),
    (7, 2),
    ("v2",),
    (6, 4),
    (5, 7),
    (6, 5),
    ("e3", 0),
    ("e3", 1),
    ("o",),
    ("k3",),
    (6, 6),
    (6, 7),
    (7, 1),
    (7, 5),
    ("v3",),
    (7, 4),
    ("e4", 0),
    ("e4", 1),
    ("k4",),
    (7, 6),
    ("e5", 1),
    (8, 2),
    (8, 3),
    (7, 7),
    (8, 4),
    (8, 6),
    (8, 5),
    ("e5", 0),
    (8, 0),
    (8, 1),
    ("k5",),
    (8, 7),
)

def dot(left, right, left_dim, right_dim):
    return lax.dot_general(
        left, right, (((left_dim,), (right_dim,)), ((), ())), preferred_element_type=F32
    )


def loop(count, body):
    def step(i, carry):
        body(i)
        return carry

    lax.fori_loop(0, count, step, 0)


def moments(values):
    mean = jnp.mean(values, -1, keepdims=True)
    centred = values - mean
    scale = lax.rsqrt(jnp.mean(centred * centred, -1, keepdims=True) + EPS)
    return centred * scale, scale


def norm_back(hat, scale, gain, grad):
    scaled = grad * gain
    inner = jnp.mean(scaled, -1, keepdims=True) + hat * jnp.mean(scaled * hat, -1, keepdims=True)
    return scale * (scaled - inner), jnp.sum(grad * hat, 0, keepdims=True)


def spread(ids, rows, experts):
    pieces = []
    for e in range(experts):
        pieces.append(
            jnp.where(ids[0:1] == e, rows[0], 0.0) + jnp.where(ids[1:2] == e, rows[1], 0.0)
        )
    return jnp.concatenate(pieces, 0).astype(LOW)


def pick(ids, everything, experts, head):
    picked = []
    for c in range(2):
        total = jnp.zeros((head, everything.shape[1]), F32)
        for e in range(experts):
            part = everything[e * head : (e + 1) * head]
            total = total + jnp.where(ids[c : c + 1] == e, part, 0.0)
        picked.append(total)
    return picked


def thirds(values):
    first = values.astype(LOW)
    rest = values - first.astype(F32)
    second = rest.astype(LOW)
    third = (rest - second.astype(F32)).astype(LOW)
    return [first.astype(F32), second.astype(F32), third.astype(F32)]


def gelu_both(x):
    root, cubic = 0.7978845608028654, 0.7978845608028654 * 0.044715
    square = x * x
    h = 0.5 + 0.5 * jnp.tanh(x * (root + cubic * square))
    slope = h * (1.0 + (1.0 - h) * (x * (2.0 * root + 6.0 * cubic * square)))
    return x * h, slope


def low_sum(first, second):
    return (first.astype(F32) + second.astype(F32)).astype(LOW)


def cut(start, size):
    return pl.ds(pl.multiple_of(start, 16), size)


class Links:
    def __init__(self, send, recv):
        self.send, self.recv = send, recv

    def start(self, kind, place, source, target, device_id):
        pltpu.make_async_remote_copy(
            src_ref=source,
            dst_ref=target,
            send_sem=self.send.at[kind],
            recv_sem=self.recv.at[kind, place],
            device_id=device_id,
            device_id_type=MESH,
        ).start()

    def arrived(self, kind, place, ref):
        pltpu.make_async_copy(ref, ref, self.recv.at[kind, place]).wait()

    def sent(self, kind, ref):
        pltpu.make_async_copy(ref, ref, self.send.at[kind]).wait()


def kernel(chips, experts, held, names, *refs):
    r = types.SimpleNamespace(**dict(zip(names, refs, strict=True)))
    positions, width = r.tokens.shape
    head = r.kv_weight.shape[1] // 2
    count = 2 * positions
    dp, device = lax.axis_index("dp"), lax.axis_index("expert")
    chip, core = device // 2, device % 2
    y, x = dp // 2, dp % 2
    place = [x, y]
    sibling = (dp, chip * 2 + 1 - core)
    beside = [(2 * y + 1 - x, device), (2 * (1 - y) + x, device)]
    dp_count = r.kv_grad_dp.shape[0]
    around = [(lax.rem(dp + k, dp_count), device) for k in range(1, dp_count)]

    def store(slot, source, target):
        if held:
            target[...] = source[...].astype(target.dtype)
        else:
            pltpu.make_async_copy(source, target, r.out_sem.at[slot]).start()
            stored.append((slot, source, target))

    stored = []

    def ahead(k):
        return (dp, lax.rem(chip + k, chips) * 2 + core)

    loads = {}
    for i, name in enumerate(LOADS):
        loads[name] = pltpu.make_async_copy(
            getattr(r, name + "_hbm"), getattr(r, name), r.load_sem.at[i]
        )
        loads[name].start()

    def loaded(*wanted):
        for name in wanted:
            loads[name].wait()

    barrier = pltpu.get_barrier_semaphore()
    for peer in [sibling] + around:
        pl.semaphore_signal(barrier, inc=1, device_id=peer, device_id_type=MESH)
    loop(
        chips - 1,
        lambda k: pl.semaphore_signal(
            barrier, inc=1, device_id=ahead(k + 1), device_id_type=MESH
        ),
    )

    loaded("tokens", "gain_one", "kv_weight", "segments")
    normed = (moments(r.tokens[...].astype(F32))[0] * r.gain_one[...]).astype(LOW)
    r.normed[...] = normed
    r.kv[0, :positions] = dot(normed, r.kv_weight[...], 1, 0).astype(LOW)
    segs = r.segments[...].astype(F32)
    lanes = 2 * head
    seg_rows = [segs[:, i * lanes : (i + 1) * lanes] for i in range(positions // lanes)]
    seg_rows.append(jnp.full((SEG_ROWS - len(seg_rows), lanes), 3.0, F32))
    r.kv[0, positions:] = jnp.concatenate(seg_rows, 0).astype(LOW)

    pl.semaphore_wait(barrier, chips + dp_count - 1)

    kv_links = Links(r.kv_send, r.kv_recv)

    parts = (slice(0, positions // 2), slice(positions // 2, positions + SEG_ROWS))

    def kv_copy(source, target, device_id, part):
        rows = parts[part]
        kv_links.start(0, 2 * target + part, r.kv.at[source, rows], r.kv.at[target, rows], device_id)

    def kv_copies(source, target, device_id):
        for part in range(2):
            kv_copy(source, target, device_id, part)

    def kv_arrived(slot, part):
        kv_links.arrived(0, 2 * slot + part, r.kv.at[slot, parts[part]])

    side, turn_of, same_side = chip % 2, chip // 2, chips // 2
    next_chip = (dp, (chip + 1 - 2 * side) * 2 + core)
    loop(same_side - 1, lambda s: kv_copies(0, 2 * (s + 1), ahead(2 * (s + 1))))
    kv_copies(0, 1, sibling)

    loaded("query_all", "ids", "keep", "router")
    ids = r.ids[...]
    kept = r.keep[...].astype(F32)
    queries = jnp.concatenate(
        pick(ids, dot(r.query_all[...], r.normed[...], 1, 1), experts, head), 1
    )
    queries = queries.astype(LOW).astype(F32) * SCALE
    seg_twice = jnp.concatenate([segs, segs], 1)
    others = [jnp.where(seg_twice == s, 0.0, NEGATIVE) for s in range(3)]
    blank = jnp.zeros((head, count), F32)
    r.q_aug[0 : 2 * head] = jnp.concatenate([queries, blank], 0).astype(LOW)
    r.q_aug[2 * head :] = jnp.concatenate(
        others + [jnp.zeros((2 * head - 3, count), F32)], 0
    ).astype(LOW)
    r.q_rows[0:count] = jnp.concatenate([queries, blank], 0).T.astype(LOW)
    logits = dot(r.router[...], r.normed[...], 1, 1)
    places = lax.broadcasted_iota(jnp.int32, logits.shape, 0)
    onehots = [(places == ids[c : c + 1]).astype(F32) for c in range(2)]
    chosen = [jnp.sum(onehots[c] * logits, 0, keepdims=True) for c in range(2)]
    top = jnp.maximum(chosen[0], chosen[1])
    expo = [jnp.exp(chosen[c] - top) for c in range(2)]
    r.soft[...] = jnp.concatenate([e / (expo[0] + expo[1]) for e in expo], 0)
    r.gates[...] = r.soft[...] * kept

    kv_copies(0, 2 * same_side, next_chip)
    r.peak[...] = jnp.full(r.peak.shape, -3e38, F32)
    r.total[...] = jnp.zeros(r.total.shape, F32)

    def key_block(slot):
        block = r.kv[slot, :positions]
        seg = r.kv[slot, positions:].astype(F32)
        first = jnp.sum(jnp.where(seg < 0.5, 1.0, 0.0), keepdims=True)
        second = jnp.sum(jnp.where(seg < 1.5, 1.0, 0.0), keepdims=True)
        row = lax.broadcasted_iota(jnp.int32, (positions, lanes), 0).astype(F32)
        lane = lax.broadcasted_iota(jnp.int32, (positions, lanes), 1)
        segment = jnp.where(row < first, 0, jnp.where(row < second, 1, 2))
        extra = jnp.where((segment == lane) | ((lane >= 3) & (lane < 6)), 1.0, 0.0)
        return block, jnp.concatenate([block, extra.astype(LOW)], 1)

    def attend(slot):
        block, keys = key_block(slot)
        values_t = jnp.concatenate([jnp.ones((16, positions), LOW), block.T[head:]], 0)
        scores = dot(keys, r.q_aug[...], 1, 0)
        old = r.peak[...]
        new = jnp.maximum(old, jnp.max(scores, 0, keepdims=True))
        probs = jnp.exp(scores - new).astype(LOW)
        r.total[...] = r.total[...] * jnp.exp(old - new) + dot(values_t, probs, 1, 0)
        r.peak[...] = new

    def attend_chip(j):
        for part in range(2):

            @pl.when(j > 0)
            def _():
                kv_arrived(2 * j, part)
                kv_copy(2 * j, 2 * j + 1, sibling, part)

            @pl.when((j > 0) & (j < same_side))
            def _():
                kv_copy(2 * j, 2 * (same_side + j), next_chip, part)

        attend(2 * j)
        for part in range(2):
            kv_arrived(2 * j + 1, part)
        attend(2 * j + 1)

    loop(chips, attend_chip)

    weight = r.total[0:1]
    attended = r.total[16:] / weight
    log_total = r.peak[...] + jnp.log(weight)
    r.total[16:] = attended
    r.q_aug[2 * head :] = jnp.concatenate(
        others + thirds(-log_total) + [jnp.zeros((2 * head - 6, count), F32)], 0
    ).astype(LOW)
    halves = [attended[:, :positions], attended[:, positions:]]
    gates = r.gates[...]
    r.gated[...] = spread(ids, [halves[c] * gates[c : c + 1] for c in range(2)], experts)
    loaded("out_all", "gain_two")
    mixed = r.tokens[...].astype(F32) + dot(r.gated[...], r.out_all[...], 0, 0)
    r.mixed[...] = mixed
    hidden = (moments(mixed)[0] * r.gain_two[...]).astype(LOW)
    r.hidden[...] = hidden
    r.hidden_t[...] = hidden.T

    groups, line_rows = r.line_sum.shape[:2]
    each = CHUNKS // groups
    share = line_rows // chips
    half, quarter, eighth = width // 2, width // 4, width // 8
    halving = Links(r.halving_send, r.halving_recv)
    line = Links(r.line_send, r.line_recv)

    PAIR, NEAR, FAR, FAR_BACK, NEAR_BACK, PAIR_BACK = range(6)
    LINE, LINE_BACK = range(2)

    def both_of(c):
        return pl.ds(2 * c, 2)

    def stage_0(c):
        for w in range(2):
            b = 2 * c + w
            source = r.own.at[b, cut((1 - core) * half, half)]
            halving.start(PAIR, c, source, r.pair_in.at[b], sibling)

    def stage_1(c):
        halving.arrived(PAIR, c, r.pair_in.at[both_of(c)])
        for w in range(2):
            b = 2 * c + w
            at = cut(core * half, half)
            r.own[b, at] = low_sum(r.own[b, at], r.pair_in[b])
            source = r.own.at[b, cut(core * half + (1 - place[w]) * quarter, quarter)]
            halving.start(NEAR, c, source, r.near_in.at[b], beside[w])

    def stage_2(c):
        halving.arrived(NEAR, c, r.near_in.at[both_of(c)])
        for w in range(2):
            b = 2 * c + w
            at = cut(core * half + place[w] * quarter, quarter)
            r.own[b, at] = low_sum(r.own[b, at], r.near_in[b])
            to = core * half + place[w] * quarter + (1 - place[1 - w]) * eighth
            source = r.own.at[b, cut(to, eighth)]
            halving.start(FAR, c, source, r.far_in.at[b], beside[1 - w])

    def stage_3(c):
        g = c // each
        halving.arrived(FAR, c, r.far_in.at[both_of(c)])
        for w in range(2):
            b = 2 * c + w
            at = cut(core * half + place[w] * quarter + place[1 - w] * eighth, eighth)
            to = (c % each * 2 + w) * eighth
            r.line_sum[g, to : to + eighth] = low_sum(r.own[b, at], r.far_in[b])
        if c % each == each - 1:

            def send_share(k):
                source = r.line_sum.at[g, cut(lax.rem(chip + k + 1, chips) * share, share)]
                line.start(LINE, g, source, r.line_in.at[g, k], ahead(k + 1))

            loop(chips - 1, send_share)

    def at_group_end(body):
        def stage(c):
            if c % each == each - 1:
                body(c // each)

        return stage

    my_share = cut(chip * share, share)

    @at_group_end
    def stage_4(g):
        line.arrived(LINE, g, r.line_in.at[g])

        def add_line(k, sum_so_far):
            return sum_so_far + r.line_in[g, k].astype(F32)

        summed = lax.fori_loop(0, chips - 1, add_line, r.line_sum[g, my_share].astype(F32))
        r.line_whole[g, my_share] = summed.astype(LOW)
        ref = r.line_whole.at[g, my_share]
        loop(chips - 1, lambda k: line.start(LINE_BACK, g, ref, ref, ahead(k + 1)))

    def blocks_of(g):
        for i in range(2 * each):
            yield i, i % 2, g * 2 * each + i

    def group_at(g):
        return pl.ds(g * 2 * each, 2 * each)

    @at_group_end
    def stage_5(g):
        line.arrived(LINE_BACK, g, r.line_in.at[g])
        for i, w, b in blocks_of(g):
            at = cut(core * half + place[w] * quarter + place[1 - w] * eighth, eighth)
            r.whole[b, at] = r.line_whole[g, i * eighth : (i + 1) * eighth]
            source = r.line_whole.at[g, i * eighth : (i + 1) * eighth]
            halving.start(FAR_BACK, g, source, r.whole.at[b, at], beside[1 - w])

    @at_group_end
    def stage_6(g):
        halving.arrived(FAR_BACK, g, r.far_in.at[group_at(g)])
        for i, w, b in blocks_of(g):
            ref = r.whole.at[b, cut(core * half + place[w] * quarter, quarter)]
            halving.start(NEAR_BACK, g, ref, ref, beside[w])

    @at_group_end
    def stage_7(g):
        halving.arrived(NEAR_BACK, g, r.near_in.at[group_at(g)])
        for i, w, b in blocks_of(g):
            ref = r.whole.at[b, cut(core * half, half)]
            halving.start(PAIR_BACK, g, ref, ref, sibling)

    @at_group_end
    def stage_8(g):
        halving.arrived(PAIR_BACK, g, r.pair_in.at[group_at(g)])
        for i, w, b in blocks_of(g):
            if held:
                r.big_out[b] = r.whole[b].astype(F32)
            else:
                pltpu.make_async_copy(r.whole.at[b], r.big_out.at[b], r.store_sem.at[0]).start()

    def big_sent():
        for kind in (PAIR, PAIR_BACK):
            halving.sent(kind, r.pair_in)
        for kind in (NEAR, NEAR_BACK):
            halving.sent(kind, r.near_in)
        for kind in (FAR, FAR_BACK):
            halving.sent(kind, r.far_in)
        for kind in (LINE, LINE_BACK):
            line.sent(kind, r.line_in)
        if not held:
            pltpu.make_async_copy(r.whole, r.big_out, r.store_sem.at[0]).wait()

    few = experts // 2
    my_experts = pl.ds(core * few, few)
    fine = width // chips % 128 == 0
    expert_links = Links(r.expert_send, r.expert_recv)
    EXPERT_PAIR, EXPERT_NEAR, EXPERT_FAR, EXPERT_LINE, EXPERT_LAST = range(5)

    def expert_half(a, first, second):
        if a == 0:
            if second is None:
                return (a, my_experts, first)
            return (a, my_experts, first, second)
        if second is None:
            return (a, my_experts, slice(None), first)
        return (a, my_experts, second, first)

    order = [(y, x), (x, y)]
    sides = [(beside[1], beside[0]), (beside[0], beside[1])]

    def expert_columns(c):
        return pl.ds(pl.multiple_of(c * (width // chips), 128), width // chips)

    def expert_0(a):
        source = r.expert_own.at[a, pl.ds((1 - core) * few, few)]
        expert_links.start(EXPERT_PAIR, a, source, r.expert_pair.at[a], sibling)

    def expert_1(a):
        expert_links.arrived(EXPERT_PAIR, a, r.expert_pair.at[a])
        r.expert_own[a, my_experts] = low_sum(r.expert_own[a, my_experts], r.expert_pair[a])
        source = r.expert_own.at[expert_half(a, 1 - order[a][0], None)]
        expert_links.start(EXPERT_NEAR, a, source, r.expert_near.at[a], sides[a][0])

    def expert_2(a):
        expert_links.arrived(EXPERT_NEAR, a, r.expert_near.at[a])
        at = expert_half(a, order[a][0], None)
        r.expert_own[at] = low_sum(r.expert_own[at], r.expert_near[a])
        source = r.expert_own.at[expert_half(a, order[a][0], 1 - order[a][1])]
        expert_links.start(EXPERT_FAR, a, source, r.expert_far.at[a], sides[a][1])

    def expert_3(a):
        expert_links.arrived(EXPERT_FAR, a, r.expert_far.at[a])
        at = expert_half(a, *order[a])
        r.expert_quarter[a] = low_sum(r.expert_own[at], r.expert_far[a])

        def send_columns(k):
            source = r.expert_quarter.at[a, :, :, expert_columns(lax.rem(chip + k + 1, chips))]
            expert_links.start(EXPERT_LINE, a, source, r.expert_line.at[a, k], ahead(k + 1))

        if fine:
            loop(chips - 1, send_columns)

    def expert_4(a):
        if not fine:
            return
        expert_links.arrived(EXPERT_LINE, a, r.expert_line.at[a])

        def add_line(k, sum_so_far):
            return sum_so_far + r.expert_line[a, k].astype(F32)

        own_part = r.expert_quarter[a, :, :, expert_columns(chip)].astype(F32)
        r.expert_last[a, 0] = lax.fori_loop(0, chips - 1, add_line, own_part).astype(LOW)
        source, target = r.expert_last.at[a, 0], r.expert_last.at[a, 1]
        expert_links.start(EXPERT_LAST, a, source, target, sibling)

    def expert_5(a):
        if fine:
            expert_links.arrived(EXPERT_LAST, a, r.expert_last.at[a, 1])
            part = width // chips // 2
            mine = r.expert_last[a, 0].astype(F32)
            other = r.expert_last[a, 1].astype(F32)
            for i in range(2):
                rows = jnp.where(core == i, mine, other)
                r.expert_out[a, i * few : (i + 1) * few] = jnp.where(
                    core == 0, rows[:, :, :part], rows[:, :, part:]
                )
        else:
            r.expert_out[a] = r.expert_quarter[a]
        store(a, r.expert_out.at[a], r.experts_out.at[a])

    def expert_sent():
        expert_links.sent(EXPERT_PAIR, r.expert_pair)
        expert_links.sent(EXPERT_NEAR, r.expert_near)
        expert_links.sent(EXPERT_FAR, r.expert_far)
        if fine:
            expert_links.sent(EXPERT_LINE, r.expert_line)
            expert_links.sent(EXPERT_LAST, r.expert_last.at[:, 0])

    late = Links(r.late_send, r.late_recv)
    KV_PAIR, KV_DP, KV_LINE, KV_DP_BACK, KV_PAIR_BACK, VEC_PAIR, VEC_DP, VEC_LINE = range(8)
    kv_half = width // 2
    kv_part = kv_half // dp_count
    others_dp = range(1, dp_count)
    kv_mine = cut(core * kv_half, kv_half)
    kv_share = cut(core * kv_half + dp * kv_part, kv_part)

    def kv_0():
        source = r.kv_grad.at[cut((1 - core) * kv_half, kv_half)]
        late.start(KV_PAIR, 0, source, r.kv_grad_pair, sibling)

    def kv_1():
        late.arrived(KV_PAIR, 0, r.kv_grad_pair)
        r.kv_grad[kv_mine] = low_sum(r.kv_grad[kv_mine], r.kv_grad_pair[...])
        for k in others_dp:
            at = cut(core * kv_half + lax.rem(dp + k, dp_count) * kv_part, kv_part)
            late.start(KV_DP, 0, r.kv_grad.at[at], r.kv_grad_dp.at[k], around[k - 1])

    def to_line(kind, buffer, value):
        buffer[chip] = value.astype(LOW)
        ref = buffer.at[chip]
        loop(chips - 1, lambda k: late.start(kind, 0, ref, ref, ahead(k + 1)))

    def from_line(kind, buffer):
        late.arrived(kind, 0, buffer.at[1:])

        def add(k, sum_so_far):
            return sum_so_far + buffer[k].astype(F32)

        return lax.fori_loop(1, chips, add, buffer[0].astype(F32))

    def kv_2():
        late.arrived(KV_DP, 0, r.kv_grad_dp.at[1:])
        summed = r.kv_grad[kv_share].astype(F32)
        for k in others_dp:
            summed = summed + r.kv_grad_dp[k].astype(F32)
        to_line(KV_LINE, r.kv_grad_line, summed)

    def kv_3():
        r.kv_grad_whole[kv_share] = from_line(KV_LINE, r.kv_grad_line).astype(LOW)
        ref = r.kv_grad_whole.at[kv_share]
        for k in others_dp:
            late.start(KV_DP_BACK, 0, ref, ref, around[k - 1])

    def kv_4():
        late.arrived(KV_DP_BACK, 0, r.kv_grad_dp.at[1:])
        ref = r.kv_grad_whole.at[kv_mine]
        late.start(KV_PAIR_BACK, 0, ref, ref, sibling)

    def kv_5():
        late.arrived(KV_PAIR_BACK, 0, r.kv_grad_pair)
        store(2, r.kv_grad_whole, r.kv_out_whole)

    def vectors_0():
        late.start(VEC_PAIR, 0, r.vectors, r.vectors_pair, sibling)

    def vectors_1():
        late.arrived(VEC_PAIR, 0, r.vectors_pair)
        r.vectors_dp[dp] = low_sum(r.vectors[...], r.vectors_pair[...])
        ref = r.vectors_dp.at[dp]
        for k in others_dp:
            late.start(VEC_DP, 0, ref, ref, around[k - 1])

    def vectors_2():
        late.arrived(VEC_DP, 0, r.vectors_dp.at[1:])
        summed = r.vectors_dp[0].astype(F32)
        for k in others_dp:
            summed = summed + r.vectors_dp[k].astype(F32)
        to_line(VEC_LINE, r.vectors_line, summed)

    def vectors_3():
        r.vectors_whole[...] = from_line(VEC_LINE, r.vectors_line)
        store(3, r.vectors_whole, r.vectors_out)

    def late_sent():
        late.sent(KV_PAIR, r.kv_grad_pair)
        late.sent(KV_PAIR_BACK, r.kv_grad_pair)
        late.sent(VEC_PAIR, r.vectors_pair)
        late.sent(KV_DP, r.kv_grad_dp.at[1:])
        late.sent(KV_DP_BACK, r.kv_grad_dp.at[1:])
        late.sent(VEC_DP, r.vectors_dp.at[1:])
        late.sent(KV_LINE, r.kv_grad_line.at[1:])
        late.sent(VEC_LINE, r.vectors_line.at[1:])

    stages = {
        "e1": expert_1,
        "e2": expert_2,
        "e3": expert_3,
        "e4": expert_4,
        "e5": expert_5,
        "k1": kv_1,
        "k2": kv_2,
        "k3": kv_3,
        "k4": kv_4,
        "k5": kv_5,
        "v1": vectors_1,
        "v2": vectors_2,
        "v3": vectors_3,
    }
    for i, stage in enumerate(
        [stage_1, stage_2, stage_3, stage_4, stage_5, stage_6, stage_7, stage_8]
    ):
        stages[i + 1] = stage

    def do(event):
        stages[event[0]](*event[1:])

    def service(plan, turn):
        for at, events in enumerate(plan):
            for event in events:
                pl.when(turn == at)(functools.partial(do, event))

    loaded("up", "cot", "down")
    chunk = r.own.shape[2]

    def layer_output():
        out = r.mixed[...] + dot(r.act[...], r.down[...], 1, 0)
        r.layer_low[...] = out.astype(LOW)
        store(4, r.layer_low, r.layer_out)

    stages["o"] = layer_output

    def units_of(c):
        return pl.ds(pl.multiple_of(c * chunk, chunk), chunk)

    def feed(c):
        units = units_of(c)
        value, slope = gelu_both(dot(r.hidden[...], r.up[:, units], 1, 0))
        r.act[:, units] = value.astype(LOW)
        r.grad_pre[:, units] = (dot(r.cot[...], r.down[units], 1, 1) * slope).astype(LOW)

    def weigh(c):
        units = units_of(c)
        r.own[2 * c] = dot(r.hidden_t[...], r.grad_pre[:, units], 1, 0).astype(LOW)
        down_grad = dot(r.act[:, units], r.cot[...], 0, 0).astype(LOW)
        for i in range(width // chunk):
            at = slice(i * chunk, (i + 1) * chunk)
            r.own[2 * c + 1, at] = down_grad[:, at]

    def feed_next(c):
        weigh(c)
        feed(c + 1)
        stage_0(c)
        service(FEED_PLAN, c)

    feed(0)
    loop(CHUNKS - 1, feed_next)
    weigh(CHUNKS - 1)
    stage_0(CHUNKS - 1)
    for event in FEED_PLAN[CHUNKS - 1]:
        do(event)

    hat, scale = moments(r.mixed[...])
    grad = dot(r.grad_pre[...], r.up[...], 1, 1)
    grad, gain = norm_back(hat, scale, r.gain_two[...], grad)
    grad = grad + r.cot[...].astype(F32)
    r.grad_mixed[...] = grad
    r.grad_mixed_low[...] = grad.astype(LOW)
    r.gain_grad[...] = gain
    for event in MIX_PLAN:
        do(event)

    shown = pick(ids, dot(r.out_all[...], r.grad_mixed_low[...], 1, 1), experts, head)
    expert_shape = r.expert_own.shape[1:]
    r.expert_own[0] = dot(r.gated[...], r.grad_mixed_low[...], 1, 0).astype(LOW).reshape(expert_shape)
    expert_0(0)
    attended = r.total[16:]
    grad_gates = [
        jnp.sum(shown[c] * attended[:, c * positions : (c + 1) * positions], 0, keepdims=True)
        for c in range(2)
    ]
    gates = r.gates[...]
    soft = [r.soft[c : c + 1] for c in range(2)]
    kept_grad = [grad_gates[c] * kept[c : c + 1] for c in range(2)]
    inner = soft[0] * kept_grad[0] + soft[1] * kept_grad[1]
    grad_logits = onehots[0] * (soft[0] * (kept_grad[0] - inner)) + onehots[1] * (
        soft[1] * (kept_grad[1] - inner)
    )
    r.grad_logits[...] = jnp.concatenate(thirds(grad_logits), 0).astype(LOW)
    in_thirds = dot(r.grad_logits[...], r.normed[...], 1, 0)
    r.router_grad[...] = (
        in_thirds[:experts] + in_thirds[experts : 2 * experts] + in_thirds[2 * experts :]
    )
    delta = jnp.concatenate([gates[c : c + 1] * grad_gates[c] for c in range(2)], 1)
    grad_attended = jnp.concatenate([gates[c : c + 1] * shown[c] for c in range(2)], 1)
    stacked = jnp.concatenate([blank, grad_attended], 0)
    r.o_aug[0 : 2 * head] = stacked.astype(LOW)
    r.o_aug[2 * head :] = jnp.concatenate(
        [jnp.zeros((3, count), F32)] + thirds(-delta) + [jnp.zeros((2 * head - 6, count), F32)], 0
    ).astype(LOW)
    r.q_rows[count:] = stacked.T.astype(LOW)
    for event in GATE_PLAN:
        do(event)

    r.grad_q[...] = jnp.zeros(r.grad_q.shape, F32)
    back_links = Links(r.back_send, r.back_recv)
    BACK_PAIR, BACK_NEXT, BACK_LINE = range(3)
    span = count // SPANS

    def target_chip(step):
        back = lax.rem(step + 1, same_side)
        return back, back + jnp.where(step < same_side, same_side, 0)

    def back_keys(k):
        for i in range(2):
            at = slice(i * positions, (i + 1) * positions)
            block, keys = key_block(2 * k + i)
            r.keys[at] = keys
            r.keys_t[:, at] = block.T[:head]

    def back_pair(step):
        back, _ = target_chip(step)
        back_links.arrived(BACK_PAIR, step, r.kv_pair.at[step])
        both = r.part[lax.rem(step, 2), :positions] + r.kv_pair[step].astype(F32)
        r.kv_pair[step] = both.astype(LOW)

        @pl.when(step < same_side)
        def _():
            back_links.start(BACK_NEXT, back, r.kv_pair.at[step], r.kv_next.at[back], next_chip)

        @pl.when(step == chips - 1)
        def _():
            r.kv_own[...] = both

    def back_line():
        def send(s):
            back, step = s + 1, same_side + s
            back_links.arrived(BACK_NEXT, back, r.kv_next.at[back])
            r.kv_pair[step] = low_sum(r.kv_pair[step], r.kv_next[back])
            target = (dp, lax.rem(chip + chips - 2 * back, chips) * 2 + core)
            back_links.start(BACK_LINE, 0, r.kv_pair.at[step], r.kv_line.at[s], target)

        loop(same_side - 1, send)

    stages["x"] = lambda: back_pair(chips - 1)
    stages["r"] = back_line

    def spans_of(turn):
        at = lax.rem(turn, SPANS) * span
        return pl.ds(pl.multiple_of(at, span), span), pl.ds(pl.multiple_of(count + at, span), span)

    def weights_of(turn):
        at, _ = spans_of(turn)
        keys = r.keys[...]
        probs = jnp.exp(dot(keys, r.q_aug[:, at], 1, 0))
        grads = (probs * dot(keys, r.o_aug[:, at], 1, 0)).astype(LOW)
        return probs.astype(LOW), grads

    def sums_of(turn):
        at, also = spans_of(turn)
        now = lax.rem(turn // SPANS, 2)
        probs, grads = r.probs[...], r.grads[...]
        r.grad_q[:, at] = r.grad_q[:, at] + dot(r.keys_t[now], grads, 1, 0)
        r.part[now] = (
            r.part[now] + dot(grads, r.q_rows[at], 1, 0) + dot(probs, r.q_rows[also], 1, 0)
        )

    def start_step(step):
        _, k = target_chip(step)
        now = lax.rem(step, 2)
        for i in range(2):
            at = slice(i * positions, (i + 1) * positions)
            block, keys = key_block(2 * k + i)
            r.keys[at] = keys
            r.keys_t[now, :, at] = block.T[:head]
        r.part[now] = jnp.zeros(r.part.shape[1:], F32)

    def end_step(step):
        r.kv_out[step] = r.part[lax.rem(step, 2), positions:].astype(LOW)
        back_links.start(BACK_PAIR, step, r.kv_out.at[step], r.kv_pair.at[step], sibling)

    def back_turn(i):
        turn = i + 1
        step, at_span = turn // SPANS, lax.rem(turn, SPANS)
        pl.when(at_span == 0)(functools.partial(start_step, step))
        sums_of(turn - 1)
        r.probs[...], r.grads[...] = weights_of(turn)
        pl.when(at_span == 0)(functools.partial(end_step, step - 1))
        pl.when((at_span == 1) & (step > 0))(functools.partial(back_pair, step - 1))
        service(block_plan, turn)

    block_plan, line_first = BLOCK_PLAN, False
    if chips != 4:
        line_first = any(("r",) in events for events in BLOCK_PLAN)
        block_plan = [[event for event in events if event != ("r",)] for events in BLOCK_PLAN]
    turns = SPANS * chips
    start_step(0)
    r.probs[...], r.grads[...] = weights_of(0)
    for event in block_plan[0]:
        do(event)
    loop(turns - 1, back_turn)
    sums_of(turns - 1)
    end_step(chips - 1)
    for events in block_plan[min(turns, len(block_plan) - 1) :]:
        for event in events:
            do(event)

    def query_grads():
        grad_queries = r.grad_q[...] * SCALE
        r.grad_spread[...] = spread(
            ids, [grad_queries[:, :positions], grad_queries[:, positions:]], experts
        )
        grads = dot(r.grad_spread[...], r.normed[...], 1, 0).astype(LOW)
        r.expert_own[1] = grads.reshape(expert_shape)
        expert_0(1)

    def token_sum():
        routers = jnp.concatenate([r.router[...].astype(F32)] * 3, 0).astype(LOW)
        r.grad_normed[...] = dot(r.grad_spread[...], r.query_all[...], 0, 0) + dot(
            r.grad_logits[...], routers, 0, 0
        )

    def kv_grads():
        back_links.arrived(BACK_NEXT, 0, r.kv_next.at[0])
        if same_side > 1:
            back_links.arrived(BACK_LINE, 0, r.kv_line)

        def add_in(k, sum_so_far):
            return sum_so_far + r.kv_line[k].astype(F32)

        summed = r.kv_own[...] + r.kv_next[0].astype(F32)
        grad_kv = lax.fori_loop(0, same_side - 1, add_in, summed).astype(LOW)
        r.kv_grad_own[...] = grad_kv
        r.kv_grad[...] = dot(r.normed[...], grad_kv, 0, 0).astype(LOW)
        kv_0()

    def token_grads():
        grad = r.grad_normed[...] + dot(r.kv_grad_own[...], r.kv_weight[...], 1, 1)
        hat, scale = moments(r.tokens[...].astype(F32))
        grad, gain = norm_back(hat, scale, r.gain_one[...], grad)
        rest = jnp.zeros((r.vectors.shape[0] - experts - 2, width), F32)
        r.vectors[...] = jnp.concatenate(
            [r.router_grad[...], gain, r.gain_grad[...], rest], 0
        ).astype(LOW)
        vectors_0()
        r.grad_mixed[...] = grad + r.grad_mixed[...]
        store(5, r.grad_mixed, r.tokens_out)

    stages.update(q=query_grads, u=token_sum, k=kv_grads, t=token_grads)
    for event in TAIL_PLAN:
        do(event)
        if event == ("x",) and line_first:
            back_line()

    big_sent()
    expert_sent()
    late_sent()
    for slot, source, target in stored:
        pltpu.make_async_copy(source, target, r.out_sem.at[slot]).wait()
    kv_links.sent(0, r.kv.at[1:])
    back_links.sent(BACK_PAIR, r.kv_out)
    back_links.sent(BACK_NEXT, r.kv_next)
    if same_side > 1:
        back_links.sent(BACK_LINE, r.kv_line)


LOADS = (
    "tokens",
    "gain_one",
    "kv_weight",
    "segments",
    "query_all",
    "ids",
    "keep",
    "router",
    "out_all",
    "gain_two",
    "up",
    "cot",
    "down",
)


def finish(names, held, *refs):
    r = types.SimpleNamespace(**dict(zip(names, refs, strict=True)))
    blocks, width, chunk = r.big_out.shape
    experts = r.grad_router.shape[0]
    sources = [r.layer_out, r.tokens_out, r.vectors_out, r.kv_out_whole]
    started = []

    def store(source, target):
        copy = pltpu.make_async_copy(source, target, r.store_sem.at[len(started)])
        copy.start()
        started.append(copy)

    def store_block(b, source):
        c = b // 2
        at = slice(c * chunk, (c + 1) * chunk)
        if b % 2 == 0:
            pltpu.make_async_copy(source, r.grad_up.at[:, at], r.block_sem.at[0]).start()
            return
        for i in range(width // chunk):
            part = slice(i * chunk, (i + 1) * chunk)
            target = r.grad_down.at[at, part]
            pltpu.make_async_copy(source.at[part], target, r.block_sem.at[0]).start()

    if held:
        for b in range(blocks):
            store_block(b, r.big_out.at[b])
        layer, tokens, vectors, kv = sources
        full = r.big_out
    else:
        loads = [
            pltpu.make_async_copy(r.big_out.at[b], r.big_low.at[b], r.load_sem.at[b])
            for b in range(blocks)
        ]
        arrays = [r.layer_held, r.tokens_held, r.vectors_held, r.kv_held]
        small = [
            pltpu.make_async_copy(a, b, r.small_sem.at[i])
            for i, (a, b) in enumerate(zip(sources, arrays, strict=True))
        ]
        for load in loads + small:
            load.start()
        for b in range(blocks):
            loads[b].wait()
            r.big_full[b] = r.big_low[b].astype(F32)
            store_block(b, r.big_full.at[b])
        for load in small:
            load.wait()
        r.kv_full[...] = r.kv_held[...].astype(F32)
        layer, tokens, vectors, kv = arrays[:3] + [r.kv_full]
        full = r.big_full
    store(layer, r.layer)
    store(tokens, r.grad_tokens)
    store(kv, r.grad_kv_weight)
    store(vectors.at[0:experts], r.grad_router)
    store(vectors.at[experts : experts + 1], r.grad_gain_one)
    store(vectors.at[experts + 1 : experts + 2], r.grad_gain_two)
    if held:
        store(r.experts_out.at[0], r.grad_out)
        store(r.experts_out.at[1], r.grad_query)
    for copy in started:
        copy.wait()
    pltpu.make_async_copy(full, full, r.block_sem.at[0]).wait()


def shards(
    tokens,
    segments,
    expert_ids,
    keep,
    gain_one,
    kv_weight,
    router_weight,
    query_weight,
    out_weight,
    gain_two,
    up_weight,
    down_weight,
    cotangent,
):
    positions, width = tokens.shape[1:]
    experts, _, head = query_weight.shape
    hidden_units = up_weight.shape[1]
    dps, chips = lax.axis_size("dp"), lax.axis_size("expert") // 2
    chunk = hidden_units // CHUNKS
    blocks = 2 * CHUNKS
    groups = max(1, min(CHUNKS, blocks * (width // 8) // (16 * chips)))
    line_rows = blocks * (width // 8) // groups
    count = 2 * positions
    few = experts // 2
    fine = width // chips % 128 == 0
    part = width // chips if fine else 128
    rows = 2 * experts

    inputs = dict(
        tokens=tokens[0],
        gain_one=gain_one[None],
        kv_weight=kv_weight,
        segments=segments,
        query_all=jnp.swapaxes(query_weight, 1, 2).reshape(experts * head, width),
        ids=expert_ids[0].T,
        keep=keep[0].T,
        router=router_weight.T,
        out_all=jnp.swapaxes(out_weight, 1, 2).reshape(experts * head, width),
        gain_two=gain_two[None],
        up=up_weight,
        cot=cotangent[0],
        down=down_weight,
    )
    inputs = {name: inputs[name] for name in LOADS}
    hbm = pl.BlockSpec(memory_space=pl.ANY)

    def struct(*shape_and_type):
        return jax.ShapeDtypeStruct(shape_and_type[:-1], shape_and_type[-1])

    def vmem(*shape_and_type):
        return pltpu.VMEM(shape_and_type[:-1], shape_and_type[-1])

    def dma(*shape):
        return pltpu.SemaphoreType.DMA(shape)

    expert_out = (few, head // 4, width, LOW)
    if fine:
        expert_out = (experts, head // 4, part // 2, F32)
    held = fine
    outputs = dict(
        layer_out=(positions, width, LOW),
        tokens_out=(positions, width, F32),
        kv_out_whole=(width, 2 * head, F32 if held else LOW),
        vectors_out=(rows, width, F32),
        experts_out=(2, *expert_out),
        big_out=(blocks, width, chunk, F32 if held else LOW),
    )
    between = vmem if held else struct
    outputs = {name: between(*value) for name, value in outputs.items()}
    vmem_spec = pl.BlockSpec(memory_space=pltpu.VMEM)
    passed = vmem_spec if held else hbm
    scratch = {name: vmem(*value.shape, value.dtype) for name, value in inputs.items()}
    scratch.update(
        normed=vmem(positions, width, LOW),
        kv=vmem(2 * chips, positions + SEG_ROWS, 2 * head, LOW),
        q_aug=vmem(4 * head, count, LOW),
        o_aug=vmem(4 * head, count, LOW),
        q_rows=vmem(2 * count, 2 * head, LOW),
        peak=vmem(1, count, F32),
        total=vmem(16 + head, count, F32),
        gates=vmem(2, positions, F32),
        soft=vmem(2, positions, F32),
        gated=vmem(experts * head, positions, LOW),
        mixed=vmem(positions, width, F32),
        hidden=vmem(positions, width, LOW),
        hidden_t=vmem(width, positions, LOW),
        act=vmem(positions, hidden_units, LOW),
        grad_pre=vmem(positions, hidden_units, LOW),
        layer_low=vmem(positions, width, LOW),
        grad_normed=vmem(positions, width, F32),
        grad_mixed=vmem(positions, width, F32),
        grad_mixed_low=vmem(positions, width, LOW),
        grad_logits=vmem(3 * experts, positions, LOW),
        router_grad=vmem(experts, width, F32),
        gain_grad=vmem(1, width, F32),
        grad_q=vmem(head, count, F32),
        kv_pair=vmem(chips, positions, 2 * head, LOW),
        kv_out=vmem(chips, positions, 2 * head, LOW),
        kv_next=vmem(max(1, chips // 2), positions, 2 * head, LOW),
        kv_line=vmem(max(1, chips // 2 - 1), positions, 2 * head, LOW),
        part=vmem(2, 2 * positions, 2 * head, F32),
        keys=vmem(2 * positions, 4 * head, LOW),
        keys_t=vmem(2, head, 2 * positions, LOW),
        probs=vmem(2 * positions, count // SPANS, LOW),
        grads=vmem(2 * positions, count // SPANS, LOW),
        kv_grad_own=vmem(positions, 2 * head, LOW),
        kv_own=vmem(positions, 2 * head, F32),
        grad_spread=vmem(experts * head, positions, LOW),
        expert_own=vmem(2, experts, 2, 2, head // 4, width, LOW),
        expert_pair=vmem(2, few, 2, 2, head // 4, width, LOW),
        expert_near=vmem(2, few, 2, head // 4, width, LOW),
        expert_far=vmem(2, few, head // 4, width, LOW),
        expert_quarter=vmem(2, few, head // 4, width, LOW),
        expert_line=vmem(2, chips - 1 if fine else 1, few, head // 4, part, LOW),
        expert_last=vmem(2, 2, few, head // 4, part, LOW),
        expert_out=vmem(2, *expert_out),
        kv_grad=vmem(width, 2 * head, LOW),
        kv_grad_pair=vmem(width // 2, 2 * head, LOW),
        kv_grad_dp=vmem(dps, width // 2 // dps, 2 * head, LOW),
        kv_grad_line=vmem(chips, width // 2 // dps, 2 * head, LOW),
        kv_grad_whole=vmem(width, 2 * head, LOW),
        vectors=vmem(rows, width, LOW),
        vectors_pair=vmem(rows, width, LOW),
        vectors_dp=vmem(dps, rows, width, LOW),
        vectors_line=vmem(chips, rows, width, LOW),
        vectors_whole=vmem(rows, width, F32),
        own=vmem(blocks, width, chunk, LOW),
        whole=vmem(blocks, width, chunk, LOW),
        pair_in=vmem(blocks, width // 2, chunk, LOW),
        near_in=vmem(blocks, width // 4, chunk, LOW),
        far_in=vmem(blocks, width // 8, chunk, LOW),
        line_sum=vmem(groups, line_rows, chunk, LOW),
        line_in=vmem(groups, chips - 1, line_rows // chips, chunk, LOW),
        line_whole=vmem(groups, line_rows, chunk, LOW),
        load_sem=dma(len(LOADS)),
        out_sem=dma(6),
        store_sem=dma(1),
        kv_send=dma(1),
        kv_recv=dma(1, 4 * chips),
        back_send=dma(3),
        back_recv=dma(3, chips),
        halving_send=dma(6),
        halving_recv=dma(6, CHUNKS),
        line_send=dma(2),
        line_recv=dma(2, groups),
        expert_send=dma(5),
        expert_recv=dma(5, 2),
        late_send=dma(8),
        late_recv=dma(8, 1),
    )
    names = [name + "_hbm" for name in LOADS] + list(outputs) + list(scratch)
    reduced = pl.pallas_call(
        functools.partial(kernel, chips, experts, held, names),
        out_shape=tuple(outputs.values()),
        in_specs=[hbm] * len(LOADS),
        out_specs=(passed,) * len(outputs),
        scratch_shapes=list(scratch.values()),
        compiler_params=pltpu.CompilerParams(
            collective_id=0, has_side_effects=True, vmem_limit_bytes=(LIMIT if held else 62) << 20
        ),
    )(*inputs.values())

    results = dict(
        layer=struct(positions, width, LOW),
        grad_tokens=struct(positions, width, F32),
        grad_gain_one=struct(1, width, F32),
        grad_kv_weight=struct(width, 2 * head, F32),
        grad_router=struct(experts, width, F32),
        grad_gain_two=struct(1, width, F32),
        grad_up=struct(width, hidden_units, F32),
        grad_down=struct(hidden_units, width, F32),
    )
    if fine:
        results.update(grad_out=struct(*expert_out), grad_query=struct(*expert_out))
    scratch = dict(store_sem=dma(len(results)), block_sem=dma(1))
    if not held:
        scratch.update(
            big_low=vmem(blocks, width, chunk, LOW),
            big_full=vmem(blocks, width, chunk, F32),
            kv_held=vmem(width, 2 * head, LOW),
            kv_full=vmem(width, 2 * head, F32),
            layer_held=vmem(positions, width, LOW),
            tokens_held=vmem(positions, width, F32),
            vectors_held=vmem(rows, width, F32),
            load_sem=dma(blocks),
            small_sem=dma(4),
        )
    names = list(outputs) + list(results) + list(scratch)
    finished = pl.pallas_call(
        functools.partial(finish, names, held),
        out_shape=tuple(results.values()),
        in_specs=[passed] * len(reduced),
        out_specs=(hbm,) * len(results),
        scratch_shapes=list(scratch.values()),
        compiler_params=pltpu.CompilerParams(vmem_limit_bytes=(4 if held else 62) << 20),
    )(*reduced)
    r = types.SimpleNamespace(**dict(zip(results, finished, strict=True)))

    def own_part(a):
        if fine:
            return jnp.swapaxes((r.grad_out, r.grad_query)[a], 1, 2)
        whole = jnp.zeros((2, few, head // 4, width), LOW)
        whole = whole.at[lax.axis_index("expert") % 2].set(reduced[4][a])
        whole = whole.reshape(experts, head // 4, width)
        whole = lax.psum_scatter(whole, "expert", scatter_dimension=2, tiled=True)
        return jnp.swapaxes(whole, 1, 2).astype(F32)

    return (
        r.layer[None],
        r.grad_tokens[None],
        r.grad_gain_one[0],
        r.grad_kv_weight,
        r.grad_router.T,
        own_part(1),
        own_part(0),
        r.grad_gain_two[0],
        r.grad_up,
        r.grad_down,
    )


def solution(mesh):
    row = P("dp", "expert", None)
    in_specs = (row, P("dp", "expert"), row, row) + (P(),) * 8 + (row,)
    expert = P(None, "expert", "dp")
    out_specs = (row, row, P(), P(), P(), expert, expert, P(), P(), P())
    return jax.shard_map(shards, mesh=mesh, in_specs=in_specs, out_specs=out_specs, check_vma=False)
```

```python
import functools
import types

import jax
import jax.numpy as jnp
from jax import lax
from jax.experimental import pallas as pl
from jax.experimental.pallas import tpu as pltpu
from jax.sharding import PartitionSpec as P

EPS = 1e-05
SCALE = 0.125
NEGATIVE = -1e30
LOW = jnp.bfloat16
F32 = jnp.float32
MESH = pl.DeviceIdType.MESH
LIMIT = 48
SPANS = 4
SEG_ROWS = 16
CHUNKS = 8
FEED_PLAN = (
    (),
    (),
    ((1, 0), ),
    ((1, 1), ),
    ((1, 2), ),
    (),
    ((2, 0), (1, 3), ),
    (),
)
MIX_PLAN = ((2, 2), )
GATE_PLAN = ((2, 1), (1, 5), (3, 0), )
BLOCK_PLAN = (
    (),
    ((2, 3), (3, 2), (1, 4), ),
    (),
    ((1, 7), (3, 1), ),
    ((3, 3), ),
    ((4, 0), (4, 2), (2, 4), (2, 5), ),
    (("e1", 0), ),
    (),
    ((1, 6), (4, 1), (4, 3), ),
    (),
    (),
    ((3, 5), ),
    ((3, 4), (5, 2), (2, 7), ),
    (("r",), (5, 0), (2, 6), ),
    ((5, 1), (5, 3), (6, 2), ),
    (),
    ((6, 0), ),
)
TAIL_PLAN = (
    ("q",),
    (3, 6),
    (6, 3),
    ("u",),
    (4, 4),
    ("e1", 1),
    (3, 7),
    ("x",),
    ("k",),
    ("t",),
    (4, 5),
    ("k1",),
    ("v1",),
    (4, 6),
    (6, 1),
    (5, 4),
    (4, 7),
    (7, 0),
    ("e2", 1),
    ("e2", 0),
    (7, 3),
    (5, 5),
    ("k2",),
    (5, 6),
    (7, 2),
    ("v2",),
    (6, 4),
    (5, 7),
    (6, 5),
    ("e3", 0),
    ("e3", 1),
    ("o",),
    ("k3",),
    (6, 6),
    (6, 7),
    (7, 1),
    (7, 5),
    ("v3",),
    (7, 4),
    ("e4", 0),
    ("e4", 1),
    ("k4",),
    (7, 6),
    ("e5", 1),
    (8, 2),
    (8, 3),
    (7, 7),
    (8, 4),
    (8, 6),
    (8, 5),
    ("e5", 0),
    (8, 0),
    (8, 1),
    ("k5",),
    (8, 7),
)

def dot(left, right, left_dim, right_dim):
    return lax.dot_general(
        left, right, (((left_dim,), (right_dim,)), ((), ())), preferred_element_type=F32
    )


def loop(count, body):
    def step(i, carry):
        body(i)
        return carry

    lax.fori_loop(0, count, step, 0)


def moments(values):
    mean = jnp.mean(values, -1, keepdims=True)
    centred = values - mean
    scale = lax.rsqrt(jnp.mean(centred * centred, -1, keepdims=True) + EPS)
    return centred * scale, scale


def norm_back(hat, scale, gain, grad):
    scaled = grad * gain
    inner = jnp.mean(scaled, -1, keepdims=True) + hat * jnp.mean(scaled * hat, -1, keepdims=True)
    return scale * (scaled - inner), jnp.sum(grad * hat, 0, keepdims=True)


def spread(ids, rows, experts):
    pieces = []
    for e in range(experts):
        pieces.append(
            jnp.where(ids[0:1] == e, rows[0], 0.0) + jnp.where(ids[1:2] == e, rows[1], 0.0)
        )
    return jnp.concatenate(pieces, 0).astype(LOW)


def pick(ids, everything, experts, head):
    picked = []
    for c in range(2):
        total = jnp.zeros((head, everything.shape[1]), F32)
        for e in range(experts):
            part = everything[e * head : (e + 1) * head]
            total = total + jnp.where(ids[c : c + 1] == e, part, 0.0)
        picked.append(total)
    return picked


def thirds(values):
    first = values.astype(LOW)
    rest = values - first.astype(F32)
    second = rest.astype(LOW)
    third = (rest - second.astype(F32)).astype(LOW)
    return [first.astype(F32), second.astype(F32), third.astype(F32)]


def gelu_both(x):
    root, cubic = 0.7978845608028654, 0.7978845608028654 * 0.044715
    square = x * x
    h = 0.5 + 0.5 * jnp.tanh(x * (root + cubic * square))
    slope = h * (1.0 + (1.0 - h) * (x * (2.0 * root + 6.0 * cubic * square)))
    return x * h, slope


def low_sum(first, second):
    return (first.astype(F32) + second.astype(F32)).astype(LOW)


def cut(start, size):
    return pl.ds(pl.multiple_of(start, 16), size)


class Links:
    def __init__(self, send, recv):
        self.send, self.recv = send, recv

    def start(self, kind, place, source, target, device_id):
        pltpu.make_async_remote_copy(
            src_ref=source,
            dst_ref=target,
            send_sem=self.send.at[kind],
            recv_sem=self.recv.at[kind, place],
            device_id=device_id,
            device_id_type=MESH,
        ).start()

    def arrived(self, kind, place, ref):
        pltpu.make_async_copy(ref, ref, self.recv.at[kind, place]).wait()

    def sent(self, kind, ref):
        pltpu.make_async_copy(ref, ref, self.send.at[kind]).wait()


def kernel(chips, experts, held, names, *refs):
    r = types.SimpleNamespace(**dict(zip(names, refs, strict=True)))
    positions, width = r.tokens.shape
    head = r.kv_weight.shape[1] // 2
    count = 2 * positions
    dp, device = lax.axis_index("dp"), lax.axis_index("expert")
    chip, core = device // 2, device % 2
    y, x = dp // 2, dp % 2
    place = [x, y]
    sibling = (dp, chip * 2 + 1 - core)
    beside = [(2 * y + 1 - x, device), (2 * (1 - y) + x, device)]
    dp_count = r.kv_grad_dp.shape[0]
    around = [(lax.rem(dp + k, dp_count), device) for k in range(1, dp_count)]

    def store(slot, source, target):
        if held:
            target[...] = source[...].astype(target.dtype)
        else:
            pltpu.make_async_copy(source, target, r.out_sem.at[slot]).start()
            stored.append((slot, source, target))

    stored = []

    def ahead(k):
        return (dp, lax.rem(chip + k, chips) * 2 + core)

    loads = {}
    for i, name in enumerate(LOADS):
        loads[name] = pltpu.make_async_copy(
            getattr(r, name + "_hbm"), getattr(r, name), r.load_sem.at[i]
        )
        loads[name].start()

    def loaded(*wanted):
        for name in wanted:
            loads[name].wait()

    barrier = pltpu.get_barrier_semaphore()
    for peer in [sibling] + around:
        pl.semaphore_signal(barrier, inc=1, device_id=peer, device_id_type=MESH)
    loop(
        chips - 1,
        lambda k: pl.semaphore_signal(
            barrier, inc=1, device_id=ahead(k + 1), device_id_type=MESH
        ),
    )

    loaded("tokens", "gain_one", "kv_weight", "segments")
    normed = (moments(r.tokens[...].astype(F32))[0] * r.gain_one[...]).astype(LOW)
    r.normed[...] = normed
    r.kv[0, :positions] = dot(normed, r.kv_weight[...], 1, 0).astype(LOW)
    segs = r.segments[...].astype(F32)
    lanes = 2 * head
    seg_rows = [segs[:, i * lanes : (i + 1) * lanes] for i in range(positions // lanes)]
    seg_rows.append(jnp.full((SEG_ROWS - len(seg_rows), lanes), 3.0, F32))
    r.kv[0, positions:] = jnp.concatenate(seg_rows, 0).astype(LOW)

    pl.semaphore_wait(barrier, chips + dp_count - 1)

    kv_links = Links(r.kv_send, r.kv_recv)

    parts = (slice(0, positions // 2), slice(positions // 2, positions + SEG_ROWS))

    def kv_copy(source, target, device_id, part):
        rows = parts[part]
        kv_links.start(0, 2 * target + part, r.kv.at[source, rows], r.kv.at[target, rows], device_id)

    def kv_copies(source, target, device_id):
        for part in range(2):
            kv_copy(source, target, device_id, part)

    def kv_arrived(slot, part):
        kv_links.arrived(0, 2 * slot + part, r.kv.at[slot, parts[part]])

    side, turn_of, same_side = chip % 2, chip // 2, chips // 2
    next_chip = (dp, (chip + 1 - 2 * side) * 2 + core)
    loop(same_side - 1, lambda s: kv_copies(0, 2 * (s + 1), ahead(2 * (s + 1))))
    kv_copies(0, 1, sibling)

    loaded("query_all", "ids", "keep", "router")
    ids = r.ids[...]
    kept = r.keep[...].astype(F32)
    queries = jnp.concatenate(
        pick(ids, dot(r.query_all[...], r.normed[...], 1, 1), experts, head), 1
    )
    queries = queries.astype(LOW).astype(F32) * SCALE
    seg_twice = jnp.concatenate([segs, segs], 1)
    others = [jnp.where(seg_twice == s, 0.0, NEGATIVE) for s in range(3)]
    blank = jnp.zeros((head, count), F32)
    r.q_aug[0 : 2 * head] = jnp.concatenate([queries, blank], 0).astype(LOW)
    r.q_aug[2 * head :] = jnp.concatenate(
        others + [jnp.zeros((2 * head - 3, count), F32)], 0
    ).astype(LOW)
    r.q_rows[0:count] = jnp.concatenate([queries, blank], 0).T.astype(LOW)
    logits = dot(r.router[...], r.normed[...], 1, 1)
    places = lax.broadcasted_iota(jnp.int32, logits.shape, 0)
    onehots = [(places == ids[c : c + 1]).astype(F32) for c in range(2)]
    chosen = [jnp.sum(onehots[c] * logits, 0, keepdims=True) for c in range(2)]
    top = jnp.maximum(chosen[0], chosen[1])
    expo = [jnp.exp(chosen[c] - top) for c in range(2)]
    r.soft[...] = jnp.concatenate([e / (expo[0] + expo[1]) for e in expo], 0)
    r.gates[...] = r.soft[...] * kept

    kv_copies(0, 2 * same_side, next_chip)
    r.peak[...] = jnp.full(r.peak.shape, -3e38, F32)
    r.total[...] = jnp.zeros(r.total.shape, F32)

    def key_block(slot):
        block = r.kv[slot, :positions]
        seg = r.kv[slot, positions:].astype(F32)
        first = jnp.sum(jnp.where(seg < 0.5, 1.0, 0.0), keepdims=True)
        second = jnp.sum(jnp.where(seg < 1.5, 1.0, 0.0), keepdims=True)
        row = lax.broadcasted_iota(jnp.int32, (positions, lanes), 0).astype(F32)
        lane = lax.broadcasted_iota(jnp.int32, (positions, lanes), 1)
        segment = jnp.where(row < first, 0, jnp.where(row < second, 1, 2))
        extra = jnp.where((segment == lane) | ((lane >= 3) & (lane < 6)), 1.0, 0.0)
        return block, jnp.concatenate([block, extra.astype(LOW)], 1)

    def attend(slot):
        block, keys = key_block(slot)
        values_t = jnp.concatenate([jnp.ones((16, positions), LOW), block.T[head:]], 0)
        scores = dot(keys, r.q_aug[...], 1, 0)
        old = r.peak[...]
        new = jnp.maximum(old, jnp.max(scores, 0, keepdims=True))
        probs = jnp.exp(scores - new).astype(LOW)
        r.total[...] = r.total[...] * jnp.exp(old - new) + dot(values_t, probs, 1, 0)
        r.peak[...] = new

    def attend_chip(j):
        for part in range(2):

            @pl.when(j > 0)
            def _():
                kv_arrived(2 * j, part)
                kv_copy(2 * j, 2 * j + 1, sibling, part)

            @pl.when((j > 0) & (j < same_side))
            def _():
                kv_copy(2 * j, 2 * (same_side + j), next_chip, part)

        attend(2 * j)
        for part in range(2):
            kv_arrived(2 * j + 1, part)
        attend(2 * j + 1)

    loop(chips, attend_chip)

    weight = r.total[0:1]
    attended = r.total[16:] / weight
    log_total = r.peak[...] + jnp.log(weight)
    r.total[16:] = attended
    r.peak[...] = log_total
    halves = [attended[:, :positions], attended[:, positions:]]
    gates = r.gates[...]
    r.gated[...] = spread(ids, [halves[c] * gates[c : c + 1] for c in range(2)], experts)
    loaded("out_all", "gain_two")
    mixed = r.tokens[...].astype(F32) + dot(r.gated[...], r.out_all[...], 0, 0)
    r.mixed[...] = mixed
    hidden = (moments(mixed)[0] * r.gain_two[...]).astype(LOW)
    r.hidden[...] = hidden
    r.hidden_t[...] = hidden.T

    groups, line_rows = r.line_sum.shape[:2]
    each = CHUNKS // groups
    share = line_rows // chips
    half, quarter, eighth = width // 2, width // 4, width // 8
    halving = Links(r.halving_send, r.halving_recv)
    line = Links(r.line_send, r.line_recv)

    PAIR, NEAR, FAR, FAR_BACK, NEAR_BACK, PAIR_BACK = range(6)
    LINE, LINE_BACK = range(2)

    def both_of(c):
        return pl.ds(2 * c, 2)

    def stage_0(c):
        for w in range(2):
            b = 2 * c + w
            source = r.own.at[b, cut((1 - core) * half, half)]
            halving.start(PAIR, c, source, r.pair_in.at[b], sibling)

    def stage_1(c):
        halving.arrived(PAIR, c, r.pair_in.at[both_of(c)])
        for w in range(2):
            b = 2 * c + w
            at = cut(core * half, half)
            r.own[b, at] = low_sum(r.own[b, at], r.pair_in[b])
            source = r.own.at[b, cut(core * half + (1 - place[w]) * quarter, quarter)]
            halving.start(NEAR, c, source, r.near_in.at[b], beside[w])

    def stage_2(c):
        halving.arrived(NEAR, c, r.near_in.at[both_of(c)])
        for w in range(2):
            b = 2 * c + w
            at = cut(core * half + place[w] * quarter, quarter)
            r.own[b, at] = low_sum(r.own[b, at], r.near_in[b])
            to = core * half + place[w] * quarter + (1 - place[1 - w]) * eighth
            source = r.own.at[b, cut(to, eighth)]
            halving.start(FAR, c, source, r.far_in.at[b], beside[1 - w])

    def stage_3(c):
        g = c // each
        halving.arrived(FAR, c, r.far_in.at[both_of(c)])
        for w in range(2):
            b = 2 * c + w
            at = cut(core * half + place[w] * quarter + place[1 - w] * eighth, eighth)
            to = (c % each * 2 + w) * eighth
            r.line_sum[g, to : to + eighth] = low_sum(r.own[b, at], r.far_in[b])
        if c % each == each - 1:

            def send_share(k):
                source = r.line_sum.at[g, cut(lax.rem(chip + k + 1, chips) * share, share)]
                line.start(LINE, g, source, r.line_in.at[g, k], ahead(k + 1))

            loop(chips - 1, send_share)

    def at_group_end(body):
        def stage(c):
            if c % each == each - 1:
                body(c // each)

        return stage

    my_share = cut(chip * share, share)

    @at_group_end
    def stage_4(g):
        line.arrived(LINE, g, r.line_in.at[g])

        def add_line(k, sum_so_far):
            return sum_so_far + r.line_in[g, k].astype(F32)

        summed = lax.fori_loop(0, chips - 1, add_line, r.line_sum[g, my_share].astype(F32))
        r.line_whole[g, my_share] = summed.astype(LOW)
        ref = r.line_whole.at[g, my_share]
        loop(chips - 1, lambda k: line.start(LINE_BACK, g, ref, ref, ahead(k + 1)))

    def blocks_of(g):
        for i in range(2 * each):
            yield i, i % 2, g * 2 * each + i

    def group_at(g):
        return pl.ds(g * 2 * each, 2 * each)

    @at_group_end
    def stage_5(g):
        line.arrived(LINE_BACK, g, r.line_in.at[g])
        for i, w, b in blocks_of(g):
            at = cut(core * half + place[w] * quarter + place[1 - w] * eighth, eighth)
            r.whole[b, at] = r.line_whole[g, i * eighth : (i + 1) * eighth]
            source = r.line_whole.at[g, i * eighth : (i + 1) * eighth]
            halving.start(FAR_BACK, g, source, r.whole.at[b, at], beside[1 - w])

    @at_group_end
    def stage_6(g):
        halving.arrived(FAR_BACK, g, r.far_in.at[group_at(g)])
        for i, w, b in blocks_of(g):
            ref = r.whole.at[b, cut(core * half + place[w] * quarter, quarter)]
            halving.start(NEAR_BACK, g, ref, ref, beside[w])

    @at_group_end
    def stage_7(g):
        halving.arrived(NEAR_BACK, g, r.near_in.at[group_at(g)])
        for i, w, b in blocks_of(g):
            ref = r.whole.at[b, cut(core * half, half)]
            halving.start(PAIR_BACK, g, ref, ref, sibling)

    @at_group_end
    def stage_8(g):
        halving.arrived(PAIR_BACK, g, r.pair_in.at[group_at(g)])
        for i, w, b in blocks_of(g):
            if held:
                r.big_out[b] = r.whole[b].astype(F32)
            else:
                pltpu.make_async_copy(r.whole.at[b], r.big_out.at[b], r.store_sem.at[0]).start()

    def big_sent():
        for kind in (PAIR, PAIR_BACK):
            halving.sent(kind, r.pair_in)
        for kind in (NEAR, NEAR_BACK):
            halving.sent(kind, r.near_in)
        for kind in (FAR, FAR_BACK):
            halving.sent(kind, r.far_in)
        for kind in (LINE, LINE_BACK):
            line.sent(kind, r.line_in)
        if not held:
            pltpu.make_async_copy(r.whole, r.big_out, r.store_sem.at[0]).wait()

    few = experts // 2
    my_experts = pl.ds(core * few, few)
    fine = width // chips % 128 == 0
    expert_links = Links(r.expert_send, r.expert_recv)
    EXPERT_PAIR, EXPERT_NEAR, EXPERT_FAR, EXPERT_LINE, EXPERT_LAST = range(5)

    def expert_half(a, first, second):
        if a == 0:
            if second is None:
                return (a, my_experts, first)
            return (a, my_experts, first, second)
        if second is None:
            return (a, my_experts, slice(None), first)
        return (a, my_experts, second, first)

    order = [(y, x), (x, y)]
    sides = [(beside[1], beside[0]), (beside[0], beside[1])]

    def expert_columns(c):
        return pl.ds(pl.multiple_of(c * (width // chips), 128), width // chips)

    def expert_0(a):
        source = r.expert_own.at[a, pl.ds((1 - core) * few, few)]
        expert_links.start(EXPERT_PAIR, a, source, r.expert_pair.at[a], sibling)

    def expert_1(a):
        expert_links.arrived(EXPERT_PAIR, a, r.expert_pair.at[a])
        r.expert_own[a, my_experts] = low_sum(r.expert_own[a, my_experts], r.expert_pair[a])
        source = r.expert_own.at[expert_half(a, 1 - order[a][0], None)]
        expert_links.start(EXPERT_NEAR, a, source, r.expert_near.at[a], sides[a][0])

    def expert_2(a):
        expert_links.arrived(EXPERT_NEAR, a, r.expert_near.at[a])
        at = expert_half(a, order[a][0], None)
        r.expert_own[at] = low_sum(r.expert_own[at], r.expert_near[a])
        source = r.expert_own.at[expert_half(a, order[a][0], 1 - order[a][1])]
        expert_links.start(EXPERT_FAR, a, source, r.expert_far.at[a], sides[a][1])

    def expert_3(a):
        expert_links.arrived(EXPERT_FAR, a, r.expert_far.at[a])
        at = expert_half(a, *order[a])
        r.expert_quarter[a] = low_sum(r.expert_own[at], r.expert_far[a])

        def send_columns(k):
            source = r.expert_quarter.at[a, :, :, expert_columns(lax.rem(chip + k + 1, chips))]
            expert_links.start(EXPERT_LINE, a, source, r.expert_line.at[a, k], ahead(k + 1))

        if fine:
            loop(chips - 1, send_columns)

    def expert_4(a):
        if not fine:
            return
        expert_links.arrived(EXPERT_LINE, a, r.expert_line.at[a])

        def add_line(k, sum_so_far):
            return sum_so_far + r.expert_line[a, k].astype(F32)

        own_part = r.expert_quarter[a, :, :, expert_columns(chip)].astype(F32)
        r.expert_last[a, 0] = lax.fori_loop(0, chips - 1, add_line, own_part).astype(LOW)
        source, target = r.expert_last.at[a, 0], r.expert_last.at[a, 1]
        expert_links.start(EXPERT_LAST, a, source, target, sibling)

    def expert_5(a):
        if fine:
            expert_links.arrived(EXPERT_LAST, a, r.expert_last.at[a, 1])
            part = width // chips // 2
            mine = r.expert_last[a, 0].astype(F32)
            other = r.expert_last[a, 1].astype(F32)
            for i in range(2):
                rows = jnp.where(core == i, mine, other)
                r.expert_out[a, i * few : (i + 1) * few] = jnp.where(
                    core == 0, rows[:, :, :part], rows[:, :, part:]
                )
        else:
            r.expert_out[a] = r.expert_quarter[a]
        store(a, r.expert_out.at[a], r.experts_out.at[a])

    def expert_sent():
        expert_links.sent(EXPERT_PAIR, r.expert_pair)
        expert_links.sent(EXPERT_NEAR, r.expert_near)
        expert_links.sent(EXPERT_FAR, r.expert_far)
        if fine:
            expert_links.sent(EXPERT_LINE, r.expert_line)
            expert_links.sent(EXPERT_LAST, r.expert_last.at[:, 0])

    late = Links(r.late_send, r.late_recv)
    KV_PAIR, KV_DP, KV_LINE, KV_DP_BACK, KV_PAIR_BACK, VEC_PAIR, VEC_DP, VEC_LINE = range(8)
    kv_half = width // 2
    kv_part = kv_half // dp_count
    others_dp = range(1, dp_count)
    kv_mine = cut(core * kv_half, kv_half)
    kv_share = cut(core * kv_half + dp * kv_part, kv_part)

    def kv_0():
        source = r.kv_grad.at[cut((1 - core) * kv_half, kv_half)]
        late.start(KV_PAIR, 0, source, r.kv_grad_pair, sibling)

    def kv_1():
        late.arrived(KV_PAIR, 0, r.kv_grad_pair)
        r.kv_grad[kv_mine] = low_sum(r.kv_grad[kv_mine], r.kv_grad_pair[...])
        for k in others_dp:
            at = cut(core * kv_half + lax.rem(dp + k, dp_count) * kv_part, kv_part)
            late.start(KV_DP, 0, r.kv_grad.at[at], r.kv_grad_dp.at[k], around[k - 1])

    def to_line(kind, buffer, value):
        buffer[chip] = value.astype(LOW)
        ref = buffer.at[chip]
        loop(chips - 1, lambda k: late.start(kind, 0, ref, ref, ahead(k + 1)))

    def from_line(kind, buffer):
        late.arrived(kind, 0, buffer.at[1:])

        def add(k, sum_so_far):
            return sum_so_far + buffer[k].astype(F32)

        return lax.fori_loop(1, chips, add, buffer[0].astype(F32))

    def kv_2():
        late.arrived(KV_DP, 0, r.kv_grad_dp.at[1:])
        summed = r.kv_grad[kv_share].astype(F32)
        for k in others_dp:
            summed = summed + r.kv_grad_dp[k].astype(F32)
        to_line(KV_LINE, r.kv_grad_line, summed)

    def kv_3():
        r.kv_grad_whole[kv_share] = from_line(KV_LINE, r.kv_grad_line).astype(LOW)
        ref = r.kv_grad_whole.at[kv_share]
        for k in others_dp:
            late.start(KV_DP_BACK, 0, ref, ref, around[k - 1])

    def kv_4():
        late.arrived(KV_DP_BACK, 0, r.kv_grad_dp.at[1:])
        ref = r.kv_grad_whole.at[kv_mine]
        late.start(KV_PAIR_BACK, 0, ref, ref, sibling)

    def kv_5():
        late.arrived(KV_PAIR_BACK, 0, r.kv_grad_pair)
        store(2, r.kv_grad_whole, r.kv_out_whole)

    def vectors_0():
        late.start(VEC_PAIR, 0, r.vectors, r.vectors_pair, sibling)

    def vectors_1():
        late.arrived(VEC_PAIR, 0, r.vectors_pair)
        r.vectors_dp[dp] = low_sum(r.vectors[...], r.vectors_pair[...])
        ref = r.vectors_dp.at[dp]
        for k in others_dp:
            late.start(VEC_DP, 0, ref, ref, around[k - 1])

    def vectors_2():
        late.arrived(VEC_DP, 0, r.vectors_dp.at[1:])
        summed = r.vectors_dp[0].astype(F32)
        for k in others_dp:
            summed = summed + r.vectors_dp[k].astype(F32)
        to_line(VEC_LINE, r.vectors_line, summed)

    def vectors_3():
        r.vectors_whole[...] = from_line(VEC_LINE, r.vectors_line)
        store(3, r.vectors_whole, r.vectors_out)

    def late_sent():
        late.sent(KV_PAIR, r.kv_grad_pair)
        late.sent(KV_PAIR_BACK, r.kv_grad_pair)
        late.sent(VEC_PAIR, r.vectors_pair)
        late.sent(KV_DP, r.kv_grad_dp.at[1:])
        late.sent(KV_DP_BACK, r.kv_grad_dp.at[1:])
        late.sent(VEC_DP, r.vectors_dp.at[1:])
        late.sent(KV_LINE, r.kv_grad_line.at[1:])
        late.sent(VEC_LINE, r.vectors_line.at[1:])

    stages = {
        "e1": expert_1,
        "e2": expert_2,
        "e3": expert_3,
        "e4": expert_4,
        "e5": expert_5,
        "k1": kv_1,
        "k2": kv_2,
        "k3": kv_3,
        "k4": kv_4,
        "k5": kv_5,
        "v1": vectors_1,
        "v2": vectors_2,
        "v3": vectors_3,
    }
    for i, stage in enumerate(
        [stage_1, stage_2, stage_3, stage_4, stage_5, stage_6, stage_7, stage_8]
    ):
        stages[i + 1] = stage

    def do(event):
        stages[event[0]](*event[1:])

    def do_all(events):
        for event in events:
            do(event)

    def service(plan, turn):
        for at, events in enumerate(plan):
            if events:
                pl.when(turn == at)(functools.partial(do_all, events))

    loaded("up", "cot", "down")
    chunk = r.own.shape[2]

    def layer_output():
        out = r.mixed[...] + dot(r.act[...], r.down[...], 1, 0)
        r.layer_low[...] = out.astype(LOW)
        store(4, r.layer_low, r.layer_out)

    stages["o"] = layer_output

    def units_of(c):
        return pl.ds(pl.multiple_of(c * chunk, chunk), chunk)

    def feed(c):
        units = units_of(c)
        value, slope = gelu_both(dot(r.hidden[...], r.up[:, units], 1, 0))
        r.act[:, units] = value.astype(LOW)
        r.grad_pre[:, units] = (dot(r.cot[...], r.down[units], 1, 1) * slope).astype(LOW)

    def weigh(c):
        units = units_of(c)
        r.own[2 * c] = dot(r.hidden_t[...], r.grad_pre[:, units], 1, 0).astype(LOW)
        down_grad = dot(r.act[:, units], r.cot[...], 0, 0).astype(LOW)
        for i in range(width // chunk):
            at = slice(i * chunk, (i + 1) * chunk)
            r.own[2 * c + 1, at] = down_grad[:, at]

    def feed_next(c):
        weigh(c)
        feed(c + 1)
        stage_0(c)
        service(FEED_PLAN, c)

    feed(0)
    loop(CHUNKS - 1, feed_next)
    weigh(CHUNKS - 1)
    stage_0(CHUNKS - 1)
    for event in FEED_PLAN[CHUNKS - 1]:
        do(event)

    hat, scale = moments(r.mixed[...])
    grad = dot(r.grad_pre[...], r.up[...], 1, 1)
    grad, gain = norm_back(hat, scale, r.gain_two[...], grad)
    grad = grad + r.cot[...].astype(F32)
    r.grad_mixed[...] = grad
    r.grad_mixed_low[...] = grad.astype(LOW)
    r.gain_grad[...] = gain
    for event in MIX_PLAN:
        do(event)

    r.q_aug[2 * head :] = jnp.concatenate(
        others + thirds(-r.peak[...]) + [jnp.zeros((2 * head - 6, count), F32)], 0
    ).astype(LOW)
    shown = pick(ids, dot(r.out_all[...], r.grad_mixed_low[...], 1, 1), experts, head)
    expert_shape = r.expert_own.shape[1:]
    r.expert_own[0] = dot(r.gated[...], r.grad_mixed_low[...], 1, 0).astype(LOW).reshape(expert_shape)
    expert_0(0)
    attended = r.total[16:]
    grad_gates = [
        jnp.sum(shown[c] * attended[:, c * positions : (c + 1) * positions], 0, keepdims=True)
        for c in range(2)
    ]
    gates = r.gates[...]
    soft = [r.soft[c : c + 1] for c in range(2)]
    kept_grad = [grad_gates[c] * kept[c : c + 1] for c in range(2)]
    inner = soft[0] * kept_grad[0] + soft[1] * kept_grad[1]
    grad_logits = onehots[0] * (soft[0] * (kept_grad[0] - inner)) + onehots[1] * (
        soft[1] * (kept_grad[1] - inner)
    )
    r.grad_logits[...] = jnp.concatenate(thirds(grad_logits), 0).astype(LOW)
    in_thirds = dot(r.grad_logits[...], r.normed[...], 1, 0)
    r.router_grad[...] = (
        in_thirds[:experts] + in_thirds[experts : 2 * experts] + in_thirds[2 * experts :]
    )
    delta = jnp.concatenate([gates[c : c + 1] * grad_gates[c] for c in range(2)], 1)
    grad_attended = jnp.concatenate([gates[c : c + 1] * shown[c] for c in range(2)], 1)
    stacked = jnp.concatenate([blank, grad_attended], 0)
    r.o_aug[0 : 2 * head] = stacked.astype(LOW)
    r.o_aug[2 * head :] = jnp.concatenate(
        [jnp.zeros((3, count), F32)] + thirds(-delta) + [jnp.zeros((2 * head - 6, count), F32)], 0
    ).astype(LOW)
    r.q_rows[count:] = stacked.T.astype(LOW)
    for event in GATE_PLAN:
        do(event)

    r.grad_q[...] = jnp.zeros(r.grad_q.shape, F32)
    back_links = Links(r.back_send, r.back_recv)
    BACK_PAIR, BACK_NEXT, BACK_LINE = range(3)
    span = count // SPANS

    def target_chip(step):
        back = lax.rem(step + 1, same_side)
        return back, back + jnp.where(step < same_side, same_side, 0)

    def back_keys(k):
        for i in range(2):
            at = slice(i * positions, (i + 1) * positions)
            block, keys = key_block(2 * k + i)
            r.keys[at] = keys
            r.keys_t[:, at] = block.T[:head]

    def back_pair(step):
        back, _ = target_chip(step)
        back_links.arrived(BACK_PAIR, step, r.kv_pair.at[step])
        both = r.part[lax.rem(step, 2), :positions] + r.kv_pair[step].astype(F32)
        r.kv_pair[step] = both.astype(LOW)

        @pl.when(step < same_side)
        def _():
            back_links.start(BACK_NEXT, back, r.kv_pair.at[step], r.kv_next.at[back], next_chip)

        @pl.when(step == chips - 1)
        def _():
            r.kv_own[...] = both

    def back_line():
        def send(s):
            back, step = s + 1, same_side + s
            back_links.arrived(BACK_NEXT, back, r.kv_next.at[back])
            r.kv_pair[step] = low_sum(r.kv_pair[step], r.kv_next[back])
            target = (dp, lax.rem(chip + chips - 2 * back, chips) * 2 + core)
            back_links.start(BACK_LINE, 0, r.kv_pair.at[step], r.kv_line.at[s], target)

        loop(same_side - 1, send)

    stages["x"] = lambda: back_pair(chips - 1)
    stages["r"] = back_line

    def spans_of(turn):
        at = lax.rem(turn, SPANS) * span
        return pl.ds(pl.multiple_of(at, span), span), pl.ds(pl.multiple_of(count + at, span), span)

    def weights_of(turn):
        at, _ = spans_of(turn)
        keys = r.keys[...]
        probs = jnp.exp(dot(keys, r.q_aug[:, at], 1, 0))
        grads = (probs * dot(keys, r.o_aug[:, at], 1, 0)).astype(LOW)
        return probs.astype(LOW), grads

    def sums_of(turn):
        at, also = spans_of(turn)
        now = lax.rem(turn // SPANS, 2)
        probs, grads = r.probs[...], r.grads[...]
        r.grad_q[:, at] = r.grad_q[:, at] + dot(r.keys_t[now], grads, 1, 0)
        r.part[now] = (
            r.part[now] + dot(grads, r.q_rows[at], 1, 0) + dot(probs, r.q_rows[also], 1, 0)
        )

    def start_step(step):
        _, k = target_chip(step)
        now = lax.rem(step, 2)
        for i in range(2):
            at = slice(i * positions, (i + 1) * positions)
            block, keys = key_block(2 * k + i)
            r.keys[at] = keys
            r.keys_t[now, :, at] = block.T[:head]
        r.part[now] = jnp.zeros(r.part.shape[1:], F32)

    def end_step(step):
        r.kv_out[step] = r.part[lax.rem(step, 2), positions:].astype(LOW)
        back_links.start(BACK_PAIR, step, r.kv_out.at[step], r.kv_pair.at[step], sibling)

    def back_turn(i):
        turn = i + 1
        step, at_span = turn // SPANS, lax.rem(turn, SPANS)
        pl.when(at_span == 0)(functools.partial(start_step, step))
        sums_of(turn - 1)
        r.probs[...], r.grads[...] = weights_of(turn)
        pl.when(at_span == 0)(functools.partial(end_step, step - 1))
        pl.when((at_span == 1) & (step > 0))(functools.partial(back_pair, step - 1))
        service(block_plan, turn)

    block_plan, line_first = BLOCK_PLAN, False
    if chips != 4:
        line_first = any(("r",) in events for events in BLOCK_PLAN)
        block_plan = [[event for event in events if event != ("r",)] for events in BLOCK_PLAN]
    turns = SPANS * chips
    start_step(0)
    r.probs[...], r.grads[...] = weights_of(0)
    for event in block_plan[0]:
        do(event)
    loop(turns - 1, back_turn)
    sums_of(turns - 1)
    end_step(chips - 1)
    for events in block_plan[min(turns, len(block_plan) - 1) :]:
        for event in events:
            do(event)

    def query_grads():
        grad_queries = r.grad_q[...] * SCALE
        r.grad_spread[...] = spread(
            ids, [grad_queries[:, :positions], grad_queries[:, positions:]], experts
        )
        grads = dot(r.grad_spread[...], r.normed[...], 1, 0).astype(LOW)
        r.expert_own[1] = grads.reshape(expert_shape)
        expert_0(1)

    def token_sum():
        routers = jnp.concatenate([r.router[...].astype(F32)] * 3, 0).astype(LOW)
        r.grad_normed[...] = dot(r.grad_spread[...], r.query_all[...], 0, 0) + dot(
            r.grad_logits[...], routers, 0, 0
        )

    def kv_grads():
        back_links.arrived(BACK_NEXT, 0, r.kv_next.at[0])
        if same_side > 1:
            back_links.arrived(BACK_LINE, 0, r.kv_line)

        def add_in(k, sum_so_far):
            return sum_so_far + r.kv_line[k].astype(F32)

        summed = r.kv_own[...] + r.kv_next[0].astype(F32)
        grad_kv = lax.fori_loop(0, same_side - 1, add_in, summed).astype(LOW)
        r.kv_grad_own[...] = grad_kv
        r.kv_grad[...] = dot(r.normed[...], grad_kv, 0, 0).astype(LOW)
        kv_0()

    def token_grads():
        grad = r.grad_normed[...] + dot(r.kv_grad_own[...], r.kv_weight[...], 1, 1)
        hat, scale = moments(r.tokens[...].astype(F32))
        grad, gain = norm_back(hat, scale, r.gain_one[...], grad)
        rest = jnp.zeros((r.vectors.shape[0] - experts - 2, width), F32)
        r.vectors[...] = jnp.concatenate(
            [r.router_grad[...], gain, r.gain_grad[...], rest], 0
        ).astype(LOW)
        vectors_0()
        r.grad_mixed[...] = grad + r.grad_mixed[...]
        store(5, r.grad_mixed, r.tokens_out)

    stages.update(q=query_grads, u=token_sum, k=kv_grads, t=token_grads)
    for event in TAIL_PLAN:
        do(event)
        if event == ("x",) and line_first:
            back_line()

    big_sent()
    expert_sent()
    late_sent()
    for slot, source, target in stored:
        pltpu.make_async_copy(source, target, r.out_sem.at[slot]).wait()
    kv_links.sent(0, r.kv.at[1:])
    back_links.sent(BACK_PAIR, r.kv_out)
    back_links.sent(BACK_NEXT, r.kv_next)
    if same_side > 1:
        back_links.sent(BACK_LINE, r.kv_line)


LOADS = (
    "tokens",
    "gain_one",
    "kv_weight",
    "segments",
    "query_all",
    "ids",
    "keep",
    "router",
    "out_all",
    "gain_two",
    "up",
    "cot",
    "down",
)


def finish(names, held, *refs):
    r = types.SimpleNamespace(**dict(zip(names, refs, strict=True)))
    blocks, width, chunk = r.big_out.shape
    experts = r.grad_router.shape[0]
    sources = [r.layer_out, r.tokens_out, r.vectors_out, r.kv_out_whole]
    started = []

    def store(source, target):
        copy = pltpu.make_async_copy(source, target, r.store_sem.at[len(started)])
        copy.start()
        started.append(copy)

    def store_block(b, source):
        c = b // 2
        at = slice(c * chunk, (c + 1) * chunk)
        if b % 2 == 0:
            pltpu.make_async_copy(source, r.grad_up.at[:, at], r.block_sem.at[0]).start()
            return
        for i in range(width // chunk):
            part = slice(i * chunk, (i + 1) * chunk)
            target = r.grad_down.at[at, part]
            pltpu.make_async_copy(source.at[part], target, r.block_sem.at[0]).start()

    if held:
        for b in range(blocks):
            store_block(b, r.big_out.at[b])
        layer, tokens, vectors, kv = sources
        full = r.big_out
    else:
        loads = [
            pltpu.make_async_copy(r.big_out.at[b], r.big_low.at[b], r.load_sem.at[b])
            for b in range(blocks)
        ]
        arrays = [r.layer_held, r.tokens_held, r.vectors_held, r.kv_held]
        small = [
            pltpu.make_async_copy(a, b, r.small_sem.at[i])
            for i, (a, b) in enumerate(zip(sources, arrays, strict=True))
        ]
        for load in loads + small:
            load.start()
        for b in range(blocks):
            loads[b].wait()
            r.big_full[b] = r.big_low[b].astype(F32)
            store_block(b, r.big_full.at[b])
        for load in small:
            load.wait()
        r.kv_full[...] = r.kv_held[...].astype(F32)
        layer, tokens, vectors, kv = arrays[:3] + [r.kv_full]
        full = r.big_full
    store(layer, r.layer)
    store(tokens, r.grad_tokens)
    store(kv, r.grad_kv_weight)
    store(vectors.at[0:experts], r.grad_router)
    store(vectors.at[experts : experts + 1], r.grad_gain_one)
    store(vectors.at[experts + 1 : experts + 2], r.grad_gain_two)
    if held:
        store(r.experts_out.at[0], r.grad_out)
        store(r.experts_out.at[1], r.grad_query)
    for copy in started:
        copy.wait()
    pltpu.make_async_copy(full, full, r.block_sem.at[0]).wait()


def shards(
    tokens,
    segments,
    expert_ids,
    keep,
    gain_one,
    kv_weight,
    router_weight,
    query_weight,
    out_weight,
    gain_two,
    up_weight,
    down_weight,
    cotangent,
):
    positions, width = tokens.shape[1:]
    experts, _, head = query_weight.shape
    hidden_units = up_weight.shape[1]
    dps, chips = lax.axis_size("dp"), lax.axis_size("expert") // 2
    chunk = hidden_units // CHUNKS
    blocks = 2 * CHUNKS
    groups = max(1, min(CHUNKS, blocks * (width // 8) // (16 * chips)))
    line_rows = blocks * (width // 8) // groups
    count = 2 * positions
    few = experts // 2
    fine = width // chips % 128 == 0
    part = width // chips if fine else 128
    rows = 2 * experts

    inputs = dict(
        tokens=tokens[0],
        gain_one=gain_one[None],
        kv_weight=kv_weight,
        segments=segments,
        query_all=jnp.swapaxes(query_weight, 1, 2).reshape(experts * head, width),
        ids=expert_ids[0].T,
        keep=keep[0].T,
        router=router_weight.T,
        out_all=jnp.swapaxes(out_weight, 1, 2).reshape(experts * head, width),
        gain_two=gain_two[None],
        up=up_weight,
        cot=cotangent[0],
        down=down_weight,
    )
    inputs = {name: inputs[name] for name in LOADS}
    hbm = pl.BlockSpec(memory_space=pl.ANY)

    def struct(*shape_and_type):
        return jax.ShapeDtypeStruct(shape_and_type[:-1], shape_and_type[-1])

    def vmem(*shape_and_type):
        return pltpu.VMEM(shape_and_type[:-1], shape_and_type[-1])

    def dma(*shape):
        return pltpu.SemaphoreType.DMA(shape)

    expert_out = (few, head // 4, width, LOW)
    if fine:
        expert_out = (experts, head // 4, part // 2, F32)
    held = fine
    outputs = dict(
        layer_out=(positions, width, LOW),
        tokens_out=(positions, width, F32),
        kv_out_whole=(width, 2 * head, F32 if held else LOW),
        vectors_out=(rows, width, F32),
        experts_out=(2, *expert_out),
        big_out=(blocks, width, chunk, F32 if held else LOW),
    )
    between = vmem if held else struct
    outputs = {name: between(*value) for name, value in outputs.items()}
    vmem_spec = pl.BlockSpec(memory_space=pltpu.VMEM)
    passed = vmem_spec if held else hbm
    scratch = {name: vmem(*value.shape, value.dtype) for name, value in inputs.items()}
    scratch.update(
        normed=vmem(positions, width, LOW),
        kv=vmem(2 * chips, positions + SEG_ROWS, 2 * head, LOW),
        q_aug=vmem(4 * head, count, LOW),
        o_aug=vmem(4 * head, count, LOW),
        q_rows=vmem(2 * count, 2 * head, LOW),
        peak=vmem(1, count, F32),
        total=vmem(16 + head, count, F32),
        gates=vmem(2, positions, F32),
        soft=vmem(2, positions, F32),
        gated=vmem(experts * head, positions, LOW),
        mixed=vmem(positions, width, F32),
        hidden=vmem(positions, width, LOW),
        hidden_t=vmem(width, positions, LOW),
        act=vmem(positions, hidden_units, LOW),
        grad_pre=vmem(positions, hidden_units, LOW),
        layer_low=vmem(positions, width, LOW),
        grad_normed=vmem(positions, width, F32),
        grad_mixed=vmem(positions, width, F32),
        grad_mixed_low=vmem(positions, width, LOW),
        grad_logits=vmem(3 * experts, positions, LOW),
        router_grad=vmem(experts, width, F32),
        gain_grad=vmem(1, width, F32),
        grad_q=vmem(head, count, F32),
        kv_pair=vmem(chips, positions, 2 * head, LOW),
        kv_out=vmem(chips, positions, 2 * head, LOW),
        kv_next=vmem(max(1, chips // 2), positions, 2 * head, LOW),
        kv_line=vmem(max(1, chips // 2 - 1), positions, 2 * head, LOW),
        part=vmem(2, 2 * positions, 2 * head, F32),
        keys=vmem(2 * positions, 4 * head, LOW),
        keys_t=vmem(2, head, 2 * positions, LOW),
        probs=vmem(2 * positions, count // SPANS, LOW),
        grads=vmem(2 * positions, count // SPANS, LOW),
        kv_grad_own=vmem(positions, 2 * head, LOW),
        kv_own=vmem(positions, 2 * head, F32),
        grad_spread=vmem(experts * head, positions, LOW),
        expert_own=vmem(2, experts, 2, 2, head // 4, width, LOW),
        expert_pair=vmem(2, few, 2, 2, head // 4, width, LOW),
        expert_near=vmem(2, few, 2, head // 4, width, LOW),
        expert_far=vmem(2, few, head // 4, width, LOW),
        expert_quarter=vmem(2, few, head // 4, width, LOW),
        expert_line=vmem(2, chips - 1 if fine else 1, few, head // 4, part, LOW),
        expert_last=vmem(2, 2, few, head // 4, part, LOW),
        expert_out=vmem(2, *expert_out),
        kv_grad=vmem(width, 2 * head, LOW),
        kv_grad_pair=vmem(width // 2, 2 * head, LOW),
        kv_grad_dp=vmem(dps, width // 2 // dps, 2 * head, LOW),
        kv_grad_line=vmem(chips, width // 2 // dps, 2 * head, LOW),
        kv_grad_whole=vmem(width, 2 * head, LOW),
        vectors=vmem(rows, width, LOW),
        vectors_pair=vmem(rows, width, LOW),
        vectors_dp=vmem(dps, rows, width, LOW),
        vectors_line=vmem(chips, rows, width, LOW),
        vectors_whole=vmem(rows, width, F32),
        own=vmem(blocks, width, chunk, LOW),
        whole=vmem(blocks, width, chunk, LOW),
        pair_in=vmem(blocks, width // 2, chunk, LOW),
        near_in=vmem(blocks, width // 4, chunk, LOW),
        far_in=vmem(blocks, width // 8, chunk, LOW),
        line_sum=vmem(groups, line_rows, chunk, LOW),
        line_in=vmem(groups, chips - 1, line_rows // chips, chunk, LOW),
        line_whole=vmem(groups, line_rows, chunk, LOW),
        load_sem=dma(len(LOADS)),
        out_sem=dma(6),
        store_sem=dma(1),
        kv_send=dma(1),
        kv_recv=dma(1, 4 * chips),
        back_send=dma(3),
        back_recv=dma(3, chips),
        halving_send=dma(6),
        halving_recv=dma(6, CHUNKS),
        line_send=dma(2),
        line_recv=dma(2, groups),
        expert_send=dma(5),
        expert_recv=dma(5, 2),
        late_send=dma(8),
        late_recv=dma(8, 1),
    )
    names = [name + "_hbm" for name in LOADS] + list(outputs) + list(scratch)
    reduced = pl.pallas_call(
        functools.partial(kernel, chips, experts, held, names),
        out_shape=tuple(outputs.values()),
        in_specs=[hbm] * len(LOADS),
        out_specs=(passed,) * len(outputs),
        scratch_shapes=list(scratch.values()),
        compiler_params=pltpu.CompilerParams(
            collective_id=0, has_side_effects=True, vmem_limit_bytes=(LIMIT if held else 62) << 20
        ),
    )(*inputs.values())

    results = dict(
        layer=struct(positions, width, LOW),
        grad_tokens=struct(positions, width, F32),
        grad_gain_one=struct(1, width, F32),
        grad_kv_weight=struct(width, 2 * head, F32),
        grad_router=struct(experts, width, F32),
        grad_gain_two=struct(1, width, F32),
        grad_up=struct(width, hidden_units, F32),
        grad_down=struct(hidden_units, width, F32),
    )
    if fine:
        results.update(grad_out=struct(*expert_out), grad_query=struct(*expert_out))
    scratch = dict(store_sem=dma(len(results)), block_sem=dma(1))
    if not held:
        scratch.update(
            big_low=vmem(blocks, width, chunk, LOW),
            big_full=vmem(blocks, width, chunk, F32),
            kv_held=vmem(width, 2 * head, LOW),
            kv_full=vmem(width, 2 * head, F32),
            layer_held=vmem(positions, width, LOW),
            tokens_held=vmem(positions, width, F32),
            vectors_held=vmem(rows, width, F32),
            load_sem=dma(blocks),
            small_sem=dma(4),
        )
    names = list(outputs) + list(results) + list(scratch)
    finished = pl.pallas_call(
        functools.partial(finish, names, held),
        out_shape=tuple(results.values()),
        in_specs=[passed] * len(reduced),
        out_specs=(hbm,) * len(results),
        scratch_shapes=list(scratch.values()),
        compiler_params=pltpu.CompilerParams(vmem_limit_bytes=(4 if held else 62) << 20),
    )(*reduced)
    r = types.SimpleNamespace(**dict(zip(results, finished, strict=True)))

    def own_part(a):
        if fine:
            return jnp.swapaxes((r.grad_out, r.grad_query)[a], 1, 2)
        whole = jnp.zeros((2, few, head // 4, width), LOW)
        whole = whole.at[lax.axis_index("expert") % 2].set(reduced[4][a])
        whole = whole.reshape(experts, head // 4, width)
        whole = lax.psum_scatter(whole, "expert", scatter_dimension=2, tiled=True)
        return jnp.swapaxes(whole, 1, 2).astype(F32)

    return (
        r.layer[None],
        r.grad_tokens[None],
        r.grad_gain_one[0],
        r.grad_kv_weight,
        r.grad_router.T,
        own_part(1),
        own_part(0),
        r.grad_gain_two[0],
        r.grad_up,
        r.grad_down,
    )


def solution(mesh):
    row = P("dp", "expert", None)
    in_specs = (row, P("dp", "expert"), row, row) + (P(),) * 8 + (row,)
    expert = P(None, "expert", "dp")
    out_specs = (row, row, P(), P(), P(), expert, expert, P(), P(), P())
    return jax.shard_map(shards, mesh=mesh, in_specs=in_specs, out_specs=out_specs, check_vma=False)
```
